32 devices in a mesh: groups: 2 (over y), band: 16 (over z, x, core).
Axes of the slice: x: 2, y: 2, z: 4, core: 2. Of those that a mesh axis runs over, the one named last changes fastest.
Arguments:
- saved_preact: bfloat16 [98304, 512], P(('groups', 'band')), parts along dimension 0
- edge_senders: int32 [49152], P('band'), may hold values from 0 to 2175, as said below
- edge_slots: int32 [49152], P('band'), may hold values from 0 to 31, as said below
- mesh_requests: int32 [16, 16, 2], P('band'), may hold values from 0 to 15, as said below
- mesh_cotangent: bfloat16 [512, 512], P(('groups', 'band')), parts along dimension 0, may hold values from -6 to 6
- out_weight: bfloat16 [512, 512], replicated, may hold values from -0.25 to 0.25
- out_bias: float32 [512], replicated, may hold values from -4 to 4
- ln_gain: float32 [512], replicated, may hold values from 0.4 to 1.6
- grid_weight: bfloat16 [512, 512], replicated, may hold values from -0.25 to 0.25
- mesh_weight: bfloat16 [512, 512], replicated, may hold values from -0.25 to 0.25
Outputs:
- grid_adjoint: bfloat16 [65536, 512], P(('groups', 'band')), parts along dimension 0
- mesh_adjoint: bfloat16 [512, 512], P(('groups', 'band')), parts along dimension 0
The draws below stay inside these ranges and needn't reach their ends.
There are 2 independent parts, one for each index of `groups`. The reference program is written for one: setup_inputs(seed, part) draws one part's arguments, and reference() takes and returns one part's arrays. A program takes and returns all parts, laid end to end along the dimension named above; an argument that names none is the same for every part. Nothing has to cross between parts.
Inputs may be any that keep to these rules, and one draw needn't show every extreme that they name: `edge_senders`: within each band's 3072 edges the values never fall and every row of the band's window (2048 own grid nodes, then the first 128 of the next band) is named at least once; the last band names only its own 2048 rows. `edge_slots`: the slot k of an edge of band b names the request mesh_requests[b, k // 2, k % 2] at owner k // 2; some slots are named by no edge, and which ones differs from band to band. `mesh_requests`: entry [b, o, j] is a row among owner o's 16 mesh nodes.
All inputs are finite; a program needn't handle non-finite values.
Results may differ from the reference program's by a relative error of at most 0.0057.
Values may be sent and summed in bfloat16 or wider, within the bound.
No kernel may reach another device: no remote copies, remote signals or barrier semaphores. Data moves between devices by JAX's collectives and lax.ppermute only.
A program may use at most 64 MiB of HBM per device.

```python
import math
import jax
import jax.numpy as jnp
from jax import lax

D = 512
G_DEV = 2048
M_DEV = 16
RIM = 128
CAP = 2
E_DEV = 3072
MESH = 256
N_BAND = 16


def draw_saved_preact(key, part):
    key = jax.random.fold_in(key, 37)
    base_key, row_key, col_key = jax.random.split(key, 3)
    total_rows = N_BAND * E_DEV
    row_scale = jnp.exp(jax.random.uniform(row_key, (total_rows, 1), jnp.float32, math.log(0.3), math.log(3.0)))
    col_scale = jnp.exp(jax.random.uniform(col_key, (1, D), jnp.float32, math.log(0.3), math.log(3.0)))
    values = jax.random.normal(base_key, (total_rows, D), jnp.float32)
    return (values * row_scale * col_scale).astype(jnp.bfloat16)


def draw_edge_senders(key, part):
    key = jax.random.fold_in(key, 11)
    band_keys = jax.random.split(key, N_BAND)

    def one_band(band_key, band_number):
        span = jnp.where(band_number == N_BAND - 1, G_DEV, G_DEV + RIM).astype(jnp.int32)
        position = jnp.arange(E_DEV, dtype=jnp.int32)
        extra = jax.random.randint(band_key, (E_DEV,), 0, span).astype(jnp.int32)
        picked = jnp.where(position < span, position, extra)
        return jnp.sort(picked)
    rows = jax.vmap(one_band)(band_keys, jnp.arange(N_BAND, dtype=jnp.int32))
    return rows.reshape(N_BAND * E_DEV).astype(jnp.int32)


def draw_edge_slots(key, part):
    key = jax.random.fold_in(key, 23)
    count_key, pick_key, order_key = jax.random.split(key, 3)
    counts = jax.random.randint(count_key, (N_BAND, N_BAND), 0, CAP + 1).astype(jnp.int32)
    counts = counts.at[0, N_BAND - 1].set(CAP)
    counts = counts.at[:, 0].set(jnp.maximum(counts[:, 0], 1))
    live = (jnp.arange(CAP, dtype=jnp.int32)[None, None, :] < counts[:, :, None]).reshape(N_BAND, N_BAND * CAP)
    live_int = live.astype(jnp.int32)
    order = jnp.argsort(1 - live_int, axis=1, stable=True).astype(jnp.int32)
    live_total = jnp.sum(live_int, axis=1, keepdims=True)
    position = jnp.arange(E_DEV, dtype=jnp.int32)[None, :]
    random_pick = jax.random.randint(pick_key, (N_BAND, E_DEV), 0, live_total).astype(jnp.int32)
    index = jnp.where(position < live_total, position, random_pick)
    slots = jnp.take_along_axis(order, index, axis=1)
    band_keys = jax.random.split(order_key, N_BAND)
    slots = jax.vmap(jax.random.permutation)(band_keys, slots)
    return slots.reshape(N_BAND * E_DEV).astype(jnp.int32)


def draw_mesh_requests(key, part):
    key = jax.random.fold_in(key, 51)
    table = jax.random.randint(key, (N_BAND, N_BAND, CAP), 0, M_DEV).astype(jnp.int32)
    table = table.at[0, 0, 0].set(0)
    table = table.at[0, 0, CAP - 1].set(M_DEV - 1)
    return table


def block_scale(rng, extent, shards, low, largest):
    gain, own = 1.0, jax.random.fold_in(rng, 6)
    for dim, parts in shards:
        draws = jnp.exp(jax.random.uniform(jax.random.fold_in(own, dim), (parts,), jnp.float32, low / len(shards), largest / len(shards)))
        gain = gain * jnp.repeat(draws, extent[dim] // parts).reshape([-1 if axis == dim else 1 for axis in range(len(extent))])
    return gain


def gaussian(own_key, shape, scale, most, shards=(), kind=jnp.bfloat16):
    values = scale * jax.random.normal(own_key, shape, jnp.float32)
    if shards:
        values = values * block_scale(own_key, shape, shards, -0.22, 0.18)
    return jnp.clip(values, -most, most).astype(kind)


def setup_inputs(seed: int = 0, part: int = 0) -> dict:
    streams_of = jax.random.split(jax.random.key(seed), 11)
    own_keys = jax.random.split(jax.random.fold_in(streams_of[10], part), 11)
    return {
        "saved_preact": draw_saved_preact(jax.random.fold_in(jax.random.fold_in(streams_of[10], part), 71), part),
        "edge_senders": draw_edge_senders(jax.random.fold_in(streams_of[10], 71), part),
        "edge_slots": draw_edge_slots(jax.random.fold_in(streams_of[10], 71), part),
        "mesh_requests": draw_mesh_requests(jax.random.fold_in(streams_of[10], 71), part),
        "mesh_cotangent": gaussian(own_keys[4], (MESH, D), 1.0, 6.0, ((0, 16),)),
        "out_weight": gaussian(streams_of[5], (D, D), D ** -0.5, 0.25),
        "out_bias": gaussian(streams_of[6], (D,), 1.0, 4.0, (), jnp.float32),
        "ln_gain": jnp.clip(jax.random.uniform(streams_of[7], (D,), jnp.float32, 0.4, 1.6), 0.4, 1.6),
        "grid_weight": gaussian(streams_of[8], (D, D), D ** -0.5, 0.25),
        "mesh_weight": gaussian(streams_of[9], (D, D), D ** -0.5, 0.25),
    }


ln_eps = 1e-05

def edge_terms(preact, cot_rows, out_weight, out_bias, ln_gain, grid_weight, mesh_weight):
    pre_float = preact.astype(jnp.float32)
    hidden = jax.nn.silu(pre_float).astype(jnp.bfloat16)
    output = jnp.dot(hidden, out_weight, preferred_element_type=jnp.float32) + out_bias
    centre = output - lax.optimization_barrier(jnp.mean(output, axis=-1, keepdims=True))
    inv_scale = lax.rsqrt(lax.optimization_barrier(jnp.mean(centre * centre, axis=-1, keepdims=True)) + ln_eps)
    normed = centre * inv_scale
    d_normed = cot_rows.astype(jnp.float32) * ln_gain
    d_output = inv_scale * (d_normed - lax.optimization_barrier(jnp.mean(d_normed, axis=-1, keepdims=True)) - normed * lax.optimization_barrier(jnp.mean(d_normed * normed, axis=-1, keepdims=True)))
    d_output = d_output.astype(jnp.bfloat16)
    contract = (((1,), (1,)), ((), ()))
    d_hidden = lax.dot_general(d_output, out_weight, contract, preferred_element_type=jnp.float32)
    gate_sig = jax.nn.sigmoid(pre_float)
    d_preact = (d_hidden * gate_sig * (1.0 + pre_float * (1.0 - gate_sig))).astype(jnp.bfloat16)
    grid_term = lax.dot_general(d_preact, grid_weight, contract, preferred_element_type=jnp.float32)
    mesh_term = lax.dot_general(d_preact, mesh_weight, contract, preferred_element_type=jnp.float32)
    return (grid_term, mesh_term)

def reference(saved_preact, edge_senders, edge_slots, mesh_requests, mesh_cotangent, out_weight, out_bias, ln_gain, grid_weight, mesh_weight):
    pre_blocks = saved_preact.reshape(N_BAND, E_DEV, D)
    sender_blocks = edge_senders.reshape(N_BAND, E_DEV)
    slot_blocks = edge_slots.reshape(N_BAND, E_DEV)
    owner_base = (jnp.arange(N_BAND, dtype=jnp.int32) * M_DEV)[:, None]

    def one_band(state_pair, inputs):
        mesh_total, rim_rows = state_pair
        preact, senders, slots, requests = inputs
        wanted = (requests + owner_base).reshape(N_BAND * CAP).astype(jnp.int32)
        receivers = jnp.take(wanted, slots)
        cot_rows = jnp.take(mesh_cotangent, receivers, axis=0)
        grid_term, mesh_term = edge_terms(preact, cot_rows, out_weight, out_bias, ln_gain, grid_weight, mesh_weight)
        window = jax.ops.segment_sum(grid_term, senders, num_segments=G_DEV + RIM)
        head_rows = window[:RIM] + rim_rows
        own_rows = jnp.concatenate([head_rows, window[RIM:G_DEV]], axis=0)
        mesh_total = mesh_total.at[receivers].add(mesh_term)
        return ((mesh_total, window[G_DEV:]), own_rows.astype(jnp.bfloat16))
    start_state = (jnp.zeros((N_BAND * M_DEV, D), jnp.float32), jnp.zeros((RIM, D), jnp.float32))
    (mesh_total, _), grid_rows = lax.scan(one_band, start_state, (pre_blocks, sender_blocks, slot_blocks, mesh_requests))
    return (grid_rows.reshape(N_BAND * G_DEV, D), mesh_total.astype(jnp.bfloat16))
```

```python
import functools

import jax
import jax.numpy as jnp
from jax import lax
from jax.experimental import pallas as pl
from jax.experimental.pallas import tpu as pltpu
from jax.sharding import PartitionSpec as P

G_DEV = 2048
RIM = 128
LANES = 128
EPS = 1e-05

VMEM = pltpu.VMEM
SMEM = pltpu.SMEM
T_CONTRACT = (((1,), (1,)), ((), ()))


def stages_of(count):
    bits = count.bit_length() - 1
    assert count == 1 << bits
    shift, stages = 0, []
    while shift < bits:
        width = min(2, bits - shift)
        stages.append((shift, 1 << width))
        shift += width
    return stages


def swap(block, count, mask):
    return lax.ppermute(block, "band", [(i, i ^ mask) for i in range(count)])


def whole(space=VMEM):
    return pl.BlockSpec(memory_space=space)


def fixed(shape):
    return pl.BlockSpec(shape, lambda i: (0,) * len(shape))


def dot(a, b):
    return jnp.dot(a, b, preferred_element_type=jnp.float32)


def dot_t(a, b):
    return lax.dot_general(a, b, T_CONTRACT, preferred_element_type=jnp.float32)


def before_kernel(pre_ref, weight_ref, bias_ref, normed_ref, q_ref, gate_ref):
    p = pre_ref[...].astype(jnp.float32)
    s = 0.5 * jnp.tanh(0.5 * p) + 0.5
    h = p * s
    weight = weight_ref[...]
    out = dot(h.astype(jnp.bfloat16), weight) + bias_ref[...]
    centre = out - jnp.mean(out, axis=-1, keepdims=True)
    inv = lax.rsqrt(jnp.mean(centre * centre, axis=-1, keepdims=True) + EPS)
    normed = (centre * inv).astype(jnp.bfloat16)
    normed_ref[...] = normed
    q_ref[...] = dot_t(normed, weight).astype(jnp.bfloat16)
    gate_ref[...] = ((s + h * (1.0 - s)) * inv).astype(jnp.bfloat16)


def before(preact, weight, bias, block):
    edges, width = preact.shape
    rows = pl.BlockSpec((block, width), lambda i: (i, 0))
    return pl.pallas_call(
        before_kernel,
        grid=(edges // block,),
        in_specs=[rows, fixed(weight.shape), fixed(bias.shape)],
        out_specs=[rows] * 3,
        out_shape=[jax.ShapeDtypeStruct((edges, width), jnp.bfloat16)] * 3,
        cost_estimate=pl.CostEstimate(
            flops=4 * edges * width * width, bytes_accessed=8 * edges * width, transcendentals=edges * width
        ),
        compiler_params=pltpu.CompilerParams(vmem_limit_bytes=40 << 20),
        name="before",
    )(preact, weight, bias)


def after_kernel(
    parts,
    chunks,
    owned,
    me_ref,
    ids_ref,
    slots_ref,
    normed_ref,
    q_ref,
    gate_ref,
    weight_ref,
    gain_ref,
    *rest,
):
    pieces, d_ref, sums_refs, (s_ref, dnt_ref) = rest[:parts], rest[parts], rest[parts + 1 : -2], rest[-2:]
    slots, width = s_ref.shape
    each = slots // chunks
    me = me_ref[0]
    step = pl.program_id(0)

    @pl.when(step == 0)
    def _():
        piece_rows = pieces[0].shape[0]
        place = lax.broadcasted_iota(jnp.int32, (slots, piece_rows), 0) // 2 * owned
        place = place + ids_ref[...][:, :1].astype(jnp.int32)
        column = lax.broadcasted_iota(jnp.int32, (slots, piece_rows), 1)
        rows = jnp.zeros((slots, width), jnp.float32)
        for k in range(parts):
            pick = (place == column + k * piece_rows).astype(jnp.float32).astype(jnp.bfloat16)
            rows += dot(pick, pieces[k][...])
        rows = rows * gain_ref[...]
        rows = rows - jnp.mean(rows, axis=-1, keepdims=True)
        centred = rows.astype(jnp.bfloat16)
        s_ref[...] = dot_t(centred, weight_ref[...]).astype(jnp.bfloat16)
        dnt_ref[...] = (rows * (1.0 / width)).astype(jnp.bfloat16)
        for k, sums_ref in enumerate(sums_refs):
            sums_ref[:, :width] = jnp.zeros((each, width), jnp.float32)
            sums_ref[:, width:] = ids_ref[k * each : (k + 1) * each, :]

    block = normed_ref.shape[0]
    row = lax.broadcasted_iota(jnp.int32, (slots, block), 0)
    key = ((row // 2) ^ me) * 2 + row % 2
    onehot_t = (key == slots_ref[...]).astype(jnp.float32)
    onehot = onehot_t.T
    g = dot_t(normed_ref[...], dnt_ref[...])
    c = jnp.sum(onehot * g, axis=-1, keepdims=True)
    s_rows = dot(onehot.astype(jnp.bfloat16), s_ref[...])
    d = gate_ref[...].astype(jnp.float32) * (s_rows - c * q_ref[...].astype(jnp.float32))
    d = d.astype(jnp.bfloat16)
    d_ref[...] = d
    sums = dot(onehot_t.astype(jnp.bfloat16), d)
    for k, sums_ref in enumerate(sums_refs):
        sums_ref[:, :width] += sums[k * each : (k + 1) * each]


def after(me, ids, slots, normed, q, gate, weight, gain, pieces, owned, chunks, block):
    edges, width = normed.shape
    slot_total = ids.shape[0]
    rows = pl.BlockSpec((block, width), lambda i: (i, 0))
    return pl.pallas_call(
        functools.partial(after_kernel, len(pieces), chunks, owned),
        grid=(edges // block,),
        in_specs=[
            whole(SMEM),
            fixed(ids.shape),
            pl.BlockSpec((1, block), lambda i: (0, i)),
            rows,
            rows,
            rows,
            fixed(weight.shape),
            fixed(gain.shape),
        ]
        + [fixed(pieces[0].shape)] * len(pieces),
        out_specs=[rows] + [fixed((slot_total // chunks, width + LANES))] * chunks,
        out_shape=[
            jax.ShapeDtypeStruct((edges, width), jnp.bfloat16),
        ]
        + [jax.ShapeDtypeStruct((slot_total // chunks, width + LANES), jnp.float32)] * chunks,
        scratch_shapes=[VMEM((slot_total, width), jnp.bfloat16)] * 2,
        cost_estimate=pl.CostEstimate(
            flops=3 * edges * width * width, bytes_accessed=8 * edges * width, transcendentals=0
        ),
        compiler_params=pltpu.CompilerParams(vmem_limit_bytes=40 << 20),
        name="after",
    )(me, ids, slots, normed, q, gate, weight, gain, *pieces)


def grid_kernel(blocks, starts_ref, senders_ref, d_ref, weight_ref, out_ref, head_ref, rim_ref, total_ref):
    step = pl.program_id(0)
    block = d_ref.shape[0]
    rows, width = out_ref.shape

    @pl.when(step == 0)
    def _():
        total_ref[:8, :] = jnp.zeros((8, width), jnp.float32)
        total_ref[G_DEV : G_DEV + RIM, :] = jnp.zeros((RIM, width), jnp.float32)

    @pl.when(step < blocks)
    def _():
        base = pl.multiple_of(starts_ref[step * block] // 8 * 8, 8)
        row = lax.broadcasted_iota(jnp.int32, (block + 16, block), 0)
        onehot = (row == senders_ref[...] - base).astype(jnp.float32).astype(jnp.bfloat16)
        sums = dot(onehot, d_ref[...])
        total_ref[pl.ds(base, 8), :] += sums[:8]
        total_ref[pl.ds(pl.multiple_of(base + 8, 8), block + 8), :] = sums[8:]

    @pl.when(step == blocks)
    def _():
        head_ref[...] = total_ref[:RIM, :]
        rim_ref[...] = total_ref[G_DEV : G_DEV + RIM, :]

    @pl.when(step >= blocks)
    def _():
        at = pl.multiple_of((step - blocks) * rows, rows)
        out_ref[...] = dot_t(total_ref[pl.ds(at, rows), :].astype(jnp.bfloat16), weight_ref[...]).astype(
            jnp.bfloat16
        )


def grid_rows(senders, d_preact, weight, block):
    edges, width = d_preact.shape
    blocks = edges // block
    row_blocks = G_DEV // block
    return pl.pallas_call(
        functools.partial(grid_kernel, blocks),
        grid=(blocks + row_blocks,),
        in_specs=[
            whole(SMEM),
            pl.BlockSpec((1, block), lambda i: (0, jnp.minimum(i, blocks - 1))),
            pl.BlockSpec((block, width), lambda i: (jnp.minimum(i, blocks - 1), 0)),
            fixed(weight.shape),
        ],
        out_specs=[
            pl.BlockSpec((block, width), lambda i: (jnp.maximum(i - blocks, 0), 0)),
            fixed((RIM, width)),
            fixed((RIM, width)),
        ],
        out_shape=[
            jax.ShapeDtypeStruct((G_DEV, width), jnp.bfloat16),
            jax.ShapeDtypeStruct((RIM, width), jnp.float32),
            jax.ShapeDtypeStruct((RIM, width), jnp.float32),
        ],
        scratch_shapes=[VMEM((G_DEV + RIM + block + 16, width), jnp.float32)],
        cost_estimate=pl.CostEstimate(
            flops=3 * edges * width * width, bytes_accessed=4 * edges * width, transcendentals=0
        ),
        compiler_params=pltpu.CompilerParams(vmem_limit_bytes=40 << 20),
        name="grid_rows",
    )(senders, senders.reshape(1, edges), d_preact, weight)


def head_kernel(grid_in, head_ref, rim_ref, weight_ref, out_ref):
    rows = (head_ref[...] + rim_ref[...]).astype(jnp.bfloat16)
    out_ref[...] = dot_t(rows, weight_ref[...]).astype(jnp.bfloat16)


def head_rows(grid_adjoint, head, rim, weight):
    return pl.pallas_call(
        head_kernel,
        grid=(1,),
        in_specs=[whole(pl.ANY), fixed(head.shape), fixed(rim.shape), fixed(weight.shape)],
        out_specs=fixed(head.shape),
        out_shape=jax.ShapeDtypeStruct(grid_adjoint.shape, grid_adjoint.dtype),
        input_output_aliases={0: 0},
        cost_estimate=pl.CostEstimate(
            flops=2 * head.size * head.shape[1], bytes_accessed=4 * head.size, transcendentals=0
        ),
        name="head_rows",
    )(grid_adjoint, head, rim, weight)


def regroup_kernel(groups, parts, *refs):
    outs = refs[parts:]
    low = groups // len(outs)
    each = refs[0].shape[0] // groups
    for j, out_ref in enumerate(outs):
        for g in range(low):
            for k in range(parts):
                to, at = (g * parts + k) * each, (j * low + g) * each
                out_ref[to : to + each, :] = refs[k][at : at + each, :]


def regroup(arrived, radix, low):
    rows, width = arrived[0].shape
    parts = len(arrived)
    return pl.pallas_call(
        functools.partial(regroup_kernel, radix * low, parts),
        out_shape=[jax.ShapeDtypeStruct((rows * parts // radix, width), arrived[0].dtype)] * radix,
        cost_estimate=pl.CostEstimate(flops=0, bytes_accessed=8 * rows * parts * width, transcendentals=0),
        name="regroup",
    )(*arrived)


def mesh_kernel(parts, *refs):
    pieces, weight_ref, out_ref = refs[:parts], refs[parts], refs[parts + 1]
    owned, width = out_ref.shape
    rows = jnp.concatenate([piece[...] for piece in pieces], axis=0)
    ids = rows[:, width:].T[:owned].astype(jnp.int32)
    pick = (lax.broadcasted_iota(jnp.int32, ids.shape, 0) == ids).astype(jnp.float32)
    total = dot(pick.astype(jnp.bfloat16), rows[:, :width].astype(jnp.bfloat16))
    out_ref[...] = dot_t(total.astype(jnp.bfloat16), weight_ref[...]).astype(jnp.bfloat16)


def mesh_rows(pieces, weight, owned):
    width = weight.shape[0]
    return pl.pallas_call(
        functools.partial(mesh_kernel, len(pieces)),
        out_shape=jax.ShapeDtypeStruct((owned, width), jnp.bfloat16),
        cost_estimate=pl.CostEstimate(
            flops=2 * owned * width * width, bytes_accessed=2 * width * width, transcendentals=0
        ),
        name="mesh_rows",
    )(*pieces, weight)


def on_device(
    saved_preact,
    edge_senders,
    edge_slots,
    mesh_requests,
    mesh_cotangent,
    out_weight,
    out_bias,
    ln_gain,
    grid_weight,
    mesh_weight,
):
    count = lax.axis_size("band")
    me = lax.axis_index("band")
    owned, width = mesh_cotangent.shape
    edges = saved_preact.shape[0]
    caps = mesh_requests.shape[2]
    slot_total = count * caps
    stages = stages_of(count)

    held = [mesh_cotangent]
    for shift, radix in stages:
        block = held[0] if len(held) == 1 else jnp.concatenate(held, axis=0)
        held = [block] + [swap(block, count, j << shift) for j in range(1, radix)]

    normed, q, gate = before(saved_preact, out_weight, out_bias.reshape(1, width), 512)

    by_distance = jnp.arange(count, dtype=jnp.int32) ^ me
    ids = jnp.take(mesh_requests[0], by_distance, axis=0).reshape(slot_total, 1)
    ids = jnp.broadcast_to(ids.astype(jnp.float32), (slot_total, LANES))
    d_preact, *slot_chunks = after(
        me.reshape(1),
        ids,
        edge_slots.reshape(1, edges),
        normed,
        q,
        gate,
        out_weight,
        ln_gain.reshape(1, width),
        held,
        owned,
        stages[-1][1],
        512,
    )

    arrived = None
    for shift, radix in reversed(stages):
        if arrived is None:
            chunks = slot_chunks
        else:
            chunks = regroup(arrived, radix, 1 << shift)
        arrived = [chunks[0]] + [swap(chunks[j], count, j << shift) for j in range(1, radix)]
    grid_adjoint, head, rim = grid_rows(edge_senders, d_preact, grid_weight, 256)
    carried = lax.ppermute(rim, "band", [(i, i + 1) for i in range(count - 1)])
    grid_adjoint = head_rows(grid_adjoint, head, carried, grid_weight)
    mesh_adjoint = mesh_rows(arrived, mesh_weight, owned)
    return (grid_adjoint, mesh_adjoint)


def solution(mesh):
    in_specs = (
        P(("groups", "band"), None),
        P("band"),
        P("band"),
        P("band", None, None),
        P(("groups", "band"), None),
        P(),
        P(),
        P(),
        P(),
        P(),
    )
    out_specs = (P(("groups", "band"), None), P(("groups", "band"), None))
    return jax.shard_map(
        on_device, mesh=mesh, in_specs=in_specs, out_specs=out_specs, check_vma=False
    )
```

```python
import functools

import jax
import jax.numpy as jnp
from jax import lax
from jax.experimental import pallas as pl
from jax.experimental.pallas import tpu as pltpu
from jax.sharding import PartitionSpec as P

G_DEV = 2048
RIM = 128
LANES = 128
EPS = 1e-05
MIB = 1 << 20

BF16 = jnp.bfloat16
F32 = jnp.float32
VMEM = pl.BlockSpec(memory_space=pltpu.VMEM)
SMEM = pl.BlockSpec(memory_space=pltpu.SMEM)
HBM = pl.BlockSpec(memory_space=pltpu.HBM)
ANY = pl.BlockSpec(memory_space=pl.ANY)
DMA = pltpu.SemaphoreType.DMA


def gather_stages(count):
    top = count.bit_length() - 1
    assert count == 1 << top and top > 1
    stages = []
    while top > 1:
        low = max(1, top - 2)
        stages.append((low, 1 << (top - low)))
        top = low
    return stages + [(0, 2)]


def return_stages(count):
    top = count.bit_length() - 1
    stages = []
    while top > 0:
        low = max(0, top - 2)
        stages.append((low, 1 << (top - low)))
        top = low
    return stages


def swap(block, count, mask):
    return lax.ppermute(block, "band", [(i, i ^ mask) for i in range(count)])


def like(shape, dtype):
    return jax.ShapeDtypeStruct(shape, dtype)


def in_hbm(x):
    return pltpu.with_memory_space_constraint(x, pltpu.HBM)


def in_vmem(shape, dtype):
    return pltpu.VMEM(shape, dtype)


def dot(a, b):
    return jnp.dot(a, b, preferred_element_type=F32)


def dot_t(a, b):
    return lax.dot_general(a, b, (((1,), (1,)), ((), ())), preferred_element_type=F32)


def split(x):
    high = x.astype(BF16)
    return high, (x - high.astype(F32)).astype(BF16)


def cost(flops, size):
    return pl.CostEstimate(flops=int(flops), bytes_accessed=int(size), transcendentals=0)


def params(limit):
    return pltpu.CompilerParams(vmem_limit_bytes=limit * MIB)


def edge_block(pre, weight, bias):
    p = pre.astype(F32)
    s = 0.5 * jnp.tanh(0.5 * p) + 0.5
    h = p * s
    out = dot(h.astype(BF16), weight) + bias
    centre = out - jnp.mean(out, axis=-1, keepdims=True)
    inv = lax.rsqrt(jnp.mean(centre * centre, axis=-1, keepdims=True) + EPS)
    normed = (centre * inv).astype(BF16)
    q = dot_t(normed, weight).astype(BF16)
    return normed, q, (s + h * (1.0 - s)) * inv


def before_kernel(first, block, copies, pre_hbm, *refs):
    sources, rest = refs[:copies], refs[copies:]
    if copies:
        me_ref, requests_ref, *rest = rest
        targets, (ids_ref, *rest) = rest[:copies], rest[copies:]
        weight_ref, bias_ref = targets[:2]
    else:
        weight_ref, bias_ref, _, *rest = rest
    normed_ref, q_ref, gate_ref, pre_ref, sem, other_sem = rest
    rows = normed_ref.shape[0]
    loads = [
        pltpu.make_async_copy(
            pre_hbm.at[pl.ds(first + at, block)], pre_ref.at[pl.ds(at, block)], sem.at[at // block]
        )
        for at in range(0, rows, block)
    ]
    others = [pltpu.make_async_copy(a, b, other_sem.at[k]) for k, (a, b) in enumerate(zip(sources, targets))] if copies else []
    for copy in others[:2] + loads + others[2:]:
        copy.start()
    for copy in others[:2]:
        copy.wait()
    weight, bias = weight_ref[...], bias_ref[...]
    for k, at in enumerate(range(0, rows, block)):
        loads[k].wait()
        piece = slice(at, at + block)
        normed_ref[piece], q_ref[piece], gate_ref[piece] = edge_block(pre_ref[piece], weight, bias)
    for copy in others[2:]:
        copy.wait()
    if copies:
        slots, caps = ids_ref.shape[0], requests_ref.shape[2]
        row = lax.broadcasted_iota(jnp.int32, ids_ref.shape, 0)
        ids = jnp.zeros(ids_ref.shape, jnp.int32)
        for r in range(slots):
            ids = jnp.where(row == r, requests_ref[0, (r // caps) ^ me_ref[0], r % caps], ids)
        ids_ref[...] = ids.astype(F32)


def before(preact, first, rows, held, sources=(), given=(), me=None, requests=None, block=256):
    width = preact.shape[1]
    copies = len(sources)
    outs = [in_vmem(a.shape, a.dtype) for a in sources]
    if copies:
        outs.append(in_vmem((requests.shape[1] * requests.shape[2], LANES), F32))
    outs += [in_vmem((rows, width), BF16)] * 2 + [in_vmem((rows, width), F32)]
    return pl.pallas_call(
        functools.partial(before_kernel, first, block, copies),
        in_specs=[HBM] * (1 + copies) + ([SMEM, SMEM] if copies else [VMEM, VMEM, ANY]),
        out_specs=[VMEM] * len(outs),
        out_shape=outs,
        scratch_shapes=[pltpu.VMEM((rows, width), BF16), DMA((rows // block,)), DMA((max(copies, 1),))],
        cost_estimate=cost(6 * rows * width * width, 10 * rows * width),
        compiler_params=params(16),
        name="before",
    )(in_hbm(preact), *[in_hbm(a) for a in sources], *((me, requests) if copies else (*given, held)))


def after_kernel(
    halves, parts, chunks, owned, block, me_ref, ids_ref, slots_ref, senders_ref, weight_ref, gain_ref, *refs
):
    edge_refs = [refs[3 * k : 3 * k + 3] for k in range(halves)]
    refs = refs[3 * halves :]
    pieces, d_ref, rim_ref, sums_refs = refs[:parts], refs[parts], refs[parts + 1], refs[parts + 2 :]
    slots = ids_ref.shape[0]
    edges, width = d_ref.shape
    each = slots // chunks
    me = me_ref[0]
    weight = weight_ref[...]

    piece_rows = pieces[0].shape[0]
    row = lax.broadcasted_iota(jnp.int32, (slots, 1), 0)
    far, place, step = row // 2, jnp.zeros_like(row), 1
    for shift, radix in gather_stages(slots // 2):
        place = place + ((far >> shift) & (radix - 1)) * step
        step *= radix
    place = place * owned + ids_ref[...][:, :1].astype(jnp.int32)
    column = lax.broadcasted_iota(jnp.int32, (slots, piece_rows), 1)
    rows = jnp.zeros((slots, width), F32)
    for k in range(parts):
        pick = (place == column + k * piece_rows).astype(F32).astype(BF16)
        rows += dot(pick, pieces[k][...])
    rows = rows * gain_ref[...]
    rows = rows - jnp.mean(rows, axis=-1, keepdims=True)
    high, low = split(rows)
    s_high, s_low = split(dot_t(high, weight) + dot_t(low, weight))
    s_both = jnp.concatenate([s_high, s_low], axis=0)
    mean_rows = (rows * (1.0 / width)).astype(BF16)

    key = ((row // 2) ^ me) * 2 + row % 2
    sums = jnp.zeros((slots, width), F32)
    rim = jnp.zeros((RIM, width), F32)
    rim_row = lax.broadcasted_iota(jnp.int32, (RIM, block), 0) + G_DEV
    for at in range(0, edges, block):
        half = edges // halves
        normed_ref, q_ref, gate_ref = edge_refs[at // half]
        piece = slice(at % half, at % half + block)
        onehot_t = (key == slots_ref[:, at : at + block]).astype(F32)
        onehot = onehot_t.T
        g = dot_t(normed_ref[piece], mean_rows)
        c = jnp.sum(onehot * g, axis=-1, keepdims=True)
        onehot = onehot.astype(BF16)
        s_rows = dot(jnp.concatenate([onehot, onehot], axis=1), s_both)
        d = (gate_ref[piece] * (s_rows - c * q_ref[piece].astype(F32))).astype(BF16)
        d_ref[at : at + block, :] = d
        sums += dot(onehot_t.astype(BF16), d)
        if at + block > G_DEV:
            pick = (rim_row == senders_ref[:, at : at + block]).astype(F32).astype(BF16)
            rim += dot(pick, d)
    rim_ref[...] = rim
    for k, sums_ref in enumerate(sums_refs):
        sums_ref[:, :width] = sums[k * each : (k + 1) * each]
        sums_ref[:, width:] = ids_ref[k * each : (k + 1) * each, :]


def after(me, ids, slots, senders, weight, gain, parts, pieces, owned, chunks, block=512):
    edges, width = slots.shape[1], weight.shape[0]
    slot_total = ids.shape[0]
    return pl.pallas_call(
        functools.partial(after_kernel, len(parts), len(pieces), chunks, owned, block),
        in_specs=[SMEM] + [VMEM] * (5 + 3 * len(parts) + len(pieces)),
        out_specs=[VMEM] * (2 + chunks),
        out_shape=[in_vmem((edges, width), BF16), in_vmem((RIM, width), F32)]
        + [in_vmem((slot_total // chunks, width + LANES), F32)] * chunks,
        cost_estimate=cost(6 * edges * width * width, 8 * edges * width),
        compiler_params=params(16),
        name="after",
    )(me, ids, slots, senders, weight, gain, *[a for part in parts for a in part], *pieces)


def grid_kernel(block, starts_ref, senders_ref, d_ref, weight_ref, out_hbm, head_ref, total_ref, out_ref, sem):
    edges, width = d_ref.shape
    total_ref[:8, :] = jnp.zeros((8, width), F32)
    row = lax.broadcasted_iota(jnp.int32, (block + 16, block), 0)
    for at in range(0, edges, block):
        base = pl.multiple_of(starts_ref[at] // 8 * 8, 8)
        onehot = (row == senders_ref[:, at : at + block] - base).astype(F32).astype(BF16)
        sums = dot(onehot, d_ref[at : at + block, :])
        total_ref[pl.ds(base, 8), :] += sums[:8]
        total_ref[pl.ds(pl.multiple_of(base + 8, 8), block + 8), :] = sums[8:]
    head_ref[...] = total_ref[:RIM, :]
    weight = weight_ref[...]
    copies = []
    for k, at in enumerate(range(RIM, G_DEV, 2 * RIM)):
        size = min(2 * RIM, G_DEV - at)
        out_ref[at : at + size, :] = dot_t(total_ref[at : at + size, :].astype(BF16), weight).astype(BF16)
        copies.append(
            pltpu.make_async_copy(out_ref.at[pl.ds(at, size)], out_hbm.at[pl.ds(at, size)], sem.at[k])
        )
        copies[-1].start()
    for copy in copies:
        copy.wait()


def grid_rows(senders, d_preact, weight, block=256):
    edges, width = d_preact.shape
    return pl.pallas_call(
        functools.partial(grid_kernel, block),
        in_specs=[SMEM] + [VMEM] * 3,
        out_specs=[HBM, VMEM],
        out_shape=[like((G_DEV, width), BF16), in_vmem((RIM, width), F32)],
        scratch_shapes=[
            pltpu.VMEM((G_DEV + RIM + block + 16, width), F32),
            pltpu.VMEM((G_DEV, width), BF16),
            DMA((-(-(G_DEV - RIM) // (2 * RIM)),)),
        ],
        cost_estimate=cost(4 * edges * width * width, 4 * edges * width),
        compiler_params=params(16),
        name="grid_rows",
    )(senders, senders.reshape(1, edges), d_preact, weight)


def head_kernel(grid_in, head_ref, rim_ref, weight_ref, out_hbm, out_ref, sem):
    rows = (head_ref[...] + rim_ref[...]).astype(BF16)
    out_ref[...] = dot_t(rows, weight_ref[...]).astype(BF16)
    copy = pltpu.make_async_copy(out_ref, out_hbm.at[pl.ds(0, RIM)], sem)
    copy.start()
    copy.wait()


def head_rows(grid_adjoint, head, rim, weight):
    return pl.pallas_call(
        head_kernel,
        in_specs=[HBM, VMEM, VMEM, VMEM],
        out_specs=HBM,
        out_shape=like(grid_adjoint.shape, grid_adjoint.dtype),
        scratch_shapes=[pltpu.VMEM(head.shape, BF16), DMA],
        input_output_aliases={0: 0},
        cost_estimate=cost(2 * head.size * head.shape[1], 4 * head.size),
        compiler_params=params(4),
        name="head_rows",
    )(grid_adjoint, head, rim, weight)


def regroup_kernel(groups, parts, *refs):
    outs = refs[parts:]
    low = groups // len(outs)
    each = refs[0].shape[0] // groups
    for j, out_ref in enumerate(outs):
        for g in range(low):
            for k in range(parts):
                to, at = (g * parts + k) * each, (j * low + g) * each
                out_ref[to : to + each, :] = refs[k][at : at + each, :]


def regroup(arrived, radix, low):
    rows, width = arrived[0].shape
    parts = len(arrived)
    return pl.pallas_call(
        functools.partial(regroup_kernel, radix * low, parts),
        in_specs=[VMEM] * parts,
        out_specs=[VMEM] * radix,
        out_shape=[in_vmem((rows * parts // radix, width), arrived[0].dtype)] * radix,
        cost_estimate=cost(0, 8 * rows * parts * width),
        compiler_params=params(8),
        name="regroup",
    )(*arrived)


def mesh_kernel(parts, *refs):
    pieces, weight_ref, out_ref = refs[:parts], refs[parts], refs[parts + 1]
    owned, width = out_ref.shape
    rows = jnp.concatenate([piece[...] for piece in pieces], axis=0)
    ids = rows[:, width:].T[:owned].astype(jnp.int32)
    pick = (lax.broadcasted_iota(jnp.int32, ids.shape, 0) == ids).astype(F32).astype(BF16)
    high, low = split(rows[:, :width])
    high, low = split(dot(pick, high) + dot(pick, low))
    both = dot_t(jnp.concatenate([high, low], axis=0), weight_ref[...])
    out_ref[...] = (both[:owned] + both[owned:]).astype(BF16)


def mesh_rows(pieces, weight, owned):
    width = weight.shape[0]
    return pl.pallas_call(
        functools.partial(mesh_kernel, len(pieces)),
        in_specs=[VMEM] * (len(pieces) + 1),
        out_specs=VMEM,
        out_shape=like((owned, width), BF16),
        cost_estimate=cost(2 * owned * width * width, 2 * width * width),
        compiler_params=params(8),
        name="mesh_rows",
    )(*pieces, weight)


def on_device(
    saved_preact,
    edge_senders,
    edge_slots,
    mesh_requests,
    mesh_cotangent,
    out_weight,
    out_bias,
    ln_gain,
    grid_weight,
    mesh_weight,
):
    count = lax.axis_size("band")
    me = lax.axis_index("band")
    owned, width = mesh_cotangent.shape
    edges = saved_preact.shape[0]
    half = edges // 2

    held, seen = [mesh_cotangent], []
    for shift, radix in gather_stages(count):
        block = held[0] if len(held) == 1 else jnp.concatenate(held, axis=0)
        seen.append(block)
        held = [block] + [swap(block, count, j << shift) for j in range(1, radix)]

    sources = (out_weight, out_bias.reshape(1, width), grid_weight, mesh_weight, ln_gain.reshape(1, width))
    weight, bias, weight_g, weight_m, gain, ids, *first = before(
        saved_preact, 0, half, None, sources, me=me.reshape(1), requests=mesh_requests
    )
    second = before(saved_preact, half, half, seen[1], given=(weight, bias))

    stages = return_stages(count)
    d_preact, rim, *chunks = after(
        me.reshape(1),
        ids,
        edge_slots.reshape(1, edges),
        edge_senders.reshape(1, edges),
        weight,
        gain,
        [first, second],
        held,
        owned,
        stages[0][1],
    )

    arrived = None
    for shift, radix in stages:
        if arrived is not None:
            chunks = regroup(arrived, radix, 1 << shift)
        arrived = [chunks[0]] + [swap(chunks[j], count, j << shift) for j in range(1, radix)]
    carried = lax.ppermute(rim, "band", [(i, i + 1) for i in range(count - 1)])
    grid_adjoint, head = grid_rows(edge_senders, d_preact, weight_g)
    grid_adjoint = head_rows(grid_adjoint, head, carried, weight_g)
    mesh_adjoint = mesh_rows(arrived, weight_m, owned)
    return (grid_adjoint, mesh_adjoint)


def solution(mesh):
    in_specs = (
        P(("groups", "band"), None),
        P("band"),
        P("band"),
        P("band", None, None),
        P(("groups", "band"), None),
        P(),
        P(),
        P(),
        P(),
        P(),
    )
    out_specs = (P(("groups", "band"), None), P(("groups", "band"), None))
    return jax.shard_map(
        on_device, mesh=mesh, in_specs=in_specs, out_specs=out_specs, check_vma=False
    )
```

```python
import functools

import jax
import jax.numpy as jnp
from jax import lax
from jax.experimental import pallas as pl
from jax.experimental.pallas import tpu as pltpu
from jax.sharding import PartitionSpec as P

G_DEV = 2048
RIM = 128
LANES = 128
EPS = 1e-05
MIB = 1 << 20

BF16 = jnp.bfloat16
F32 = jnp.float32
VMEM = pl.BlockSpec(memory_space=pltpu.VMEM)
SMEM = pl.BlockSpec(memory_space=pltpu.SMEM)
HBM = pl.BlockSpec(memory_space=pltpu.HBM)
ANY = pl.BlockSpec(memory_space=pl.ANY)
DMA = pltpu.SemaphoreType.DMA


def stages_of(count):
    top = count.bit_length() - 1
    assert count == 1 << top
    stages = []
    while top > 0:
        low = max(0, top - 2)
        stages.append((low, 1 << (top - low)))
        top = low
    return stages


def swap(block, count, mask):
    return lax.ppermute(block, "band", [(i, i ^ mask) for i in range(count)])


def like(shape, dtype):
    return jax.ShapeDtypeStruct(shape, dtype)


def in_hbm(x):
    return pltpu.with_memory_space_constraint(x, pltpu.HBM)


def in_vmem(shape, dtype):
    return pltpu.VMEM(shape, dtype)


def dot(a, b):
    return jnp.dot(a, b, preferred_element_type=F32)


def dot_t(a, b):
    return lax.dot_general(a, b, (((1,), (1,)), ((), ())), preferred_element_type=F32)


def split(x):
    high = x.astype(BF16)
    return high, (x - high.astype(F32)).astype(BF16)


def cost(flops, size):
    return pl.CostEstimate(flops=int(flops), bytes_accessed=int(size), transcendentals=0)


def params(limit):
    return pltpu.CompilerParams(vmem_limit_bytes=limit * MIB)


def products(pre, weight, bias):
    p = pre.astype(F32)
    s = 0.5 * jnp.tanh(0.5 * p) + 0.5
    h = p * s
    return dot(h.astype(BF16), weight) + bias, s + h * (1.0 - s)


def edge_blocks(pre_ref, weight, bias, normed_ref, q_ref, gate_ref, block, arrive):
    rows, last = pre_ref.shape[0], None
    for at in range(0, rows + block, block):
        this = None
        if at < rows:
            arrive(at)
            this = products(pre_ref[at : at + block], weight, bias)
        if last is not None:
            out, gate = last
            centre = out - jnp.mean(out, axis=-1, keepdims=True)
            inv = lax.rsqrt(jnp.mean(centre * centre, axis=-1, keepdims=True) + EPS)
            normed = (centre * inv).astype(BF16)
            piece = slice(at - block, at)
            normed_ref[piece] = normed
            q_ref[piece] = dot_t(normed, weight).astype(BF16)
            gate_ref[piece] = gate * inv
        last = this


def first_kernel(block, copies, pre_hbm, *refs):
    sources, (me_ref, requests_hbm), refs = refs[:copies], refs[copies : copies + 2], refs[copies + 2 :]
    targets, refs = refs[:copies], refs[copies:]
    ids_ref, other_ref, normed_ref, q_ref, gate_ref, pre_ref, requests_ref, sem = refs
    rows = normed_ref.shape[0]

    def load(k, source, target):
        return pltpu.make_async_copy(source, target, sem.at[k])

    others = [load(k, a, b) for k, (a, b) in enumerate(zip(sources, targets))]
    starts = list(range(0, rows, block))
    loads = [
        load(copies + k, pre_hbm.at[pl.ds(at, block)], pre_ref.at[pl.ds(at, block)])
        for k, at in enumerate(starts)
    ]
    more = load(copies + len(loads), pre_hbm.at[pl.ds(rows, rows)], other_ref)
    asked = load(copies + len(loads) + 1, requests_hbm, requests_ref)
    for copy in others[:2] + loads + others[2:] + [more, asked]:
        copy.start()
    for copy in others[:2]:
        copy.wait()
    edge_blocks(
        pre_ref,
        targets[0][...],
        targets[1][...],
        normed_ref,
        q_ref,
        gate_ref,
        block,
        lambda at: loads[at // block].wait(),
    )
    for copy in others[2:] + [more, asked]:
        copy.wait()
    slots, caps = ids_ref.shape[0], requests_ref.shape[1]
    row = lax.broadcasted_iota(jnp.int32, ids_ref.shape, 0)
    ids = jnp.zeros(ids_ref.shape, jnp.int32)
    for r in range(slots):
        ids = jnp.where(row == r, requests_ref[0, r % caps, (r // caps) ^ me_ref[0]], ids)
    ids_ref[...] = ids.astype(F32)


def first_half(preact, sources, me, requests, block=512):
    edges, width = preact.shape
    rows = edges // 2
    copies = len(sources)
    outs = [in_vmem(a.shape, a.dtype) for a in sources]
    outs += [in_vmem((requests.shape[1] * requests.shape[2], LANES), F32)]
    outs += [in_vmem((rows, width), BF16)] * 3 + [in_vmem((rows, width), F32)]
    return pl.pallas_call(
        functools.partial(first_kernel, block, copies),
        in_specs=[HBM] * (1 + copies) + [SMEM, HBM],
        out_specs=[VMEM] * len(outs),
        out_shape=outs,
        scratch_shapes=[
            pltpu.VMEM((rows, width), BF16),
            pltpu.SMEM(requests.shape, jnp.int32),
            DMA((copies + rows // block + 2,)),
        ],
        cost_estimate=cost(6 * rows * width * width, 10 * rows * width),
        compiler_params=params(16),
        name="first_half",
    )(in_hbm(preact), *[in_hbm(a) for a in sources], me, in_hbm(requests))


def second_kernel(block, pre_ref, weight_ref, bias_ref, after_ref, normed_ref, q_ref, gate_ref):
    edge_blocks(
        pre_ref, weight_ref[...], bias_ref[...], normed_ref, q_ref, gate_ref, block, lambda at: None
    )


def second_half(pre, weight, bias, after, block=512):
    rows, width = pre.shape
    outs = [in_vmem((rows, width), BF16)] * 2 + [in_vmem((rows, width), F32)]
    return pl.pallas_call(
        functools.partial(second_kernel, block),
        in_specs=[VMEM, VMEM, VMEM, ANY],
        out_specs=[VMEM] * len(outs),
        out_shape=outs,
        cost_estimate=cost(6 * rows * width * width, 10 * rows * width),
        compiler_params=params(16),
        name="second_half",
    )(pre, weight, bias, after)


def join_kernel(parts, *refs):
    out_ref, rows = refs[-1], refs[0].shape[0]
    for k in range(parts):
        out_ref[k * rows : (k + 1) * rows, :] = refs[k][...]


def join(pieces, after):
    rows, width = pieces[0].shape
    return pl.pallas_call(
        functools.partial(join_kernel, len(pieces)),
        in_specs=[VMEM] * len(pieces) + [ANY],
        out_specs=VMEM,
        out_shape=in_vmem((len(pieces) * rows, width), pieces[0].dtype),
        cost_estimate=cost(0, 4 * len(pieces) * rows * width),
        compiler_params=params(8),
        name="join",
    )(*pieces, after)


def after_kernel(
    halves, parts, chunks, owned, block, me_ref, ids_ref, slots_ref, senders_ref, weight_ref, gain_ref, *refs
):
    edge_refs = [refs[3 * k : 3 * k + 3] for k in range(halves)]
    refs = refs[3 * halves :]
    pieces, d_ref, rim_ref, sums_refs = refs[:parts], refs[parts], refs[parts + 1], refs[parts + 2 :]
    slots = ids_ref.shape[0]
    edges, width = d_ref.shape
    each = slots // chunks
    me = me_ref[0]
    weight = weight_ref[...]

    piece_rows = pieces[0].shape[0]
    row = lax.broadcasted_iota(jnp.int32, (slots, 1), 0)
    far, place, step = row // 2, jnp.zeros_like(row), 1
    for shift, radix in stages_of(slots // 2):
        place = place + ((far >> shift) & (radix - 1)) * step
        step *= radix
    place = place * owned + ids_ref[...][:, :1].astype(jnp.int32)
    column = lax.broadcasted_iota(jnp.int32, (slots, piece_rows), 1)
    rows = jnp.zeros((slots, width), F32)
    for k in range(parts):
        pick = (place == column + k * piece_rows).astype(F32).astype(BF16)
        rows += dot(pick, pieces[k][...])
    rows = rows * gain_ref[...]
    rows = rows - jnp.mean(rows, axis=-1, keepdims=True)
    high, low = split(rows)
    s_high, s_low = split(dot_t(high, weight) + dot_t(low, weight))
    s_both = jnp.concatenate([s_high, s_low], axis=0)
    mean_rows = (rows * (1.0 / width)).astype(BF16)

    key = ((row // 2) ^ me) * 2 + row % 2
    sums = jnp.zeros((slots, width), F32)
    rim = jnp.zeros((RIM, width), F32)
    rim_row = lax.broadcasted_iota(jnp.int32, (RIM, block), 0) + G_DEV
    for at in range(0, edges, block):
        half = edges // halves
        normed_ref, q_ref, gate_ref = edge_refs[at // half]
        piece = slice(at % half, at % half + block)
        onehot_t = (key == slots_ref[:, at : at + block]).astype(F32)
        onehot = onehot_t.T
        g = dot_t(normed_ref[piece], mean_rows)
        c = jnp.sum(onehot * g, axis=-1, keepdims=True)
        onehot = onehot.astype(BF16)
        s_rows = dot(jnp.concatenate([onehot, onehot], axis=1), s_both)
        d = (gate_ref[piece] * (s_rows - c * q_ref[piece].astype(F32))).astype(BF16)
        d_ref[at : at + block, :] = d
        sums += dot(onehot_t.astype(BF16), d)
        if at + block > G_DEV:
            pick = (rim_row == senders_ref[:, at : at + block]).astype(F32).astype(BF16)
            rim += dot(pick, d)
    rim_ref[...] = rim
    for k, sums_ref in enumerate(sums_refs):
        sums_ref[:, :width] = sums[k * each : (k + 1) * each]
        sums_ref[:, width:] = ids_ref[k * each : (k + 1) * each, :]


def after(me, ids, slots, senders, weight, gain, parts, pieces, owned, chunks, block=512):
    edges, width = slots.shape[1], weight.shape[0]
    slot_total = ids.shape[0]
    return pl.pallas_call(
        functools.partial(after_kernel, len(parts), len(pieces), chunks, owned, block),
        in_specs=[SMEM] + [VMEM] * (5 + 3 * len(parts) + len(pieces)),
        out_specs=[VMEM] * (2 + chunks),
        out_shape=[in_vmem((edges, width), BF16), in_vmem((RIM, width), F32)]
        + [in_vmem((slot_total // chunks, width + LANES), F32)] * chunks,
        cost_estimate=cost(6 * edges * width * width, 8 * edges * width),
        compiler_params=params(16),
        name="after",
    )(me, ids, slots, senders, weight, gain, *[a for part in parts for a in part], *pieces)


def grid_kernel(block, starts_ref, senders_ref, d_ref, weight_ref, out_hbm, head_ref, total_ref, out_ref, sem):
    edges, width = d_ref.shape
    total_ref[:8, :] = jnp.zeros((8, width), F32)
    row = lax.broadcasted_iota(jnp.int32, (block + 16, block), 0)
    for at in range(0, edges, block):
        base = pl.multiple_of(starts_ref[at] // 8 * 8, 8)
        onehot = (row == senders_ref[:, at : at + block] - base).astype(F32).astype(BF16)
        sums = dot(onehot, d_ref[at : at + block, :])
        total_ref[pl.ds(base, 8), :] += sums[:8]
        total_ref[pl.ds(pl.multiple_of(base + 8, 8), block + 8), :] = sums[8:]
    head_ref[...] = total_ref[:RIM, :]
    weight = weight_ref[...]
    copies = []
    for k, at in enumerate(range(RIM, G_DEV, 2 * RIM)):
        size = min(2 * RIM, G_DEV - at)
        out_ref[at : at + size, :] = dot_t(total_ref[at : at + size, :].astype(BF16), weight).astype(BF16)
        copies.append(
            pltpu.make_async_copy(out_ref.at[pl.ds(at, size)], out_hbm.at[pl.ds(at, size)], sem.at[k])
        )
        copies[-1].start()
    for copy in copies:
        copy.wait()


def grid_rows(senders, d_preact, weight, block=256):
    edges, width = d_preact.shape
    return pl.pallas_call(
        functools.partial(grid_kernel, block),
        in_specs=[SMEM] + [VMEM] * 3,
        out_specs=[HBM, VMEM],
        out_shape=[like((G_DEV, width), BF16), in_vmem((RIM, width), F32)],
        scratch_shapes=[
            pltpu.VMEM((G_DEV + RIM + block + 16, width), F32),
            pltpu.VMEM((G_DEV, width), BF16),
            DMA((-(-(G_DEV - RIM) // (2 * RIM)),)),
        ],
        cost_estimate=cost(4 * edges * width * width, 4 * edges * width),
        compiler_params=params(16),
        name="grid_rows",
    )(senders, senders.reshape(1, edges), d_preact, weight)


def head_kernel(grid_in, head_ref, rim_ref, weight_ref, out_hbm, out_ref, sem):
    rows = (head_ref[...] + rim_ref[...]).astype(BF16)
    out_ref[...] = dot_t(rows, weight_ref[...]).astype(BF16)
    copy = pltpu.make_async_copy(out_ref, out_hbm.at[pl.ds(0, RIM)], sem)
    copy.start()
    copy.wait()


def head_rows(grid_adjoint, head, rim, weight):
    return pl.pallas_call(
        head_kernel,
        in_specs=[HBM, VMEM, VMEM, VMEM],
        out_specs=HBM,
        out_shape=like(grid_adjoint.shape, grid_adjoint.dtype),
        scratch_shapes=[pltpu.VMEM(head.shape, BF16), DMA],
        input_output_aliases={0: 0},
        cost_estimate=cost(2 * head.size * head.shape[1], 4 * head.size),
        compiler_params=params(4),
        name="head_rows",
    )(grid_adjoint, head, rim, weight)


def regroup_kernel(groups, parts, *refs):
    outs = refs[parts + 1 :]
    low = groups // len(outs)
    each = refs[0].shape[0] // groups
    for j, out_ref in enumerate(outs):
        for g in range(low):
            for k in range(parts):
                to, at = (g * parts + k) * each, (j * low + g) * each
                out_ref[to : to + each, :] = refs[k][at : at + each, :]


def regroup(arrived, radix, low, after):
    rows, width = arrived[0].shape
    parts = len(arrived)
    return pl.pallas_call(
        functools.partial(regroup_kernel, radix * low, parts),
        in_specs=[VMEM] * parts + [ANY],
        out_specs=[VMEM] * radix,
        out_shape=[in_vmem((rows * parts // radix, width), arrived[0].dtype)] * radix,
        cost_estimate=cost(0, 8 * rows * parts * width),
        compiler_params=params(8),
        name="regroup",
    )(*arrived, after)


def mesh_kernel(parts, *refs):
    pieces, weight_ref, out_ref = refs[:parts], refs[parts], refs[-1]
    owned, width = out_ref.shape
    rows = jnp.concatenate([piece[...] for piece in pieces], axis=0)
    ids = rows[:, width:].T[:owned].astype(jnp.int32)
    pick = (lax.broadcasted_iota(jnp.int32, ids.shape, 0) == ids).astype(F32).astype(BF16)
    high, low = split(rows[:, :width])
    high, low = split(dot(pick, high) + dot(pick, low))
    both = dot_t(jnp.concatenate([high, low], axis=0), weight_ref[...])
    out_ref[...] = (both[:owned] + both[owned:]).astype(BF16)


def mesh_rows(pieces, weight, owned, after):
    width = weight.shape[0]
    return pl.pallas_call(
        functools.partial(mesh_kernel, len(pieces)),
        in_specs=[VMEM] * (len(pieces) + 1) + [ANY],
        out_specs=VMEM,
        out_shape=like((owned, width), BF16),
        cost_estimate=cost(2 * owned * width * width, 2 * width * width),
        compiler_params=params(8),
        name="mesh_rows",
    )(*pieces, weight, in_hbm(after))


def on_device(
    saved_preact,
    edge_senders,
    edge_slots,
    mesh_requests,
    mesh_cotangent,
    out_weight,
    out_bias,
    ln_gain,
    grid_weight,
    mesh_weight,
):
    count = lax.axis_size("band")
    me = lax.axis_index("band")
    owned, width = mesh_cotangent.shape
    edges = saved_preact.shape[0]
    stages = stages_of(count)

    sources = (
        out_weight,
        out_bias.reshape(1, width),
        grid_weight,
        mesh_weight,
        ln_gain.reshape(1, width),
        mesh_cotangent,
    )
    weight, bias, weight_g, weight_m, gain, own_rows, ids, more, *first = first_half(
        saved_preact, sources, me.reshape(1), mesh_requests.swapaxes(1, 2)
    )

    held = [mesh_cotangent]
    for number, (shift, radix) in enumerate(stages):
        if number == 1:
            held = [join([own_rows, *held[1:]], first[0])]
        elif number > 1:
            held = [join(held, ids)]
        held += [swap(held[0], count, j << shift) for j in range(1, radix)]
        if number == 1:
            second = second_half(more, weight, bias, held[0])

    d_preact, rim, *chunks = after(
        me.reshape(1),
        ids,
        edge_slots.reshape(1, edges),
        edge_senders.reshape(1, edges),
        weight,
        gain,
        [first, second],
        held,
        owned,
        stages[0][1],
    )

    grid_adjoint, head = grid_rows(edge_senders, d_preact, weight_g)
    carried = lax.ppermute(rim, "band", [(i, i + 1) for i in range(count - 1)])
    arrived = None
    for shift, radix in stages:
        if arrived is not None:
            chunks = regroup(arrived, radix, 1 << shift, head)
        arrived = [chunks[0]] + [swap(chunks[j], count, j << shift) for j in range(1, radix)]
    grid_adjoint = head_rows(grid_adjoint, head, carried, weight_g)
    mesh_adjoint = mesh_rows(arrived, weight_m, owned, grid_adjoint)
    return (grid_adjoint, mesh_adjoint)


def solution(mesh):
    in_specs = (
        P(("groups", "band"), None),
        P("band"),
        P("band"),
        P("band", None, None),
        P(("groups", "band"), None),
        P(),
        P(),
        P(),
        P(),
        P(),
    )
    out_specs = (P(("groups", "band"), None), P(("groups", "band"), None))
    return jax.shard_map(
        on_device, mesh=mesh, in_specs=in_specs, out_specs=out_specs, check_vma=False
    )
```

```python
import functools

import jax
import jax.numpy as jnp
from jax import lax
from jax.experimental import pallas as pl
from jax.experimental.pallas import tpu as pltpu
from jax.sharding import PartitionSpec as P

G_DEV = 2048
RIM = 128
LANES = 128
EPS = 1e-05
MIB = 1 << 20

BF16 = jnp.bfloat16
F32 = jnp.float32
VMEM = pl.BlockSpec(memory_space=pltpu.VMEM)
SMEM = pl.BlockSpec(memory_space=pltpu.SMEM)
HBM = pl.BlockSpec(memory_space=pltpu.HBM)
ANY = pl.BlockSpec(memory_space=pl.ANY)
DMA = pltpu.SemaphoreType.DMA


def stages_of(count):
    top = count.bit_length() - 1
    assert count == 1 << top
    stages = []
    while top > 0:
        low = max(0, top - 2)
        stages.append((low, 1 << (top - low)))
        top = low
    return stages


def distance_of(row, caps, count):
    group, distance, left = row // caps, 0, count
    for shift, radix in reversed(stages_of(count)):
        left //= radix
        distance = distance + ((group // left) % radix << shift)
    return distance


def swap(block, count, mask):
    return lax.ppermute(block, "band", [(i, i ^ mask) for i in range(count)])


def pass_on(block, count, distance):
    return lax.ppermute(block, "band", [(i, (i + distance) % count) for i in range(count)])


def like(shape, dtype):
    return jax.ShapeDtypeStruct(shape, dtype)


def in_hbm(x):
    return pltpu.with_memory_space_constraint(x, pltpu.HBM)


def in_vmem(shape, dtype):
    return pltpu.VMEM(shape, dtype)


def dot(a, b):
    return jnp.dot(a, b, preferred_element_type=F32)


def dot_t(a, b):
    return lax.dot_general(a, b, (((1,), (1,)), ((), ())), preferred_element_type=F32)


def split(x):
    high = x.astype(BF16)
    return high, (x - high.astype(F32)).astype(BF16)


def cost(flops, size):
    return pl.CostEstimate(flops=int(flops), bytes_accessed=int(size), transcendentals=0)


def params(limit):
    return pltpu.CompilerParams(vmem_limit_bytes=limit * MIB)


def products(pre, weight, bias):
    p = pre.astype(F32)
    s = 0.5 * jnp.tanh(0.5 * p) + 0.5
    h = p * s
    return dot(h.astype(BF16), weight) + bias, s + h * (1.0 - s)


def edge_blocks(pre_ref, weight, bias, normed_ref, q_ref, gate_ref, block, arrive):
    rows, last = pre_ref.shape[0], None
    for at in range(0, rows + block, block):
        this = None
        if at < rows:
            arrive(at)
            this = products(pre_ref[at : at + block], weight, bias)
        if last is not None:
            out, gate = last
            centre = out - jnp.mean(out, axis=-1, keepdims=True)
            inv = lax.rsqrt(jnp.mean(centre * centre, axis=-1, keepdims=True) + EPS)
            normed = (centre * inv).astype(BF16)
            piece = slice(at - block, at)
            normed_ref[piece] = normed
            q_ref[piece] = dot_t(normed, weight).astype(BF16)
            gate_ref[piece] = gate * inv
        last = this


def first_kernel(block, copies, pre_hbm, *refs):
    sources, (me_ref, requests_hbm), refs = refs[:copies], refs[copies : copies + 2], refs[copies + 2 :]
    targets, refs = refs[:copies], refs[copies:]
    ids_ref, other_ref, normed_ref, q_ref, gate_ref, pre_ref, requests_ref, sem = refs
    rows = normed_ref.shape[0]

    def load(k, source, target):
        return pltpu.make_async_copy(source, target, sem.at[k])

    others = [load(k, a, b) for k, (a, b) in enumerate(zip(sources, targets))]
    starts = list(range(0, rows, block))
    more_rows = other_ref.shape[0]
    loads = [
        load(copies + k, pre_hbm.at[pl.ds(at, block)], pre_ref.at[pl.ds(at, block)])
        for k, at in enumerate(starts)
    ]
    more = load(copies + len(loads), pre_hbm.at[pl.ds(rows, more_rows)], other_ref)
    asked = load(copies + len(loads) + 1, requests_hbm, requests_ref)
    for copy in others[:2] + loads + others[2:] + [more, asked]:
        copy.start()
    for copy in others[:2]:
        copy.wait()
    edge_blocks(
        pre_ref,
        targets[0][...],
        targets[1][...],
        normed_ref,
        q_ref,
        gate_ref,
        block,
        lambda at: loads[at // block].wait(),
    )
    for copy in others[2:] + [more, asked]:
        copy.wait()
    slots, caps = ids_ref.shape[0], requests_ref.shape[1]
    count = slots // caps
    row = lax.broadcasted_iota(jnp.int32, ids_ref.shape, 0)
    ids = jnp.zeros(ids_ref.shape, jnp.int32)
    for r in range(slots):
        owner = (me_ref[0] + distance_of(r, caps, count)) % count
        ids = jnp.where(row == r, requests_ref[0, r % caps, owner], ids)
    ids_ref[...] = ids.astype(F32)


def first_part(preact, rows, sources, me, requests, block=512):
    edges, width = preact.shape
    copies = len(sources)
    outs = [in_vmem(a.shape, a.dtype) for a in sources]
    outs += [in_vmem((requests.shape[1] * requests.shape[2], LANES), F32)]
    outs += [in_vmem((edges - rows, width), BF16)]
    outs += [in_vmem((rows, width), BF16)] * 2 + [in_vmem((rows, width), F32)]
    return pl.pallas_call(
        functools.partial(first_kernel, block, copies),
        in_specs=[HBM] * (1 + copies) + [SMEM, HBM],
        out_specs=[VMEM] * len(outs),
        out_shape=outs,
        scratch_shapes=[
            pltpu.VMEM((rows, width), BF16),
            pltpu.SMEM(requests.shape, jnp.int32),
            DMA((copies + rows // block + 2,)),
        ],
        cost_estimate=cost(6 * rows * width * width, 10 * rows * width),
        compiler_params=params(16),
        name="first_part",
    )(in_hbm(preact), *[in_hbm(a) for a in sources], me, in_hbm(requests))


def second_kernel(block, pre_ref, weight_ref, bias_ref, after_ref, normed_ref, q_ref, gate_ref):
    edge_blocks(
        pre_ref, weight_ref[...], bias_ref[...], normed_ref, q_ref, gate_ref, block, lambda at: None
    )


def second_part(pre, weight, bias, after, block=512):
    rows, width = pre.shape
    outs = [in_vmem((rows, width), BF16)] * 2 + [in_vmem((rows, width), F32)]
    return pl.pallas_call(
        functools.partial(second_kernel, block),
        in_specs=[VMEM, VMEM, VMEM, ANY],
        out_specs=[VMEM] * len(outs),
        out_shape=outs,
        cost_estimate=cost(6 * rows * width * width, 10 * rows * width),
        compiler_params=params(16),
        name="second_part",
    )(pre, weight, bias, after)


def join_kernel(parts, *refs):
    out_ref, rows = refs[-1], refs[0].shape[0]
    for k in range(parts):
        out_ref[k * rows : (k + 1) * rows, :] = refs[k][...]


def join(pieces, after):
    rows, width = pieces[0].shape
    return pl.pallas_call(
        functools.partial(join_kernel, len(pieces)),
        in_specs=[VMEM] * len(pieces) + [ANY],
        out_specs=VMEM,
        out_shape=in_vmem((len(pieces) * rows, width), pieces[0].dtype),
        cost_estimate=cost(0, 4 * len(pieces) * rows * width),
        compiler_params=params(8),
        name="join",
    )(*pieces, after)


def after_kernel(
    parts, chunks, owned, caps, block, me_ref, ids_ref, slots_ref, senders_ref, weight_ref, gain_ref, *refs
):
    edge_refs = [refs[3 * k : 3 * k + 3] for k in range(parts)]
    refs = refs[3 * parts :]
    d_ref, sums_refs = refs[-1 - chunks], refs[-chunks:]
    pieces = refs[: -1 - chunks]
    slots = ids_ref.shape[0]
    count = slots // caps
    edges, width = d_ref.shape
    me = me_ref[0]
    weight = weight_ref[...]

    row = lax.broadcasted_iota(jnp.int32, (slots, 1), 0)
    owner = (distance_of(row, caps, count) + me) % count
    far, place, step = owner ^ me, jnp.zeros_like(row), 1
    for shift, radix in stages_of(count):
        place = place + ((far >> shift) & (radix - 1)) * step
        step *= radix
    place = place * owned + ids_ref[...][:, :1].astype(jnp.int32)
    piece_rows = pieces[0].shape[0]
    column = lax.broadcasted_iota(jnp.int32, (slots, piece_rows), 1)
    rows = jnp.zeros((slots, width), F32)
    for k, piece in enumerate(pieces):
        pick = (place == column + k * piece_rows).astype(F32).astype(BF16)
        rows += dot(pick, piece[...])
    rows = rows * gain_ref[...]
    rows = rows - jnp.mean(rows, axis=-1, keepdims=True)
    mean_rows = (rows * (1.0 / width)).astype(BF16)
    both = dot_t(jnp.concatenate(split(rows), axis=0), weight)
    s_both = jnp.concatenate(split(both[:slots] + both[slots:]), axis=0)

    key = owner * caps + row % caps
    rim_row = lax.broadcasted_iota(jnp.int32, (RIM, block), 0) + G_DEV
    sums = jnp.zeros((slots, width), F32)
    rim = jnp.zeros((RIM, width), F32)
    edge_at = [(part, at) for part in edge_refs for at in range(0, part[0].shape[0], block)]
    last = None
    for number in range(len(edge_at) + 1):
        this = None
        if number < len(edge_at):
            (normed_ref, q_ref, gate_ref), at = edge_at[number]
            piece = slice(at, at + block)
            onehot_t = (key == slots_ref[:, number * block : (number + 1) * block]).astype(F32)
            onehot = onehot_t.T
            c = jnp.sum(onehot * dot_t(normed_ref[piece], mean_rows), axis=-1, keepdims=True)
            onehot = onehot.astype(BF16)
            s_rows = dot(jnp.concatenate([onehot, onehot], axis=1), s_both)
            this = (onehot_t.astype(BF16), c, s_rows, q_ref, gate_ref, piece)
        if last is not None:
            onehot_t, c, s_rows, q_ref, gate_ref, piece = last
            at = (number - 1) * block
            d = (gate_ref[piece] * (s_rows - c * q_ref[piece].astype(F32))).astype(BF16)
            d_ref[at : at + block, :] = d
            sums += dot(onehot_t, d)
            if at + block > G_DEV:
                pick = (rim_row == senders_ref[:, at : at + block]).astype(F32).astype(BF16)
                rim += dot(pick, d)
        last = this

    each = slots // chunks
    for k, sums_ref in enumerate(sums_refs):
        sums_ref[:each, :] = sums[k * each : (k + 1) * each]
        for at in range(0, width, LANES):
            sums_ref[each : 2 * each, at : at + LANES] = ids_ref[k * each : (k + 1) * each, :]
    sums_refs[1][2 * each :, :] = rim


def after(me, ids, slots, senders, weight, gain, parts, pieces, owned, caps, chunks, block=512):
    edges, width = slots.shape[1], weight.shape[0]
    each = ids.shape[0] // chunks
    sizes = [2 * each + (RIM if k == 1 else 0) for k in range(chunks)]
    return pl.pallas_call(
        functools.partial(after_kernel, len(parts), chunks, owned, caps, block),
        in_specs=[SMEM] + [VMEM] * (5 + 3 * len(parts) + len(pieces)),
        out_specs=[VMEM] * (1 + chunks),
        out_shape=[in_vmem((edges, width), BF16)] + [in_vmem((size, width), F32) for size in sizes],
        cost_estimate=cost(6 * edges * width * width, 8 * edges * width),
        compiler_params=params(20),
        name="after",
    )(me, ids, slots, senders, weight, gain, *[a for part in parts for a in part], *pieces)


def segments_kernel(block, starts_ref, senders_ref, d_ref, total_ref):
    edges, width = d_ref.shape
    total_ref[:8, :] = jnp.zeros((8, width), F32)
    row = lax.broadcasted_iota(jnp.int32, (block + 16, block), 0)
    for at in range(0, edges, block):
        base = pl.multiple_of(starts_ref[at] // 8 * 8, 8)
        onehot = (row == senders_ref[:, at : at + block] - base).astype(F32).astype(BF16)
        sums = dot(onehot, d_ref[at : at + block, :])
        total_ref[pl.ds(base, 8), :] += sums[:8]
        total_ref[pl.ds(pl.multiple_of(base + 8, 8), block + 8), :] = sums[8:]


def segments(senders, d_preact, block=256):
    edges, width = d_preact.shape
    return pl.pallas_call(
        functools.partial(segments_kernel, block),
        in_specs=[SMEM] + [VMEM] * 2,
        out_specs=VMEM,
        out_shape=in_vmem((G_DEV + RIM + block + 16, width), F32),
        cost_estimate=cost(4 * edges * width * width, 4 * edges * width),
        compiler_params=params(16),
        name="segments",
    )(senders, senders.reshape(1, edges), d_preact)


def grid_kernel(block, total_ref, carried_ref, weight_ref, out_hbm, out_ref, sem):
    weight = weight_ref[...]
    copies = []
    for k, at in enumerate(range(0, G_DEV, block)):
        rows = total_ref[at : at + block, :]
        if at == 0:
            rim = carried_ref[carried_ref.shape[0] - RIM :, :]
            rows = jnp.concatenate([rows[:RIM] + rim, rows[RIM:]], axis=0)
        out_ref[at : at + block, :] = dot_t(rows.astype(BF16), weight).astype(BF16)
        copies.append(
            pltpu.make_async_copy(out_ref.at[pl.ds(at, block)], out_hbm.at[pl.ds(at, block)], sem.at[k])
        )
        copies[-1].start()
    for copy in copies:
        copy.wait()


def grid_rows(total, carried, weight, block=512):
    width = weight.shape[0]
    return pl.pallas_call(
        functools.partial(grid_kernel, block),
        in_specs=[VMEM] * 3,
        out_specs=HBM,
        out_shape=like((G_DEV, width), BF16),
        scratch_shapes=[pltpu.VMEM((G_DEV, width), BF16), DMA((G_DEV // block,))],
        cost_estimate=cost(2 * G_DEV * width * width, 6 * G_DEV * width),
        compiler_params=params(16),
        name="grid_rows",
    )(total, carried, weight)


def regroup_kernel(groups, parts, rows, *refs):
    outs = refs[parts + 1 :]
    low = groups // len(outs)
    each = rows // groups
    for j, out_ref in enumerate(outs):
        half = out_ref.shape[0] // 2
        for g in range(low):
            for k in range(parts):
                to, at = (g * parts + k) * each, (j * low + g) * each
                out_ref[to : to + each, :] = refs[k][at : at + each, :]
                out_ref[half + to : half + to + each, :] = refs[k][rows + at : rows + at + each, :]


def regroup(arrived, radix, low, after):
    height, width = arrived[0].shape
    parts = len(arrived)
    return pl.pallas_call(
        functools.partial(regroup_kernel, radix * low, parts, height // 2),
        in_specs=[VMEM] * parts + [ANY],
        out_specs=[VMEM] * radix,
        out_shape=[in_vmem((height * parts // radix, width), arrived[0].dtype)] * radix,
        cost_estimate=cost(0, 8 * height * parts * width),
        compiler_params=params(8),
        name="regroup",
    )(*arrived, after)


def mesh_kernel(parts, *refs):
    pieces, weight_ref, out_ref = refs[:parts], refs[parts], refs[-1]
    owned, width = out_ref.shape
    half = pieces[0].shape[0] // 2
    rows = jnp.concatenate([piece[:half, :] for piece in pieces], axis=0)
    ids = jnp.concatenate([piece[half:, :LANES] for piece in pieces], axis=0)
    ids = ids.T[:owned].astype(jnp.int32)
    pick = (lax.broadcasted_iota(jnp.int32, ids.shape, 0) == ids).astype(F32).astype(BF16)
    high, low = split(rows)
    high, low = split(dot(pick, high) + dot(pick, low))
    both = dot_t(jnp.concatenate([high, low], axis=0), weight_ref[...])
    out_ref[...] = (both[:owned] + both[owned:]).astype(BF16)


def mesh_rows(pieces, weight, owned, after):
    width = weight.shape[0]
    return pl.pallas_call(
        functools.partial(mesh_kernel, len(pieces)),
        in_specs=[VMEM] * (len(pieces) + 1) + [ANY],
        out_specs=VMEM,
        out_shape=like((owned, width), BF16),
        cost_estimate=cost(2 * owned * width * width, 2 * width * width),
        compiler_params=params(8),
        name="mesh_rows",
    )(*pieces, weight, in_hbm(after))


def on_device(
    saved_preact,
    edge_senders,
    edge_slots,
    mesh_requests,
    mesh_cotangent,
    out_weight,
    out_bias,
    ln_gain,
    grid_weight,
    mesh_weight,
):
    count = lax.axis_size("band")
    me = lax.axis_index("band")
    owned, width = mesh_cotangent.shape
    edges = saved_preact.shape[0]
    stages = stages_of(count)

    sources = (
        out_weight,
        out_bias.reshape(1, width),
        grid_weight,
        mesh_weight,
        ln_gain.reshape(1, width),
        mesh_cotangent,
    )
    weight, bias, weight_g, weight_m, gain, own_rows, ids, more, *first = first_part(
        saved_preact, edges // 3, sources, me.reshape(1), mesh_requests.swapaxes(1, 2)
    )

    held = [mesh_cotangent]
    for number, (shift, radix) in enumerate(stages):
        if number == 1:
            held = [join([own_rows, *held[1:]], first[0])]
        elif number > 1:
            held = [join(held, ids)]
        held += [swap(held[0], count, j << shift) for j in range(1, radix)]
        if number == 1:
            second = second_part(more, weight, bias, held[0])

    back = stages[::-1]
    d_preact, *chunks = after(
        me.reshape(1),
        ids,
        edge_slots.reshape(1, edges),
        edge_senders.reshape(1, edges),
        weight,
        gain,
        [first, second],
        held,
        owned,
        mesh_requests.shape[2],
        back[0][1],
    )

    total = segments(edge_senders, d_preact)
    arrived, left = None, count
    for shift, radix in back:
        if arrived is not None:
            chunks = regroup(arrived, radix, left // radix, total)
        left //= radix
        arrived = [chunks[0]] + [pass_on(chunks[j], count, j << shift) for j in range(1, radix)]
        if shift == 0:
            grid_adjoint = grid_rows(total, arrived[1], weight_g)
    mesh_adjoint = mesh_rows(arrived, weight_m, owned, grid_adjoint)
    return (grid_adjoint, mesh_adjoint)


def solution(mesh):
    in_specs = (
        P(("groups", "band"), None),
        P("band"),
        P("band"),
        P("band", None, None),
        P(("groups", "band"), None),
        P(),
        P(),
        P(),
        P(),
        P(),
    )
    out_specs = (P(("groups", "band"), None), P(("groups", "band"), None))
    return jax.shard_map(
        on_device, mesh=mesh, in_specs=in_specs, out_specs=out_specs, check_vma=False
    )
```

```python
import functools

import jax
import jax.numpy as jnp
from jax import lax
from jax.experimental import pallas as pl
from jax.experimental.pallas import tpu as pltpu
from jax.sharding import PartitionSpec as P

G_DEV = 2048
RIM = 128
LANES = 128
EPS = 1e-05
MIB = 1 << 20

BF16 = jnp.bfloat16
F32 = jnp.float32
VMEM = pl.BlockSpec(memory_space=pltpu.VMEM)
SMEM = pl.BlockSpec(memory_space=pltpu.SMEM)
HBM = pl.BlockSpec(memory_space=pltpu.HBM)
ANY = pl.BlockSpec(memory_space=pl.ANY)
DMA = pltpu.SemaphoreType.DMA


def stages_of(count):
    top = count.bit_length() - 1
    assert count == 1 << top
    stages = []
    while top > 0:
        low = max(0, top - 2)
        stages.append((low, 1 << (top - low)))
        top = low
    return stages


def distance_of(row, caps, count):
    group, distance, left = row // caps, 0, count
    for shift, radix in reversed(stages_of(count)):
        left //= radix
        distance = distance + ((group // left) % radix << shift)
    return distance


def swap(block, count, mask):
    return lax.ppermute(block, "band", [(i, i ^ mask) for i in range(count)])


def pass_on(block, count, distance):
    return lax.ppermute(block, "band", [(i, (i + distance) % count) for i in range(count)])


def like(shape, dtype):
    return jax.ShapeDtypeStruct(shape, dtype)


def in_hbm(x):
    return pltpu.with_memory_space_constraint(x, pltpu.HBM)


def in_vmem(shape, dtype):
    return pltpu.VMEM(shape, dtype)


def dot(a, b):
    return jnp.dot(a, b, preferred_element_type=F32)


def dot_t(a, b):
    return lax.dot_general(a, b, (((1,), (1,)), ((), ())), preferred_element_type=F32)


def split(x):
    high = x.astype(BF16)
    return high, (x - high.astype(F32)).astype(BF16)


def cost(flops, size):
    return pl.CostEstimate(flops=int(flops), bytes_accessed=int(size), transcendentals=0)


def params(limit):
    return pltpu.CompilerParams(vmem_limit_bytes=limit * MIB)


def products(pre, weight, bias):
    p = pre.astype(F32)
    s = 0.5 * jnp.tanh(0.5 * p) + 0.5
    h = p * s
    return dot(h.astype(BF16), weight) + bias, s + h * (1.0 - s)


def edge_blocks(pre_ref, weight, bias, normed_ref, q_ref, gate_ref, block, arrive):
    rows, last = pre_ref.shape[0], None
    for at in range(0, rows + block, block):
        this = None
        if at < rows:
            arrive(at)
            this = products(pre_ref[at : at + block], weight, bias)
        if last is not None:
            out, gate = last
            centre = out - jnp.mean(out, axis=-1, keepdims=True)
            inv = lax.rsqrt(jnp.mean(centre * centre, axis=-1, keepdims=True) + EPS)
            normed = (centre * inv).astype(BF16)
            piece = slice(at - block, at)
            normed_ref[piece] = normed
            q_ref[piece] = dot_t(normed, weight).astype(BF16)
            gate_ref[piece] = gate * inv
        last = this


def first_kernel(block, copies, pre_hbm, *refs):
    sources, (me_ref, requests_hbm), refs = refs[:copies], refs[copies : copies + 2], refs[copies + 2 :]
    targets, refs = refs[:copies], refs[copies:]
    ids_ref, other_ref, normed_ref, q_ref, gate_ref, pre_ref, requests_ref, sem = refs
    rows = normed_ref.shape[0]

    def load(k, source, target):
        return pltpu.make_async_copy(source, target, sem.at[k])

    others = [load(k, a, b) for k, (a, b) in enumerate(zip(sources, targets))]
    starts = list(range(0, rows, block))
    more_rows = other_ref.shape[0]
    loads = [
        load(copies + k, pre_hbm.at[pl.ds(at, block)], pre_ref.at[pl.ds(at, block)])
        for k, at in enumerate(starts)
    ]
    more = load(copies + len(loads), pre_hbm.at[pl.ds(rows, more_rows)], other_ref)
    asked = load(copies + len(loads) + 1, requests_hbm, requests_ref)
    for copy in others[:2] + loads + others[2:] + [more, asked]:
        copy.start()
    for copy in others[:2]:
        copy.wait()
    edge_blocks(
        pre_ref,
        targets[0][...],
        targets[1][...],
        normed_ref,
        q_ref,
        gate_ref,
        block,
        lambda at: loads[at // block].wait(),
    )
    for copy in others[2:] + [more, asked]:
        copy.wait()
    slots, caps = ids_ref.shape[0], requests_ref.shape[1]
    count = slots // caps
    row = lax.broadcasted_iota(jnp.int32, ids_ref.shape, 0)
    ids = jnp.zeros(ids_ref.shape, jnp.int32)
    for r in range(slots):
        owner = (me_ref[0] + distance_of(r, caps, count)) % count
        ids = jnp.where(row == r, requests_ref[0, r % caps, owner], ids)
    ids_ref[...] = ids.astype(F32)


def first_part(preact, rows, sources, me, requests, block=512):
    edges, width = preact.shape
    copies = len(sources)
    outs = [in_vmem(a.shape, a.dtype) for a in sources]
    outs += [in_vmem((requests.shape[1] * requests.shape[2], LANES), F32)]
    outs += [in_vmem((edges - rows, width), BF16)]
    outs += [in_vmem((rows, width), BF16)] * 2 + [in_vmem((rows, width), F32)]
    return pl.pallas_call(
        functools.partial(first_kernel, block, copies),
        in_specs=[HBM] * (1 + copies) + [SMEM, HBM],
        out_specs=[VMEM] * len(outs),
        out_shape=outs,
        scratch_shapes=[
            pltpu.VMEM((rows, width), BF16),
            pltpu.SMEM(requests.shape, jnp.int32),
            DMA((copies + rows // block + 2,)),
        ],
        cost_estimate=cost(6 * rows * width * width, 10 * rows * width),
        compiler_params=params(16),
        name="first_part",
    )(in_hbm(preact), *[in_hbm(a) for a in sources], me, in_hbm(requests))


def second_kernel(block, pre_ref, weight_ref, bias_ref, after_ref, normed_ref, q_ref, gate_ref):
    edge_blocks(
        pre_ref, weight_ref[...], bias_ref[...], normed_ref, q_ref, gate_ref, block, lambda at: None
    )


def second_part(pre, weight, bias, after, block=512):
    rows, width = pre.shape
    outs = [in_vmem((rows, width), BF16)] * 2 + [in_vmem((rows, width), F32)]
    return pl.pallas_call(
        functools.partial(second_kernel, block),
        in_specs=[VMEM, VMEM, VMEM, ANY],
        out_specs=[VMEM] * len(outs),
        out_shape=outs,
        cost_estimate=cost(6 * rows * width * width, 10 * rows * width),
        compiler_params=params(16),
        name="second_part",
    )(pre, weight, bias, after)


def join_kernel(parts, *refs):
    out_ref, rows = refs[-1], refs[0].shape[0]
    for k in range(parts):
        out_ref[k * rows : (k + 1) * rows, :] = refs[k][...]


def join(pieces, after):
    rows, width = pieces[0].shape
    return pl.pallas_call(
        functools.partial(join_kernel, len(pieces)),
        in_specs=[VMEM] * len(pieces) + [ANY],
        out_specs=VMEM,
        out_shape=in_vmem((len(pieces) * rows, width), pieces[0].dtype),
        cost_estimate=cost(0, 4 * len(pieces) * rows * width),
        compiler_params=params(8),
        name="join",
    )(*pieces, after)


def height_of(rows):
    return 2 * rows + max(rows, 16)


def store_rows(ref, sums, ids):
    rows, width = sums.shape
    high, low = split(sums)
    ref[: 2 * rows, :] = jnp.concatenate([high.astype(F32), low.astype(F32)], axis=0).astype(BF16)
    if rows < 16:
        ids = jnp.concatenate([ids, jnp.zeros((16 - rows, ids.shape[1]), F32)], axis=0)
    for at in range(0, width, LANES):
        ref[2 * rows : height_of(rows), at : at + LANES] = ids.astype(BF16)


def load_rows(ref, rows):
    both = ref[: 2 * rows, :].astype(F32)
    ids = ref[2 * rows : height_of(rows), :LANES].astype(F32)
    return both[:rows] + both[rows:], ids[:rows]


def after_kernel(
    parts, chunks, owned, caps, block, me_ref, ids_ref, slots_ref, senders_ref, weight_ref, gain_ref, *refs
):
    edge_refs = [refs[3 * k : 3 * k + 3] for k in range(parts)]
    refs = refs[3 * parts :]
    d_ref, sums_refs = refs[-1 - chunks], refs[-chunks:]
    pieces = refs[: -1 - chunks]
    slots = ids_ref.shape[0]
    count = slots // caps
    edges, width = d_ref.shape
    me = me_ref[0]
    weight = weight_ref[...]

    row = lax.broadcasted_iota(jnp.int32, (slots, 1), 0)
    owner = (distance_of(row, caps, count) + me) % count
    far, place, step = owner ^ me, jnp.zeros_like(row), 1
    for shift, radix in stages_of(count):
        place = place + ((far >> shift) & (radix - 1)) * step
        step *= radix
    place = place * owned + ids_ref[...][:, :1].astype(jnp.int32)
    piece_rows = pieces[0].shape[0]
    column = lax.broadcasted_iota(jnp.int32, (slots, piece_rows), 1)
    rows = jnp.zeros((slots, width), F32)
    for k, piece in enumerate(pieces):
        pick = (place == column + k * piece_rows).astype(F32).astype(BF16)
        rows += dot(pick, piece[...])
    rows = rows * gain_ref[...]
    rows = rows - jnp.mean(rows, axis=-1, keepdims=True)
    mean_rows = (rows * (1.0 / width)).astype(BF16)
    both = dot_t(jnp.concatenate(split(rows), axis=0), weight)
    s_both = jnp.concatenate(split(both[:slots] + both[slots:]), axis=0)

    key = owner * caps + row % caps
    rim_row = lax.broadcasted_iota(jnp.int32, (RIM, block), 0) + G_DEV
    sums = jnp.zeros((slots, width), F32)
    rim = jnp.zeros((RIM, width), F32)
    edge_at = [(part, at) for part in edge_refs for at in range(0, part[0].shape[0], block)]
    last = None
    for number in range(len(edge_at) + 1):
        this = None
        if number < len(edge_at):
            (normed_ref, q_ref, gate_ref), at = edge_at[number]
            piece = slice(at, at + block)
            onehot_t = (key == slots_ref[:, number * block : (number + 1) * block]).astype(F32)
            onehot = onehot_t.T
            c = jnp.sum(onehot * dot_t(normed_ref[piece], mean_rows), axis=-1, keepdims=True)
            onehot = onehot.astype(BF16)
            s_rows = dot(jnp.concatenate([onehot, onehot], axis=1), s_both)
            this = (onehot_t.astype(BF16), c, s_rows, q_ref, gate_ref, piece)
        if last is not None:
            onehot_t, c, s_rows, q_ref, gate_ref, piece = last
            at = (number - 1) * block
            d = (gate_ref[piece] * (s_rows - c * q_ref[piece].astype(F32))).astype(BF16)
            d_ref[at : at + block, :] = d
            sums += dot(onehot_t, d)
            if at + block > G_DEV:
                pick = (rim_row == senders_ref[:, at : at + block]).astype(F32).astype(BF16)
                rim += dot(pick, d)
        last = this

    each = slots // chunks
    for k, sums_ref in enumerate(sums_refs):
        piece = slice(k * each, (k + 1) * each)
        store_rows(sums_ref, sums[piece], ids_ref[piece, :])
    sums_refs[1][sums_refs[1].shape[0] - RIM :, :] = rim.astype(BF16)


def after(me, ids, slots, senders, weight, gain, parts, pieces, owned, caps, chunks, block=512):
    edges, width = slots.shape[1], weight.shape[0]
    each = ids.shape[0] // chunks
    sizes = [height_of(each) + (RIM if k == 1 else 0) for k in range(chunks)]
    return pl.pallas_call(
        functools.partial(after_kernel, len(parts), chunks, owned, caps, block),
        in_specs=[SMEM] + [VMEM] * (5 + 3 * len(parts) + len(pieces)),
        out_specs=[VMEM] * (1 + chunks),
        out_shape=[in_vmem((edges, width), BF16)] + [in_vmem((size, width), BF16) for size in sizes],
        cost_estimate=cost(6 * edges * width * width, 8 * edges * width),
        compiler_params=params(20),
        name="after",
    )(me, ids, slots, senders, weight, gain, *[a for part in parts for a in part], *pieces)


def segments_kernel(block, starts_ref, senders_ref, d_ref, total_ref):
    edges, width = d_ref.shape
    total_ref[:8, :] = jnp.zeros((8, width), F32)
    row = lax.broadcasted_iota(jnp.int32, (block + 16, block), 0)
    for at in range(0, edges, block):
        base = pl.multiple_of(starts_ref[at] // 8 * 8, 8)
        onehot = (row == senders_ref[:, at : at + block] - base).astype(F32).astype(BF16)
        sums = dot(onehot, d_ref[at : at + block, :])
        total_ref[pl.ds(base, 8), :] += sums[:8]
        total_ref[pl.ds(pl.multiple_of(base + 8, 8), block + 8), :] = sums[8:]


def segments(senders, d_preact, block=256):
    edges, width = d_preact.shape
    return pl.pallas_call(
        functools.partial(segments_kernel, block),
        in_specs=[SMEM] + [VMEM] * 2,
        out_specs=VMEM,
        out_shape=in_vmem((G_DEV + RIM + block + 16, width), F32),
        cost_estimate=cost(4 * edges * width * width, 4 * edges * width),
        compiler_params=params(16),
        name="segments",
    )(senders, senders.reshape(1, edges), d_preact)


def grid_kernel(block, total_ref, carried_ref, weight_ref, out_hbm, out_ref, sem):
    weight = weight_ref[...]
    copies = []
    for k, at in enumerate(range(0, G_DEV, block)):
        rows = total_ref[at : at + block, :]
        if at == 0:
            rim = carried_ref[carried_ref.shape[0] - RIM :, :].astype(F32)
            rows = jnp.concatenate([rows[:RIM] + rim, rows[RIM:]], axis=0)
        out_ref[at : at + block, :] = dot_t(rows.astype(BF16), weight).astype(BF16)
        copies.append(
            pltpu.make_async_copy(out_ref.at[pl.ds(at, block)], out_hbm.at[pl.ds(at, block)], sem.at[k])
        )
        copies[-1].start()
    for copy in copies:
        copy.wait()


def grid_rows(total, carried, weight, block=512):
    width = weight.shape[0]
    return pl.pallas_call(
        functools.partial(grid_kernel, block),
        in_specs=[VMEM] * 3,
        out_specs=HBM,
        out_shape=like((G_DEV, width), BF16),
        scratch_shapes=[pltpu.VMEM((G_DEV, width), BF16), DMA((G_DEV // block,))],
        cost_estimate=cost(2 * G_DEV * width * width, 6 * G_DEV * width),
        compiler_params=params(16),
        name="grid_rows",
    )(total, carried, weight)


def regroup_kernel(groups, parts, rows, *refs):
    outs = refs[parts + 1 :]
    low = groups // len(outs)
    each = rows // groups
    loaded = [load_rows(ref, rows) for ref in refs[:parts]]
    for j, out_ref in enumerate(outs):
        spans = [(k, (j * low + g) * each) for g in range(low) for k in range(parts)]
        sums = jnp.concatenate([loaded[k][0][at : at + each] for k, at in spans], axis=0)
        ids = jnp.concatenate([loaded[k][1][at : at + each] for k, at in spans], axis=0)
        store_rows(out_ref, sums, ids)


def regroup(arrived, radix, low, rows, after):
    width = arrived[0].shape[1]
    parts = len(arrived)
    return pl.pallas_call(
        functools.partial(regroup_kernel, radix * low, parts, rows),
        in_specs=[VMEM] * parts + [ANY],
        out_specs=[VMEM] * radix,
        out_shape=[in_vmem((height_of(rows * parts // radix), width), BF16)] * radix,
        cost_estimate=cost(0, 8 * rows * parts * width),
        compiler_params=params(8),
        name="regroup",
    )(*arrived, after)


def mesh_kernel(parts, size, *refs):
    pieces, weight_ref, out_ref = refs[:parts], refs[parts], refs[-1]
    owned, width = out_ref.shape
    loaded = [load_rows(piece, size) for piece in pieces]
    rows = jnp.concatenate([sums for sums, _ in loaded], axis=0)
    ids = jnp.concatenate([ids for _, ids in loaded], axis=0).T[:owned].astype(jnp.int32)
    pick = (lax.broadcasted_iota(jnp.int32, ids.shape, 0) == ids).astype(F32).astype(BF16)
    high, low = split(rows)
    high, low = split(dot(pick, high) + dot(pick, low))
    both = dot_t(jnp.concatenate([high, low], axis=0), weight_ref[...])
    out_ref[...] = (both[:owned] + both[owned:]).astype(BF16)


def mesh_rows(pieces, size, weight, owned, after):
    width = weight.shape[0]
    return pl.pallas_call(
        functools.partial(mesh_kernel, len(pieces), size),
        in_specs=[VMEM] * (len(pieces) + 1) + [ANY],
        out_specs=VMEM,
        out_shape=like((owned, width), BF16),
        cost_estimate=cost(2 * owned * width * width, 2 * width * width),
        compiler_params=params(8),
        name="mesh_rows",
    )(*pieces, weight, in_hbm(after))


def on_device(
    saved_preact,
    edge_senders,
    edge_slots,
    mesh_requests,
    mesh_cotangent,
    out_weight,
    out_bias,
    ln_gain,
    grid_weight,
    mesh_weight,
):
    count = lax.axis_size("band")
    me = lax.axis_index("band")
    owned, width = mesh_cotangent.shape
    edges = saved_preact.shape[0]
    stages = stages_of(count)

    sources = (
        out_weight,
        out_bias.reshape(1, width),
        grid_weight,
        mesh_weight,
        ln_gain.reshape(1, width),
        mesh_cotangent,
    )
    weight, bias, weight_g, weight_m, gain, own_rows, ids, more, *first = first_part(
        saved_preact, edges // 3, sources, me.reshape(1), mesh_requests.swapaxes(1, 2)
    )

    held = [mesh_cotangent]
    for number, (shift, radix) in enumerate(stages):
        if number == 1:
            held = [join([own_rows, *held[1:]], first[0])]
        elif number > 1:
            held = [join(held, ids)]
        held += [swap(held[0], count, j << shift) for j in range(1, radix)]
        if number == 1:
            second = second_part(more, weight, bias, held[0])

    back = stages[::-1]
    d_preact, *chunks = after(
        me.reshape(1),
        ids,
        edge_slots.reshape(1, edges),
        edge_senders.reshape(1, edges),
        weight,
        gain,
        [first, second],
        held,
        owned,
        mesh_requests.shape[2],
        back[0][1],
    )

    total = segments(edge_senders, d_preact)
    arrived, left, size = None, count, ids.shape[0] // back[0][1]
    for shift, radix in back:
        if arrived is not None:
            chunks = regroup(arrived, radix, left // radix, size, total)
            size = size * len(arrived) // radix
        left //= radix
        arrived = [chunks[0]] + [pass_on(chunks[j], count, j << shift) for j in range(1, radix)]
        if shift == 0:
            grid_adjoint = grid_rows(total, arrived[1], weight_g)
    mesh_adjoint = mesh_rows(arrived, size, weight_m, owned, grid_adjoint)
    return (grid_adjoint, mesh_adjoint)


def solution(mesh):
    in_specs = (
        P(("groups", "band"), None),
        P("band"),
        P("band"),
        P("band", None, None),
        P(("groups", "band"), None),
        P(),
        P(),
        P(),
        P(),
        P(),
    )
    out_specs = (P(("groups", "band"), None), P(("groups", "band"), None))
    return jax.shard_map(
        on_device, mesh=mesh, in_specs=in_specs, out_specs=out_specs, check_vma=False
    )
```

```python
import functools

import jax
import jax.numpy as jnp
from jax import lax
from jax.experimental import pallas as pl
from jax.experimental.pallas import tpu as pltpu
from jax.sharding import PartitionSpec as P

G_DEV = 2048
RIM = 128
LANES = 128
EPS = 1e-05
MIB = 1 << 20

BF16 = jnp.bfloat16
F32 = jnp.float32
VMEM = pl.BlockSpec(memory_space=pltpu.VMEM)
SMEM = pl.BlockSpec(memory_space=pltpu.SMEM)
HBM = pl.BlockSpec(memory_space=pltpu.HBM)
ANY = pl.BlockSpec(memory_space=pl.ANY)
DMA = pltpu.SemaphoreType.DMA


def stages_of(count):
    top = count.bit_length() - 1
    assert count == 1 << top
    stages = []
    while top > 0:
        low = max(0, top - 2)
        stages.append((low, 1 << (top - low)))
        top = low
    return stages


def distance_of(row, caps, count):
    group, distance, left = row // caps, 0, count
    for shift, radix in reversed(stages_of(count)):
        left //= radix
        distance = distance + ((group // left) % radix << shift)
    return distance


def swap(block, count, mask):
    return lax.ppermute(block, "band", [(i, i ^ mask) for i in range(count)])


def like(shape, dtype):
    return jax.ShapeDtypeStruct(shape, dtype)


def in_hbm(x):
    return pltpu.with_memory_space_constraint(x, pltpu.HBM)


def in_vmem(shape, dtype):
    return pltpu.VMEM(shape, dtype)


def dot(a, b):
    return jnp.dot(a, b, preferred_element_type=F32)


def dot_t(a, b):
    return lax.dot_general(a, b, (((1,), (1,)), ((), ())), preferred_element_type=F32)


def split(x):
    high = x.astype(BF16)
    return high, (x - high.astype(F32)).astype(BF16)


def cost(flops, size):
    return pl.CostEstimate(flops=int(flops), bytes_accessed=int(size), transcendentals=0)


def params(limit):
    return pltpu.CompilerParams(vmem_limit_bytes=limit * MIB)


def products(pre, weight, bias):
    p = pre.astype(F32)
    s = 0.5 * jnp.tanh(0.5 * p) + 0.5
    h = p * s
    return dot(h.astype(BF16), weight) + bias, s + h * (1.0 - s)


def edge_blocks(pre_ref, weight, bias, normed_ref, q_ref, gate_ref, block, arrive):
    rows, last = pre_ref.shape[0], None
    for at in range(0, rows + block, block):
        this = None
        if at < rows:
            arrive(at)
            this = products(pre_ref[at : at + block], weight, bias)
        if last is not None:
            out, gate = last
            centre = out - jnp.mean(out, axis=-1, keepdims=True)
            inv = lax.rsqrt(jnp.mean(centre * centre, axis=-1, keepdims=True) + EPS)
            normed = (centre * inv).astype(BF16)
            piece = slice(at - block, at)
            normed_ref[piece] = normed
            q_ref[piece] = dot_t(normed, weight).astype(BF16)
            gate_ref[piece] = gate * inv
        last = this


def first_kernel(block, copies, pre_hbm, *refs):
    sources, (me_ref, requests_hbm), refs = refs[:copies], refs[copies : copies + 2], refs[copies + 2 :]
    targets, refs = refs[:copies], refs[copies:]
    ids_ref, other_ref, normed_ref, q_ref, gate_ref, pre_ref, requests_ref, sem = refs
    rows = normed_ref.shape[0]

    def load(k, source, target):
        return pltpu.make_async_copy(source, target, sem.at[k])

    others = [load(k, a, b) for k, (a, b) in enumerate(zip(sources, targets))]
    starts = list(range(0, rows, block))
    more_rows = other_ref.shape[0]
    loads = [
        load(copies + k, pre_hbm.at[pl.ds(at, block)], pre_ref.at[pl.ds(at, block)])
        for k, at in enumerate(starts)
    ]
    more = load(copies + len(loads), pre_hbm.at[pl.ds(rows, more_rows)], other_ref)
    asked = load(copies + len(loads) + 1, requests_hbm, requests_ref)
    for copy in others[:2] + loads + others[2:] + [more, asked]:
        copy.start()
    for copy in others[:2]:
        copy.wait()
    edge_blocks(
        pre_ref,
        targets[0][...],
        targets[1][...],
        normed_ref,
        q_ref,
        gate_ref,
        block,
        lambda at: loads[at // block].wait(),
    )
    for copy in others[2:] + [more, asked]:
        copy.wait()
    slots, caps = ids_ref.shape[0], requests_ref.shape[1]
    count = slots // caps
    row = lax.broadcasted_iota(jnp.int32, ids_ref.shape, 0)
    ids = jnp.zeros(ids_ref.shape, jnp.int32)
    for r in range(slots):
        owner = me_ref[0] ^ distance_of(r, caps, count)
        ids = jnp.where(row == r, requests_ref[0, r % caps, owner], ids)
    ids_ref[...] = ids.astype(F32)


def first_part(preact, rows, sources, me, requests, block=512):
    edges, width = preact.shape
    copies = len(sources)
    outs = [in_vmem(a.shape, a.dtype) for a in sources]
    outs += [in_vmem((requests.shape[1] * requests.shape[2], LANES), F32)]
    outs += [in_vmem((edges - rows, width), BF16)]
    outs += [in_vmem((rows, width), BF16)] * 2 + [in_vmem((rows, width), F32)]
    return pl.pallas_call(
        functools.partial(first_kernel, block, copies),
        in_specs=[HBM] * (1 + copies) + [SMEM, HBM],
        out_specs=[VMEM] * len(outs),
        out_shape=outs,
        scratch_shapes=[
            pltpu.VMEM((rows, width), BF16),
            pltpu.SMEM(requests.shape, jnp.int32),
            DMA((copies + rows // block + 2,)),
        ],
        cost_estimate=cost(6 * rows * width * width, 10 * rows * width),
        compiler_params=params(16),
        name="first_part",
    )(in_hbm(preact), *[in_hbm(a) for a in sources], me, in_hbm(requests))


def second_kernel(block, pre_ref, weight_ref, bias_ref, after_ref, normed_ref, q_ref, gate_ref):
    edge_blocks(
        pre_ref, weight_ref[...], bias_ref[...], normed_ref, q_ref, gate_ref, block, lambda at: None
    )


def second_part(pre, weight, bias, after, block=512):
    rows, width = pre.shape
    outs = [in_vmem((rows, width), BF16)] * 2 + [in_vmem((rows, width), F32)]
    return pl.pallas_call(
        functools.partial(second_kernel, block),
        in_specs=[VMEM, VMEM, VMEM, ANY],
        out_specs=[VMEM] * len(outs),
        out_shape=outs,
        cost_estimate=cost(6 * rows * width * width, 10 * rows * width),
        compiler_params=params(16),
        name="second_part",
    )(pre, weight, bias, after)


def join_kernel(parts, *refs):
    out_ref, rows = refs[-1], refs[0].shape[0]
    for k in range(parts):
        out_ref[k * rows : (k + 1) * rows, :] = refs[k][...]


def join(pieces, after):
    rows, width = pieces[0].shape
    return pl.pallas_call(
        functools.partial(join_kernel, len(pieces)),
        in_specs=[VMEM] * len(pieces) + [ANY],
        out_specs=VMEM,
        out_shape=in_vmem((len(pieces) * rows, width), pieces[0].dtype),
        cost_estimate=cost(0, 4 * len(pieces) * rows * width),
        compiler_params=params(8),
        name="join",
    )(*pieces, after)


def height_of(rows):
    return 2 * rows + max(rows, 16)


def store_rows(ref, sums, ids):
    rows, width = sums.shape
    high, low = split(sums)
    ref[: 2 * rows, :] = jnp.concatenate([high.astype(F32), low.astype(F32)], axis=0).astype(BF16)
    if rows < 16:
        ids = jnp.concatenate([ids, jnp.zeros((16 - rows, ids.shape[1]), F32)], axis=0)
    for at in range(0, width, LANES):
        ref[2 * rows : height_of(rows), at : at + LANES] = ids.astype(BF16)


def load_rows(ref, rows):
    both = ref[: 2 * rows, :].astype(F32)
    ids = ref[2 * rows : height_of(rows), :LANES].astype(F32)
    return both[:rows] + both[rows:], ids[:rows]


def after_kernel(
    parts, chunks, owned, caps, block, me_ref, ids_ref, slots_ref, senders_ref, weight_ref, gain_ref, *refs
):
    edge_refs = [refs[3 * k : 3 * k + 3] for k in range(parts)]
    refs = refs[3 * parts :]
    pieces, (d_ref, rim_ref), sums_refs = refs[: -2 - chunks], refs[-2 - chunks : -chunks], refs[-chunks:]
    slots = ids_ref.shape[0]
    count = slots // caps
    edges, width = d_ref.shape
    me = me_ref[0]
    weight = weight_ref[...]

    row = lax.broadcasted_iota(jnp.int32, (slots, 1), 0)
    distance, place, step = distance_of(row, caps, count), jnp.zeros_like(row), 1
    for shift, radix in stages_of(count):
        place = place + ((distance >> shift) & (radix - 1)) * step
        step *= radix
    place = place * owned + ids_ref[...][:, :1].astype(jnp.int32)
    piece_rows = pieces[0].shape[0]
    column = lax.broadcasted_iota(jnp.int32, (slots, piece_rows), 1)
    rows = jnp.zeros((slots, width), F32)
    for k, piece in enumerate(pieces):
        pick = (place == column + k * piece_rows).astype(F32).astype(BF16)
        rows += dot(pick, piece[...])
    rows = rows * gain_ref[...]
    rows = rows - jnp.mean(rows, axis=-1, keepdims=True)
    mean_rows = (rows * (1.0 / width)).astype(BF16)
    both = dot_t(jnp.concatenate(split(rows), axis=0), weight)
    s_both = jnp.concatenate(split(both[:slots] + both[slots:]), axis=0)

    key = (distance ^ me) * caps + row % caps
    rim_row = lax.broadcasted_iota(jnp.int32, (RIM, block), 0) + G_DEV
    sums = jnp.zeros((slots, width), F32)
    rim = jnp.zeros((RIM, width), F32)
    edge_at = [(part, at) for part in edge_refs for at in range(0, part[0].shape[0], block)]
    last = None
    for number in range(len(edge_at) + 1):
        this = None
        if number < len(edge_at):
            (normed_ref, q_ref, gate_ref), at = edge_at[number]
            piece = slice(at, at + block)
            onehot_t = (key == slots_ref[:, number * block : (number + 1) * block]).astype(F32)
            onehot = onehot_t.T
            c = jnp.sum(onehot * dot_t(normed_ref[piece], mean_rows), axis=-1, keepdims=True)
            onehot = onehot.astype(BF16)
            s_rows = dot(jnp.concatenate([onehot, onehot], axis=1), s_both)
            this = (onehot_t.astype(BF16), c, s_rows, q_ref, gate_ref, piece)
        if last is not None:
            onehot_t, c, s_rows, q_ref, gate_ref, piece = last
            at = (number - 1) * block
            d = (gate_ref[piece] * (s_rows - c * q_ref[piece].astype(F32))).astype(BF16)
            d_ref[at : at + block, :] = d
            sums += dot(onehot_t, d)
            if at + block > G_DEV:
                pick = (rim_row == senders_ref[:, at : at + block]).astype(F32).astype(BF16)
                rim += dot(pick, d)
        last = this

    each = slots // chunks
    for k, sums_ref in enumerate(sums_refs):
        piece = slice(k * each, (k + 1) * each)
        store_rows(sums_ref, sums[piece], ids_ref[piece, :])
    rim_ref[...] = rim.astype(BF16)


def after(me, ids, slots, senders, weight, gain, parts, pieces, owned, caps, chunks, block=512):
    edges, width = slots.shape[1], weight.shape[0]
    each = ids.shape[0] // chunks
    return pl.pallas_call(
        functools.partial(after_kernel, len(parts), chunks, owned, caps, block),
        in_specs=[SMEM] + [VMEM] * (5 + 3 * len(parts) + len(pieces)),
        out_specs=[VMEM] * (2 + chunks),
        out_shape=[in_vmem((edges, width), BF16), in_vmem((RIM, width), BF16)]
        + [in_vmem((height_of(each), width), BF16)] * chunks,
        cost_estimate=cost(6 * edges * width * width, 8 * edges * width),
        compiler_params=params(20),
        name="after",
    )(me, ids, slots, senders, weight, gain, *[a for part in parts for a in part], *pieces)


def segments_kernel(block, starts_ref, senders_ref, d_ref, total_ref):
    edges, width = d_ref.shape
    total_ref[:8, :] = jnp.zeros((8, width), F32)
    row = lax.broadcasted_iota(jnp.int32, (block + 16, block), 0)
    for at in range(0, edges, block):
        base = pl.multiple_of(starts_ref[at] // 8 * 8, 8)
        onehot = (row == senders_ref[:, at : at + block] - base).astype(F32).astype(BF16)
        sums = dot(onehot, d_ref[at : at + block, :])
        total_ref[pl.ds(base, 8), :] += sums[:8]
        total_ref[pl.ds(pl.multiple_of(base + 8, 8), block + 8), :] = sums[8:]


def segments(senders, d_preact, block=256):
    edges, width = d_preact.shape
    return pl.pallas_call(
        functools.partial(segments_kernel, block),
        in_specs=[SMEM] + [VMEM] * 2,
        out_specs=VMEM,
        out_shape=in_vmem((G_DEV + RIM + block + 16, width), F32),
        cost_estimate=cost(4 * edges * width * width, 4 * edges * width),
        compiler_params=params(16),
        name="segments",
    )(senders, senders.reshape(1, edges), d_preact)


def grid_kernel(block, total_ref, carried_ref, weight_ref, out_hbm, out_ref, sem):
    weight = weight_ref[...]
    copies = []
    for k, at in enumerate(range(0, G_DEV, block)):
        rows = total_ref[at : at + block, :]
        if at == 0:
            rows = jnp.concatenate([rows[:RIM] + carried_ref[...].astype(F32), rows[RIM:]], axis=0)
        out_ref[at : at + block, :] = dot_t(rows.astype(BF16), weight).astype(BF16)
        copies.append(
            pltpu.make_async_copy(out_ref.at[pl.ds(at, block)], out_hbm.at[pl.ds(at, block)], sem.at[k])
        )
        copies[-1].start()
    for copy in copies:
        copy.wait()


def grid_rows(total, carried, weight, block=512):
    width = weight.shape[0]
    return pl.pallas_call(
        functools.partial(grid_kernel, block),
        in_specs=[VMEM] * 3,
        out_specs=HBM,
        out_shape=like((G_DEV, width), BF16),
        scratch_shapes=[pltpu.VMEM((G_DEV, width), BF16), DMA((G_DEV // block,))],
        cost_estimate=cost(2 * G_DEV * width * width, 6 * G_DEV * width),
        compiler_params=params(16),
        name="grid_rows",
    )(total, carried, weight)


def regroup_kernel(groups, parts, rows, *refs):
    outs = refs[parts + 1 :]
    low = groups // len(outs)
    each = rows // groups
    loaded = [load_rows(ref, rows) for ref in refs[:parts]]
    for j, out_ref in enumerate(outs):
        spans = [(k, (j * low + g) * each) for g in range(low) for k in range(parts)]
        sums = jnp.concatenate([loaded[k][0][at : at + each] for k, at in spans], axis=0)
        ids = jnp.concatenate([loaded[k][1][at : at + each] for k, at in spans], axis=0)
        store_rows(out_ref, sums, ids)


def regroup(arrived, radix, low, rows, after):
    width = arrived[0].shape[1]
    parts = len(arrived)
    return pl.pallas_call(
        functools.partial(regroup_kernel, radix * low, parts, rows),
        in_specs=[VMEM] * parts + [ANY],
        out_specs=[VMEM] * radix,
        out_shape=[in_vmem((height_of(rows * parts // radix), width), BF16)] * radix,
        cost_estimate=cost(0, 8 * rows * parts * width),
        compiler_params=params(8),
        name="regroup",
    )(*arrived, after)


def mesh_kernel(parts, size, *refs):
    pieces, weight_ref, out_ref = refs[:parts], refs[parts], refs[-1]
    owned, width = out_ref.shape
    loaded = [load_rows(piece, size) for piece in pieces]
    rows = jnp.concatenate([sums for sums, _ in loaded], axis=0)
    ids = jnp.concatenate([ids for _, ids in loaded], axis=0).T[:owned].astype(jnp.int32)
    pick = (lax.broadcasted_iota(jnp.int32, ids.shape, 0) == ids).astype(F32).astype(BF16)
    high, low = split(rows)
    high, low = split(dot(pick, high) + dot(pick, low))
    both = dot_t(jnp.concatenate([high, low], axis=0), weight_ref[...])
    out_ref[...] = (both[:owned] + both[owned:]).astype(BF16)


def mesh_rows(pieces, size, weight, owned, after):
    width = weight.shape[0]
    return pl.pallas_call(
        functools.partial(mesh_kernel, len(pieces), size),
        in_specs=[VMEM] * (len(pieces) + 1) + [ANY],
        out_specs=VMEM,
        out_shape=like((owned, width), BF16),
        cost_estimate=cost(2 * owned * width * width, 2 * width * width),
        compiler_params=params(8),
        name="mesh_rows",
    )(*pieces, weight, in_hbm(after))


def on_device(
    saved_preact,
    edge_senders,
    edge_slots,
    mesh_requests,
    mesh_cotangent,
    out_weight,
    out_bias,
    ln_gain,
    grid_weight,
    mesh_weight,
):
    count = lax.axis_size("band")
    me = lax.axis_index("band")
    owned, width = mesh_cotangent.shape
    edges = saved_preact.shape[0]
    stages = stages_of(count)

    sources = (
        out_weight,
        out_bias.reshape(1, width),
        grid_weight,
        mesh_weight,
        ln_gain.reshape(1, width),
        mesh_cotangent,
    )
    weight, bias, weight_g, weight_m, gain, own_rows, ids, more, *first = first_part(
        saved_preact, edges // 3, sources, me.reshape(1), mesh_requests.swapaxes(1, 2)
    )

    held = [mesh_cotangent]
    for number, (shift, radix) in enumerate(stages):
        if number == 1:
            held = [join([own_rows, *held[1:]], first[0])]
        elif number > 1:
            held = [join(held, ids)]
        held += [swap(held[0], count, j << shift) for j in range(1, radix)]
        if number == 1:
            second = second_part(more, weight, bias, held[0])

    back = stages[::-1]
    d_preact, rim, *chunks = after(
        me.reshape(1),
        ids,
        edge_slots.reshape(1, edges),
        edge_senders.reshape(1, edges),
        weight,
        gain,
        [first, second],
        held,
        owned,
        mesh_requests.shape[2],
        back[0][1],
    )

    total = segments(edge_senders, d_preact)
    carried = lax.ppermute(rim, "band", [(i, i + 1) for i in range(count - 1)])
    arrived, left, size = None, count, ids.shape[0] // back[0][1]
    for shift, radix in back:
        if arrived is not None:
            chunks = regroup(arrived, radix, left // radix, size, total)
            size = size * len(arrived) // radix
        left //= radix
        arrived = [chunks[0]] + [swap(chunks[j], count, j << shift) for j in range(1, radix)]
    grid_adjoint = grid_rows(total, carried, weight_g)
    mesh_adjoint = mesh_rows(arrived, size, weight_m, owned, grid_adjoint)
    return (grid_adjoint, mesh_adjoint)


def solution(mesh):
    in_specs = (
        P(("groups", "band"), None),
        P("band"),
        P("band"),
        P("band", None, None),
        P(("groups", "band"), None),
        P(),
        P(),
        P(),
        P(),
        P(),
    )
    out_specs = (P(("groups", "band"), None), P(("groups", "band"), None))
    return jax.shard_map(
        on_device, mesh=mesh, in_specs=in_specs, out_specs=out_specs, check_vma=False
    )
```

```python
import functools

import jax
import jax.numpy as jnp
from jax import lax
from jax.experimental import pallas as pl
from jax.experimental.pallas import tpu as pltpu
from jax.sharding import PartitionSpec as P

G_DEV = 2048
RIM = 128
LANES = 128
EPS = 1e-05
MIB = 1 << 20

BF16 = jnp.bfloat16
F32 = jnp.float32
VMEM = pl.BlockSpec(memory_space=pltpu.VMEM)
SMEM = pl.BlockSpec(memory_space=pltpu.SMEM)
HBM = pl.BlockSpec(memory_space=pltpu.HBM)
ANY = pl.BlockSpec(memory_space=pl.ANY)
DMA = pltpu.SemaphoreType.DMA


def bits_of(count):
    top = count.bit_length() - 1
    assert count == 1 << top
    return list(range(top))[::-1]


def distance_of(row, caps, count):
    group, distance, left = row // caps, 0, count
    for bit in reversed(bits_of(count)):
        left //= 2
        distance = distance + ((group // left) % 2 << bit)
    return distance


def swap(block, count, mask):
    return lax.ppermute(block, "band", [(i, i ^ mask) for i in range(count)])


def like(shape, dtype):
    return jax.ShapeDtypeStruct(shape, dtype)


def in_hbm(x):
    return pltpu.with_memory_space_constraint(x, pltpu.HBM)


def in_vmem(shape, dtype):
    return pltpu.VMEM(shape, dtype)


def dot(a, b):
    return jnp.dot(a, b, preferred_element_type=F32)


def dot_t(a, b):
    return lax.dot_general(a, b, (((1,), (1,)), ((), ())), preferred_element_type=F32)


def split(x):
    high = x.astype(BF16)
    return high, (x - high.astype(F32)).astype(BF16)


def cost(flops, size):
    return pl.CostEstimate(flops=int(flops), bytes_accessed=int(size), transcendentals=0)


def params(limit):
    return pltpu.CompilerParams(vmem_limit_bytes=limit * MIB)


def products(pre, weight, bias):
    p = pre.astype(F32)
    s = 0.5 * jnp.tanh(0.5 * p) + 0.5
    h = p * s
    return dot(h.astype(BF16), weight) + bias, s + h * (1.0 - s)


def edge_blocks(pre_ref, weight, bias, normed_ref, q_ref, gate_ref, block, arrive):
    rows, last = pre_ref.shape[0], None
    for at in range(0, rows + block, block):
        this = None
        if at < rows:
            arrive(at)
            this = products(pre_ref[at : at + block], weight, bias)
        if last is not None:
            out, gate = last
            centre = out - jnp.mean(out, axis=-1, keepdims=True)
            inv = lax.rsqrt(jnp.mean(centre * centre, axis=-1, keepdims=True) + EPS)
            normed = (centre * inv).astype(BF16)
            piece = slice(at - block, at)
            normed_ref[piece] = normed
            q_ref[piece] = dot_t(normed, weight).astype(BF16)
            gate_ref[piece] = gate * inv
        last = this


def first_kernel(block, copies, pre_hbm, *refs):
    sources, (me_ref, requests_hbm), refs = refs[:copies], refs[copies : copies + 2], refs[copies + 2 :]
    targets, (ids_ref, *refs) = refs[:copies], refs[copies:]
    *later, normed_ref, q_ref, gate_ref, pre_ref, requests_ref, sem = refs
    rows = normed_ref.shape[0]

    def load(k, source, target):
        return pltpu.make_async_copy(source, target, sem.at[k])

    others = [load(k, a, b) for k, (a, b) in enumerate(zip(sources, targets))]
    parts, at = [], 0
    for target in [pre_ref.at[pl.ds(k, block)] for k in range(0, rows, block)] + later:
        size = target.shape[0]
        parts.append(load(copies + len(parts), pre_hbm.at[pl.ds(at, size)], target))
        at += size
    loads, more = parts[: rows // block], parts[rows // block :]
    asked = load(copies + len(parts), requests_hbm, requests_ref)
    for copy in others[:2] + loads + others[2:] + more + [asked]:
        copy.start()
    for copy in others[:2]:
        copy.wait()
    edge_blocks(
        pre_ref,
        targets[0][...],
        targets[1][...],
        normed_ref,
        q_ref,
        gate_ref,
        block,
        lambda at: loads[at // block].wait(),
    )
    for copy in others[2:] + more + [asked]:
        copy.wait()
    slots, caps = ids_ref.shape[0], requests_ref.shape[1]
    count = slots // caps
    row = lax.broadcasted_iota(jnp.int32, ids_ref.shape, 0)
    ids = jnp.zeros(ids_ref.shape, jnp.int32)
    for r in range(slots):
        owner = me_ref[0] ^ distance_of(r, caps, count)
        ids = jnp.where(row == r, requests_ref[0, r % caps, owner], ids)
    ids_ref[...] = ids.astype(F32)


def first_part(preact, sizes, sources, me, requests, block=512):
    width, rows = preact.shape[1], sizes[0]
    copies = len(sources)
    outs = [in_vmem(a.shape, a.dtype) for a in sources]
    outs += [in_vmem((requests.shape[1] * requests.shape[2], LANES), F32)]
    outs += [in_vmem((size, width), BF16) for size in sizes[1:]]
    outs += [in_vmem((rows, width), BF16)] * 2 + [in_vmem((rows, width), F32)]
    return pl.pallas_call(
        functools.partial(first_kernel, block, copies),
        in_specs=[HBM] * (1 + copies) + [SMEM, HBM],
        out_specs=[VMEM] * len(outs),
        out_shape=outs,
        scratch_shapes=[
            pltpu.VMEM((rows, width), BF16),
            pltpu.SMEM(requests.shape, jnp.int32),
            DMA((copies + rows // block + len(sizes),)),
        ],
        cost_estimate=cost(6 * rows * width * width, 10 * rows * width),
        compiler_params=params(16),
        name="first_part",
    )(in_hbm(preact), *[in_hbm(a) for a in sources], me, in_hbm(requests))


def later_kernel(block, pre_ref, weight_ref, bias_ref, after_ref, normed_ref, q_ref, gate_ref):
    edge_blocks(
        pre_ref, weight_ref[...], bias_ref[...], normed_ref, q_ref, gate_ref, block, lambda at: None
    )


def later_part(pre, weight, bias, after, block=512):
    rows, width = pre.shape
    outs = [in_vmem((rows, width), BF16)] * 2 + [in_vmem((rows, width), F32)]
    return pl.pallas_call(
        functools.partial(later_kernel, block),
        in_specs=[VMEM, VMEM, VMEM, ANY],
        out_specs=[VMEM] * len(outs),
        out_shape=outs,
        cost_estimate=cost(6 * rows * width * width, 10 * rows * width),
        compiler_params=params(16),
        name="later_part",
    )(pre, weight, bias, after)


def join_kernel(parts, *refs):
    out_ref, rows = refs[-1], refs[0].shape[0]
    for k in range(parts):
        out_ref[k * rows : (k + 1) * rows, :] = refs[k][...]


def join(pieces, after):
    rows, width = pieces[0].shape
    return pl.pallas_call(
        functools.partial(join_kernel, len(pieces)),
        in_specs=[VMEM] * len(pieces) + [ANY],
        out_specs=VMEM,
        out_shape=in_vmem((len(pieces) * rows, width), pieces[0].dtype),
        cost_estimate=cost(0, 4 * len(pieces) * rows * width),
        compiler_params=params(8),
        name="join",
    )(*pieces, after)


def height_of(rows):
    return 2 * rows + max(rows, 16)


def store_rows(ref, sums, ids):
    rows, width = sums.shape
    high, low = split(sums)
    ref[: 2 * rows, :] = jnp.concatenate([high.astype(F32), low.astype(F32)], axis=0).astype(BF16)
    if rows < 16:
        ids = jnp.concatenate([ids, jnp.zeros((16 - rows, ids.shape[1]), F32)], axis=0)
    for at in range(0, width, LANES):
        ref[2 * rows : height_of(rows), at : at + LANES] = ids.astype(BF16)


def load_rows(ref, rows):
    both = ref[: 2 * rows, :].astype(F32)
    ids = ref[2 * rows : height_of(rows), :LANES].astype(F32)
    return both[:rows] + both[rows:], ids[:rows]


def after_kernel(
    parts, chunks, owned, caps, block, me_ref, ids_ref, slots_ref, senders_ref, weight_ref, gain_ref, *refs
):
    edge_refs = [refs[3 * k : 3 * k + 3] for k in range(parts)]
    refs = refs[3 * parts :]
    pieces, (d_ref, rim_ref), sums_refs = refs[: -2 - chunks], refs[-2 - chunks : -chunks], refs[-chunks:]
    slots = ids_ref.shape[0]
    count = slots // caps
    edges, width = d_ref.shape
    me = me_ref[0]
    weight = weight_ref[...]

    row = lax.broadcasted_iota(jnp.int32, (slots, 1), 0)
    distance, place, step = distance_of(row, caps, count), jnp.zeros_like(row), 1
    for bit in bits_of(count):
        place = place + ((distance >> bit) & 1) * step
        step *= 2
    place = place * owned + ids_ref[...][:, :1].astype(jnp.int32)
    piece_rows = pieces[0].shape[0]
    column = lax.broadcasted_iota(jnp.int32, (slots, piece_rows), 1)
    rows = jnp.zeros((slots, width), F32)
    for k, piece in enumerate(pieces):
        pick = (place == column + k * piece_rows).astype(F32).astype(BF16)
        rows += dot(pick, piece[...])
    rows = rows * gain_ref[...]
    rows = rows - jnp.mean(rows, axis=-1, keepdims=True)
    mean_rows = (rows * (1.0 / width)).astype(BF16)
    both = dot_t(jnp.concatenate(split(rows), axis=0), weight)
    s_both = jnp.concatenate(split(both[:slots] + both[slots:]), axis=0)

    key = (distance ^ me) * caps + row % caps
    rim_row = lax.broadcasted_iota(jnp.int32, (RIM, block), 0) + G_DEV
    sums = jnp.zeros((slots, width), F32)
    rim = jnp.zeros((RIM, width), F32)
    edge_at = [(part, at) for part in edge_refs for at in range(0, part[0].shape[0], block)]
    last = None
    for number in range(len(edge_at) + 1):
        this = None
        if number < len(edge_at):
            (normed_ref, q_ref, gate_ref), at = edge_at[number]
            piece = slice(at, at + block)
            onehot_t = (key == slots_ref[:, number * block : (number + 1) * block]).astype(F32)
            onehot = onehot_t.T
            c = jnp.sum(onehot * dot_t(normed_ref[piece], mean_rows), axis=-1, keepdims=True)
            onehot = onehot.astype(BF16)
            s_rows = dot(jnp.concatenate([onehot, onehot], axis=1), s_both)
            this = (onehot_t.astype(BF16), c, s_rows, q_ref, gate_ref, piece)
        if last is not None:
            onehot_t, c, s_rows, q_ref, gate_ref, piece = last
            at = (number - 1) * block
            d = (gate_ref[piece] * (s_rows - c * q_ref[piece].astype(F32))).astype(BF16)
            d_ref[at : at + block, :] = d
            sums += dot(onehot_t, d)
            if at + block > G_DEV:
                pick = (rim_row == senders_ref[:, at : at + block]).astype(F32).astype(BF16)
                rim += dot(pick, d)
        last = this

    each = slots // chunks
    for k, sums_ref in enumerate(sums_refs):
        piece = slice(k * each, (k + 1) * each)
        store_rows(sums_ref, sums[piece], ids_ref[piece, :])
    rim_ref[...] = rim.astype(BF16)


def after(me, ids, slots, senders, weight, gain, parts, pieces, owned, caps, chunks, block=512):
    edges, width = slots.shape[1], weight.shape[0]
    each = ids.shape[0] // chunks
    return pl.pallas_call(
        functools.partial(after_kernel, len(parts), chunks, owned, caps, block),
        in_specs=[SMEM] + [VMEM] * (5 + 3 * len(parts) + len(pieces)),
        out_specs=[VMEM] * (2 + chunks),
        out_shape=[in_vmem((edges, width), BF16), in_vmem((RIM, width), BF16)]
        + [in_vmem((height_of(each), width), BF16)] * chunks,
        cost_estimate=cost(6 * edges * width * width, 8 * edges * width),
        compiler_params=params(20),
        name="after",
    )(me, ids, slots, senders, weight, gain, *[a for part in parts for a in part], *pieces)


def segments_kernel(block, starts_ref, senders_ref, d_ref, total_ref):
    edges, width = d_ref.shape
    total_ref[:8, :] = jnp.zeros((8, width), F32)
    row = lax.broadcasted_iota(jnp.int32, (block + 16, block), 0)
    for at in range(0, edges, block):
        base = pl.multiple_of(starts_ref[at] // 8 * 8, 8)
        onehot = (row == senders_ref[:, at : at + block] - base).astype(F32).astype(BF16)
        sums = dot(onehot, d_ref[at : at + block, :])
        total_ref[pl.ds(base, 8), :] += sums[:8]
        total_ref[pl.ds(pl.multiple_of(base + 8, 8), block + 8), :] = sums[8:]


def segments(senders, d_preact, block=256):
    edges, width = d_preact.shape
    return pl.pallas_call(
        functools.partial(segments_kernel, block),
        in_specs=[SMEM] + [VMEM] * 2,
        out_specs=VMEM,
        out_shape=in_vmem((G_DEV + RIM + block + 16, width), F32),
        cost_estimate=cost(4 * edges * width * width, 4 * edges * width),
        compiler_params=params(16),
        name="segments",
    )(senders, senders.reshape(1, edges), d_preact)


def grid_kernel(first, block, total_ref, carried_ref, weight_ref, after_ref, out_hbm, out_ref, sem):
    weight = weight_ref[...]
    copies = []
    for k, at in enumerate(range(0, out_ref.shape[0], block)):
        rows = total_ref[first + at : first + at + block, :]
        if first + at == 0:
            rows = jnp.concatenate([rows[:RIM] + carried_ref[...].astype(F32), rows[RIM:]], axis=0)
        out_ref[at : at + block, :] = dot_t(rows.astype(BF16), weight).astype(BF16)
        copies.append(
            pltpu.make_async_copy(
                out_ref.at[pl.ds(at, block)], out_hbm.at[pl.ds(first + at, block)], sem.at[k]
            )
        )
        copies[-1].start()
    for copy in copies:
        copy.wait()


def grid_rows(first, rows, total, carried, weight, after, block=512):
    width = weight.shape[0]
    whole = after.shape == (G_DEV, width)
    return pl.pallas_call(
        functools.partial(grid_kernel, first, block),
        in_specs=[VMEM] * 3 + [HBM if whole else ANY],
        out_specs=HBM,
        out_shape=like((G_DEV, width), BF16),
        scratch_shapes=[pltpu.VMEM((rows, width), BF16), DMA((rows // block,))],
        input_output_aliases={3: 0} if whole else {},
        cost_estimate=cost(2 * rows * width * width, 6 * rows * width),
        compiler_params=params(16),
        name="grid_rows",
    )(total, carried, weight, after)


def regroup_kernel(groups, parts, rows, *refs):
    outs = refs[parts + 1 :]
    low = groups // len(outs)
    each = rows // groups
    loaded = [load_rows(ref, rows) for ref in refs[:parts]]
    for j, out_ref in enumerate(outs):
        spans = [(k, (j * low + g) * each) for g in range(low) for k in range(parts)]
        sums = jnp.concatenate([loaded[k][0][at : at + each] for k, at in spans], axis=0)
        ids = jnp.concatenate([loaded[k][1][at : at + each] for k, at in spans], axis=0)
        store_rows(out_ref, sums, ids)


def regroup(arrived, radix, low, rows, after):
    width = arrived[0].shape[1]
    parts = len(arrived)
    return pl.pallas_call(
        functools.partial(regroup_kernel, radix * low, parts, rows),
        in_specs=[VMEM] * parts + [ANY],
        out_specs=[VMEM] * radix,
        out_shape=[in_vmem((height_of(rows * parts // radix), width), BF16)] * radix,
        cost_estimate=cost(0, 8 * rows * parts * width),
        compiler_params=params(8),
        name="regroup",
    )(*arrived, after)


def mesh_kernel(parts, size, *refs):
    pieces, weight_ref, out_ref = refs[:parts], refs[parts], refs[-1]
    owned, width = out_ref.shape
    loaded = [load_rows(piece, size) for piece in pieces]
    rows = jnp.concatenate([sums for sums, _ in loaded], axis=0)
    ids = jnp.concatenate([ids for _, ids in loaded], axis=0).T[:owned].astype(jnp.int32)
    pick = (lax.broadcasted_iota(jnp.int32, ids.shape, 0) == ids).astype(F32).astype(BF16)
    high, low = split(rows)
    high, low = split(dot(pick, high) + dot(pick, low))
    both = dot_t(jnp.concatenate([high, low], axis=0), weight_ref[...])
    out_ref[...] = (both[:owned] + both[owned:]).astype(BF16)


def mesh_rows(pieces, size, weight, owned):
    width = weight.shape[0]
    return pl.pallas_call(
        functools.partial(mesh_kernel, len(pieces), size),
        in_specs=[VMEM] * (len(pieces) + 1),
        out_specs=VMEM,
        out_shape=like((owned, width), BF16),
        cost_estimate=cost(2 * owned * width * width, 2 * width * width),
        compiler_params=params(8),
        name="mesh_rows",
    )(*pieces, weight)


def on_device(
    saved_preact,
    edge_senders,
    edge_slots,
    mesh_requests,
    mesh_cotangent,
    out_weight,
    out_bias,
    ln_gain,
    grid_weight,
    mesh_weight,
):
    count = lax.axis_size("band")
    me = lax.axis_index("band")
    owned, width = mesh_cotangent.shape
    edges = saved_preact.shape[0]
    bits = bits_of(count)
    sizes = [edges // 6, edges // 3, edges // 3, edges // 6]

    sources = (
        out_weight,
        out_bias.reshape(1, width),
        grid_weight,
        mesh_weight,
        ln_gain.reshape(1, width),
        mesh_cotangent,
    )
    weight, bias, weight_g, weight_m, gain, own_rows, ids, *later = first_part(
        saved_preact, sizes, sources, me.reshape(1), mesh_requests.swapaxes(1, 2)
    )
    later, parts = later[:-3], [later[-3:]]

    held = [mesh_cotangent, swap(mesh_cotangent, count, 1 << bits[0])]
    for bit in bits[1:]:
        whole = join([own_rows, held[1]] if len(parts) == 1 and bit == bits[1] else held, parts[-1][0])
        held = [whole, swap(whole, count, 1 << bit)]
        if later:
            parts.append(later_part(later.pop(0), weight, bias, whole))

    d_preact, rim, *chunks = after(
        me.reshape(1),
        ids,
        edge_slots.reshape(1, edges),
        edge_senders.reshape(1, edges),
        weight,
        gain,
        parts,
        held,
        owned,
        mesh_requests.shape[2],
        2,
    )

    carried = lax.ppermute(rim, "band", [(i, i + 1) for i in range(count - 1)])
    left, size = count, ids.shape[0] // 2
    for number, bit in enumerate(reversed(bits)):
        if number:
            chunks = regroup(arrived, 2, left // 2, size, last)
        left //= 2
        arrived = [chunks[0], swap(chunks[1], count, 1 << bit)]
        if number == 0:
            last = total = segments(edge_senders, d_preact)
        elif number == 1:
            last = in_hbm(grid_rows(G_DEV // 2, G_DEV // 2, total, rim, weight_g, chunks[0]))
        elif number == 2:
            last = in_hbm(grid_rows(0, G_DEV // 2, total, carried, weight_g, last))
    grid_adjoint = last
    mesh_adjoint = mesh_rows(arrived, size, weight_m, owned)
    return (grid_adjoint, mesh_adjoint)


def solution(mesh):
    in_specs = (
        P(("groups", "band"), None),
        P("band"),
        P("band"),
        P("band", None, None),
        P(("groups", "band"), None),
        P(),
        P(),
        P(),
        P(),
        P(),
    )
    out_specs = (P(("groups", "band"), None), P(("groups", "band"), None))
    return jax.shard_map(
        on_device, mesh=mesh, in_specs=in_specs, out_specs=out_specs, check_vma=False
    )
```

```python
import functools

import jax
import jax.numpy as jnp
from jax import lax
from jax.experimental import pallas as pl
from jax.experimental.pallas import tpu as pltpu
from jax.sharding import PartitionSpec as P

G_DEV = 2048
RIM = 128
LANES = 128
EPS = 1e-05
MIB = 1 << 20

BF16 = jnp.bfloat16
F32 = jnp.float32
VMEM = pl.BlockSpec(memory_space=pltpu.VMEM)
SMEM = pl.BlockSpec(memory_space=pltpu.SMEM)
HBM = pl.BlockSpec(memory_space=pltpu.HBM)
ANY = pl.BlockSpec(memory_space=pl.ANY)
DMA = pltpu.SemaphoreType.DMA


def stages_of(count):
    top = count.bit_length() - 1
    assert count == 1 << top
    stages = []
    while top > 0:
        low = max(0, top - 2)
        stages.append((low, 1 << (top - low)))
        top = low
    return stages


def distance_of(row, caps, count):
    group, distance, left = row // caps, 0, count
    for shift, radix in reversed(stages_of(count)):
        left //= radix
        distance = distance + ((group // left) % radix << shift)
    return distance


def swap(block, count, mask):
    return lax.ppermute(block, "band", [(i, i ^ mask) for i in range(count)])


def like(shape, dtype):
    return jax.ShapeDtypeStruct(shape, dtype)


def in_hbm(x):
    return pltpu.with_memory_space_constraint(x, pltpu.HBM)


def in_vmem(shape, dtype):
    return pltpu.VMEM(shape, dtype)


def dot(a, b):
    return jnp.dot(a, b, preferred_element_type=F32)


def dot_t(a, b):
    return lax.dot_general(a, b, (((1,), (1,)), ((), ())), preferred_element_type=F32)


def split(x):
    high = x.astype(BF16)
    return high, (x - high.astype(F32)).astype(BF16)


def cost(flops, size):
    return pl.CostEstimate(flops=int(flops), bytes_accessed=int(size), transcendentals=0)


def params(limit):
    return pltpu.CompilerParams(vmem_limit_bytes=limit * MIB)


def edge_blocks(pre_ref, weight_ref, bias_ref, normed_ref, q_ref, gate_ref, block, arrive, weigh):
    rows, last = pre_ref.shape[0], None
    for at in range(0, rows + block, block):
        this = None
        if at < rows:
            arrive(at)
            p = pre_ref[at : at + block].astype(F32)
            s = 0.5 * jnp.tanh(0.5 * p) + 0.5
            h = p * s
            hidden, gate = h.astype(BF16), s + h * (1.0 - s)
            if at == 0:
                weigh()
                weight, bias = weight_ref[...], bias_ref[...]
            this = dot(hidden, weight) + bias, gate
        if last is not None:
            out, gate = last
            centre = out - jnp.mean(out, axis=-1, keepdims=True)
            inv = lax.rsqrt(jnp.mean(centre * centre, axis=-1, keepdims=True) + EPS)
            normed = (centre * inv).astype(BF16)
            piece = slice(at - block, at)
            normed_ref[piece] = normed
            q_ref[piece] = dot_t(normed, weight).astype(BF16)
            gate_ref[piece] = gate * inv
        last = this


def first_kernel(block, copies, pre_hbm, *refs):
    sources, (me_ref, requests_hbm), refs = refs[:copies], refs[copies : copies + 2], refs[copies + 2 :]
    targets, refs = refs[:copies], refs[copies:]
    ids_ref, other_ref, normed_ref, q_ref, gate_ref, pre_ref, requests_ref, sem = refs
    rows = normed_ref.shape[0]

    def load(k, source, target):
        return pltpu.make_async_copy(source, target, sem.at[k])

    others = [load(k, a, b) for k, (a, b) in enumerate(zip(sources, targets))]
    starts = list(range(0, rows, block))
    more_rows = other_ref.shape[0]
    loads = [
        load(copies + k, pre_hbm.at[pl.ds(at, block)], pre_ref.at[pl.ds(at, block)])
        for k, at in enumerate(starts)
    ]
    more = load(copies + len(loads), pre_hbm.at[pl.ds(rows, more_rows)], other_ref)
    asked = load(copies + len(loads) + 1, requests_hbm, requests_ref)
    for copy in loads[:1] + others[:2] + loads[1:] + others[2:] + [more, asked]:
        copy.start()

    def weigh():
        for copy in others[:2]:
            copy.wait()

    edge_blocks(
        pre_ref,
        targets[0],
        targets[1],
        normed_ref,
        q_ref,
        gate_ref,
        block,
        lambda at: loads[at // block].wait(),
        weigh,
    )
    for copy in others[2:] + [more, asked]:
        copy.wait()
    slots, caps = ids_ref.shape[0], requests_ref.shape[1]
    count = slots // caps
    row = lax.broadcasted_iota(jnp.int32, ids_ref.shape, 0)
    ids = jnp.zeros(ids_ref.shape, jnp.int32)
    for r in range(slots):
        owner = me_ref[0] ^ distance_of(r, caps, count)
        ids = jnp.where(row == r, requests_ref[0, r % caps, owner], ids)
    ids_ref[...] = ids.astype(F32)


def first_part(preact, rows, sources, me, requests, block=512):
    edges, width = preact.shape
    copies = len(sources)
    outs = [in_vmem(a.shape, a.dtype) for a in sources]
    outs += [in_vmem((requests.shape[1] * requests.shape[2], LANES), F32)]
    outs += [in_vmem((edges - rows, width), BF16)]
    outs += [in_vmem((rows, width), BF16)] * 2 + [in_vmem((rows, width), F32)]
    return pl.pallas_call(
        functools.partial(first_kernel, block, copies),
        in_specs=[HBM] * (1 + copies) + [SMEM, HBM],
        out_specs=[VMEM] * len(outs),
        out_shape=outs,
        scratch_shapes=[
            pltpu.VMEM((rows, width), BF16),
            pltpu.SMEM(requests.shape, jnp.int32),
            DMA((copies + rows // block + 2,)),
        ],
        cost_estimate=cost(6 * rows * width * width, 10 * rows * width),
        compiler_params=params(16),
        name="first_part",
    )(in_hbm(preact), *[in_hbm(a) for a in sources], me, in_hbm(requests))


def second_kernel(block, pre_ref, weight_ref, bias_ref, after_ref, normed_ref, q_ref, gate_ref):
    edge_blocks(
        pre_ref, weight_ref, bias_ref, normed_ref, q_ref, gate_ref, block, lambda at: None, lambda: None
    )


def second_part(pre, weight, bias, after, block=512):
    rows, width = pre.shape
    outs = [in_vmem((rows, width), BF16)] * 2 + [in_vmem((rows, width), F32)]
    return pl.pallas_call(
        functools.partial(second_kernel, block),
        in_specs=[VMEM, VMEM, VMEM, ANY],
        out_specs=[VMEM] * len(outs),
        out_shape=outs,
        cost_estimate=cost(6 * rows * width * width, 10 * rows * width),
        compiler_params=params(16),
        name="second_part",
    )(pre, weight, bias, after)


def join_kernel(parts, *refs):
    out_ref, rows = refs[-1], refs[0].shape[0]
    for k in range(parts):
        out_ref[k * rows : (k + 1) * rows, :] = refs[k][...]


def join(pieces, after):
    rows, width = pieces[0].shape
    return pl.pallas_call(
        functools.partial(join_kernel, len(pieces)),
        in_specs=[VMEM] * len(pieces) + [ANY],
        out_specs=VMEM,
        out_shape=in_vmem((len(pieces) * rows, width), pieces[0].dtype),
        cost_estimate=cost(0, 4 * len(pieces) * rows * width),
        compiler_params=params(8),
        name="join",
    )(*pieces, after)


def after_kernel(
    parts, chunks, owned, caps, block, me_ref, ids_ref, slots_ref, senders_ref, weight_ref, gain_ref, *refs
):
    edge_refs = [refs[3 * k : 3 * k + 3] for k in range(parts)]
    refs = refs[3 * parts :]
    pieces, (d_ref, rim_ref), sums_refs = refs[: -2 - chunks], refs[-2 - chunks : -chunks], refs[-chunks:]
    slots = ids_ref.shape[0]
    count = slots // caps
    edges, width = d_ref.shape
    me = me_ref[0]
    weight = weight_ref[...]

    row = lax.broadcasted_iota(jnp.int32, (slots, 1), 0)
    distance, place, step = distance_of(row, caps, count), jnp.zeros_like(row), 1
    for shift, radix in stages_of(count):
        place = place + ((distance >> shift) & (radix - 1)) * step
        step *= radix
    place = place * owned + ids_ref[...][:, :1].astype(jnp.int32)
    piece_rows = pieces[0].shape[0]
    column = lax.broadcasted_iota(jnp.int32, (slots, piece_rows), 1)
    rows = jnp.zeros((slots, width), F32)
    for k, piece in enumerate(pieces):
        pick = (place == column + k * piece_rows).astype(F32).astype(BF16)
        rows += dot(pick, piece[...])
    rows = rows * gain_ref[...]
    rows = rows - jnp.mean(rows, axis=-1, keepdims=True)
    mean_rows = (rows * (1.0 / width)).astype(BF16)
    both = dot_t(jnp.concatenate(split(rows), axis=0), weight)
    s_both = jnp.concatenate(split(both[:slots] + both[slots:]), axis=0)

    key = (distance ^ me) * caps + row % caps
    key = jnp.concatenate([key, key], axis=0)
    mean_rows = jnp.concatenate([mean_rows, jnp.zeros_like(mean_rows)], axis=0)
    rim_row = lax.broadcasted_iota(jnp.int32, (RIM, block), 0) + G_DEV
    sums = jnp.zeros((slots, width), F32)
    rim = jnp.zeros((RIM, width), F32)
    edge_at = [(part, at) for part in edge_refs for at in range(0, part[0].shape[0], block)]
    last = None
    for number in range(len(edge_at) + 1):
        this = None
        if number < len(edge_at):
            (normed_ref, q_ref, gate_ref), at = edge_at[number]
            piece = slice(at, at + block)
            onehot_t = (key == slots_ref[:, number * block : (number + 1) * block]).astype(F32)
            onehot = onehot_t.T
            c = jnp.sum(onehot * dot_t(normed_ref[piece], mean_rows), axis=-1, keepdims=True)
            s_rows = dot(onehot.astype(BF16), s_both)
            this = (onehot_t[:slots].astype(BF16), c, s_rows, q_ref, gate_ref, piece)
        if last is not None:
            onehot_t, c, s_rows, q_ref, gate_ref, piece = last
            at = (number - 1) * block
            d = (gate_ref[piece] * (s_rows - c * q_ref[piece].astype(F32))).astype(BF16)
            d_ref[at : at + block, :] = d
            sums += dot(onehot_t, d)
            if at + block > G_DEV:
                pick = (rim_row == senders_ref[:, at : at + block]).astype(F32).astype(BF16)
                rim += dot(pick, d)
        last = this

    each = slots // chunks
    for k, sums_ref in enumerate(sums_refs):
        sums_ref[:, :width] = sums[k * each : (k + 1) * each]
        sums_ref[:, width:] = ids_ref[k * each : (k + 1) * each, :]
    rim_ref[...] = rim.astype(BF16)


def after(me, ids, slots, senders, weight, gain, parts, pieces, owned, caps, chunks, block=512):
    edges, width = slots.shape[1], weight.shape[0]
    each = ids.shape[0] // chunks
    return pl.pallas_call(
        functools.partial(after_kernel, len(parts), chunks, owned, caps, block),
        in_specs=[SMEM] + [VMEM] * (5 + 3 * len(parts) + len(pieces)),
        out_specs=[VMEM] * (2 + chunks),
        out_shape=[in_vmem((edges, width), BF16), in_vmem((RIM, width), BF16)]
        + [in_vmem((each, width + LANES), F32)] * chunks,
        cost_estimate=cost(6 * edges * width * width, 8 * edges * width),
        compiler_params=params(20),
        name="after",
    )(me, ids, slots, senders, weight, gain, *[a for part in parts for a in part], *pieces)


def segments_kernel(block, starts_ref, senders_ref, d_ref, total_ref):
    edges, width = d_ref.shape
    total_ref[:8, :] = jnp.zeros((8, width), F32)
    row = lax.broadcasted_iota(jnp.int32, (block + 16, block), 0)
    for at in range(0, edges, block):
        base = pl.multiple_of(starts_ref[at] // 8 * 8, 8)
        onehot = (row == senders_ref[:, at : at + block] - base).astype(F32).astype(BF16)
        sums = dot(onehot, d_ref[at : at + block, :])
        total_ref[pl.ds(base, 8), :] += sums[:8]
        total_ref[pl.ds(pl.multiple_of(base + 8, 8), block + 8), :] = sums[8:]


def segments(senders, d_preact, block=256):
    edges, width = d_preact.shape
    return pl.pallas_call(
        functools.partial(segments_kernel, block),
        in_specs=[SMEM] + [VMEM] * 2,
        out_specs=VMEM,
        out_shape=in_vmem((G_DEV + RIM + block + 16, width), F32),
        cost_estimate=cost(4 * edges * width * width, 4 * edges * width),
        compiler_params=params(16),
        name="segments",
    )(senders, senders.reshape(1, edges), d_preact)


def grid_kernel(block, total_ref, carried_ref, weight_ref, out_hbm, out_ref, sem):
    weight = weight_ref[...]
    copies = []
    for k, at in enumerate(range(0, G_DEV, block)):
        rows = total_ref[at : at + block, :]
        if at == 0:
            rows = jnp.concatenate([rows[:RIM] + carried_ref[...].astype(F32), rows[RIM:]], axis=0)
        out_ref[at : at + block, :] = dot_t(rows.astype(BF16), weight).astype(BF16)
        copies.append(
            pltpu.make_async_copy(out_ref.at[pl.ds(at, block)], out_hbm.at[pl.ds(at, block)], sem.at[k])
        )
        copies[-1].start()
    for copy in copies:
        copy.wait()


def grid_rows(total, carried, weight, block=512):
    width = weight.shape[0]
    return pl.pallas_call(
        functools.partial(grid_kernel, block),
        in_specs=[VMEM] * 3,
        out_specs=HBM,
        out_shape=like((G_DEV, width), BF16),
        scratch_shapes=[pltpu.VMEM((G_DEV, width), BF16), DMA((G_DEV // block,))],
        cost_estimate=cost(2 * G_DEV * width * width, 6 * G_DEV * width),
        compiler_params=params(16),
        name="grid_rows",
    )(total, carried, weight)


def regroup_kernel(groups, parts, *refs):
    outs = refs[parts + 1 :]
    low = groups // len(outs)
    each = refs[0].shape[0] // groups
    for j, out_ref in enumerate(outs):
        for g in range(low):
            for k in range(parts):
                to, at = (g * parts + k) * each, (j * low + g) * each
                out_ref[to : to + each, :] = refs[k][at : at + each, :]


def regroup(arrived, radix, low, after):
    rows, width = arrived[0].shape
    parts = len(arrived)
    return pl.pallas_call(
        functools.partial(regroup_kernel, radix * low, parts),
        in_specs=[VMEM] * parts + [ANY],
        out_specs=[VMEM] * radix,
        out_shape=[in_vmem((rows * parts // radix, width), F32)] * radix,
        cost_estimate=cost(0, 8 * rows * parts * width),
        compiler_params=params(8),
        name="regroup",
    )(*arrived, after)


def mesh_kernel(parts, *refs):
    pieces, weight_ref, out_ref = refs[:parts], refs[parts], refs[-1]
    owned, width = out_ref.shape
    rows = jnp.concatenate([piece[:, :width] for piece in pieces], axis=0)
    ids = jnp.concatenate([piece[:, width:] for piece in pieces], axis=0)
    ids = jnp.concatenate([ids, ids], axis=0).T[:owned].astype(jnp.int32)
    pick = (lax.broadcasted_iota(jnp.int32, ids.shape, 0) == ids).astype(F32)
    total = dot(pick.astype(BF16), jnp.concatenate(split(rows), axis=0))
    both = dot_t(jnp.concatenate(split(total), axis=0), weight_ref[...])
    out_ref[...] = (both[:owned] + both[owned:]).astype(BF16)


def mesh_rows(pieces, weight, owned, after):
    width = weight.shape[0]
    return pl.pallas_call(
        functools.partial(mesh_kernel, len(pieces)),
        in_specs=[VMEM] * (len(pieces) + 1) + [ANY],
        out_specs=VMEM,
        out_shape=like((owned, width), BF16),
        cost_estimate=cost(2 * owned * width * width, 2 * width * width),
        compiler_params=params(8),
        name="mesh_rows",
    )(*pieces, weight, in_hbm(after))


def on_device(
    saved_preact,
    edge_senders,
    edge_slots,
    mesh_requests,
    mesh_cotangent,
    out_weight,
    out_bias,
    ln_gain,
    grid_weight,
    mesh_weight,
):
    count = lax.axis_size("band")
    me = lax.axis_index("band")
    owned, width = mesh_cotangent.shape
    edges = saved_preact.shape[0]
    stages = stages_of(count)

    sources = (
        out_weight,
        out_bias.reshape(1, width),
        grid_weight,
        mesh_weight,
        ln_gain.reshape(1, width),
        mesh_cotangent,
    )
    weight, bias, weight_g, weight_m, gain, own_rows, ids, more, *first = first_part(
        saved_preact, edges // 3, sources, me.reshape(1), mesh_requests.swapaxes(1, 2)
    )

    held = [mesh_cotangent]
    for number, (shift, radix) in enumerate(stages):
        if number == 1:
            held = [join([own_rows, *held[1:]], first[0])]
        elif number > 1:
            held = [join(held, ids)]
        held += [swap(held[0], count, j << shift) for j in range(1, radix)]
        if number == 1:
            second = second_part(more, weight, bias, held[0])

    back = stages[::-1]
    d_preact, rim, *chunks = after(
        me.reshape(1),
        ids,
        edge_slots.reshape(1, edges),
        edge_senders.reshape(1, edges),
        weight,
        gain,
        [first, second],
        held,
        owned,
        mesh_requests.shape[2],
        back[0][1],
    )

    total = segments(edge_senders, d_preact)
    carried = lax.ppermute(rim, "band", [(i, (i + 1) % count) for i in range(count)])
    arrived, left = None, count
    for shift, radix in back:
        if arrived is not None:
            chunks = regroup(arrived, radix, left // radix, total)
        left //= radix
        arrived = [chunks[0]] + [swap(chunks[j], count, j << shift) for j in range(1, radix)]
    grid_adjoint = grid_rows(total, carried, weight_g)
    mesh_adjoint = mesh_rows(arrived, weight_m, owned, grid_adjoint)
    return (grid_adjoint, mesh_adjoint)


def solution(mesh):
    in_specs = (
        P(("groups", "band"), None),
        P("band"),
        P("band"),
        P("band", None, None),
        P(("groups", "band"), None),
        P(),
        P(),
        P(),
        P(),
        P(),
    )
    out_specs = (P(("groups", "band"), None), P(("groups", "band"), None))
    return jax.shard_map(
        on_device, mesh=mesh, in_specs=in_specs, out_specs=out_specs, check_vma=False
    )
```

```python
import functools

import jax
import jax.numpy as jnp
from jax import lax
from jax.experimental import pallas as pl
from jax.experimental.pallas import tpu as pltpu
from jax.sharding import PartitionSpec as P

G_DEV = 2048
RIM = 128
LANES = 128
EPS = 1e-05
CHUNK = 32
MIB = 1 << 20

BF16 = jnp.bfloat16
F32 = jnp.float32
VMEM = pl.BlockSpec(memory_space=pltpu.VMEM)
SMEM = pl.BlockSpec(memory_space=pltpu.SMEM)
HBM = pl.BlockSpec(memory_space=pltpu.HBM)
ANY = pl.BlockSpec(memory_space=pl.ANY)
DMA = pltpu.SemaphoreType.DMA


def stages_of(count):
    top = count.bit_length() - 1
    assert count == 1 << top
    stages = []
    while top > 0:
        low = max(0, top - 2)
        stages.append((low, 1 << (top - low)))
        top = low
    return stages


def distance_of(row, caps, count):
    group, distance, left = row // caps, 0, count
    for shift, radix in reversed(stages_of(count)):
        left //= radix
        distance = distance + ((group // left) % radix << shift)
    return distance


def swap(block, count, mask):
    return lax.ppermute(block, "band", [(i, i ^ mask) for i in range(count)])


def like(shape, dtype):
    return jax.ShapeDtypeStruct(shape, dtype)


def in_hbm(x):
    return pltpu.with_memory_space_constraint(x, pltpu.HBM)


def in_vmem(shape, dtype):
    return pltpu.VMEM(shape, dtype)


def dot(a, b):
    return jnp.dot(a, b, preferred_element_type=F32)


def dot_t(a, b):
    return lax.dot_general(a, b, (((1,), (1,)), ((), ())), preferred_element_type=F32)


def split(x):
    high = x.astype(BF16)
    return high, (x - high.astype(F32)).astype(BF16)


def cost(flops, size):
    return pl.CostEstimate(flops=int(flops), bytes_accessed=int(size), transcendentals=0)


def params(limit):
    return pltpu.CompilerParams(vmem_limit_bytes=limit * MIB)


def edge_blocks(pre_ref, weight_ref, bias_ref, normed_ref, q_ref, gate_ref, hidden_ref, block, arrive):
    weight, bias = weight_ref[...], bias_ref[...]
    rows, last = pre_ref.shape[0], None
    for at in range(0, rows + block, block):
        this = None
        if at < rows:
            arrive(at)
            for row in range(at, at + block, CHUNK):
                piece = slice(row, row + CHUNK)
                half = 0.5 * pre_ref[piece].astype(F32)
                t = jnp.tanh(half)
                double = 1.0 + t
                h = half * double
                hidden_ref[piece] = h.astype(BF16)
                gate_ref[piece] = double + h * (1.0 - t)
            this = dot(hidden_ref[at : at + block], weight)
        if last is not None:
            for row in range(0, block, CHUNK):
                piece = slice(at - block + row, at - block + row + CHUNK)
                out = last[row : row + CHUNK] + bias
                centre = out - jnp.mean(out, axis=-1, keepdims=True)
                inv = lax.rsqrt(jnp.mean(centre * centre, axis=-1, keepdims=True) + EPS)
                normed_ref[piece] = (centre * inv).astype(BF16)
                gate_ref[piece] = gate_ref[piece] * (0.5 * inv)
            q_ref[at - block : at] = dot_t(normed_ref[at - block : at], weight).astype(BF16)
        last = this


def first_kernel(block, copies, pre_hbm, *refs):
    sources, (me_ref, requests_hbm), refs = refs[:copies], refs[copies : copies + 2], refs[copies + 2 :]
    targets, refs = refs[:copies], refs[copies:]
    ids_ref, other_ref, normed_ref, q_ref, gate_ref, pre_ref, hidden_ref, requests_ref, sem = refs
    rows = normed_ref.shape[0]

    def load(k, source, target):
        return pltpu.make_async_copy(source, target, sem.at[k])

    others = [load(k, a, b) for k, (a, b) in enumerate(zip(sources, targets))]
    starts = list(range(0, rows, block))
    more_rows = other_ref.shape[0]
    loads = [
        load(copies + k, pre_hbm.at[pl.ds(at, block)], pre_ref.at[pl.ds(at, block)])
        for k, at in enumerate(starts)
    ]
    more = load(copies + len(loads), pre_hbm.at[pl.ds(rows, more_rows)], other_ref)
    asked = load(copies + len(loads) + 1, requests_hbm, requests_ref)
    for copy in others[:2] + loads + others[2:] + [more, asked]:
        copy.start()
    for copy in others[:2]:
        copy.wait()
    edge_blocks(
        pre_ref,
        targets[0],
        targets[1],
        normed_ref,
        q_ref,
        gate_ref,
        hidden_ref,
        block,
        lambda at: loads[at // block].wait(),
    )
    for copy in others[2:] + [more, asked]:
        copy.wait()
    slots, caps = ids_ref.shape[0], requests_ref.shape[1]
    count = slots // caps
    row = lax.broadcasted_iota(jnp.int32, ids_ref.shape, 0)
    ids = jnp.zeros(ids_ref.shape, jnp.int32)
    for r in range(slots):
        owner = me_ref[0] ^ distance_of(r, caps, count)
        ids = jnp.where(row == r, requests_ref[0, r % caps, owner], ids)
    ids_ref[...] = ids.astype(F32)


def first_part(preact, rows, sources, me, requests, block=512):
    edges, width = preact.shape
    copies = len(sources)
    outs = [in_vmem(a.shape, a.dtype) for a in sources]
    outs += [in_vmem((requests.shape[1] * requests.shape[2], LANES), F32)]
    outs += [in_vmem((edges - rows, width), BF16)]
    outs += [in_vmem((rows, width), BF16)] * 2 + [in_vmem((rows, width), F32)]
    return pl.pallas_call(
        functools.partial(first_kernel, block, copies),
        in_specs=[HBM] * (1 + copies) + [SMEM, HBM],
        out_specs=[VMEM] * len(outs),
        out_shape=outs,
        scratch_shapes=[
            pltpu.VMEM((rows, width), BF16),
            pltpu.VMEM((rows, width), BF16),
            pltpu.SMEM(requests.shape, jnp.int32),
            DMA((copies + rows // block + 2,)),
        ],
        cost_estimate=cost(6 * rows * width * width, 10 * rows * width),
        compiler_params=params(16),
        name="first_part",
    )(in_hbm(preact), *[in_hbm(a) for a in sources], me, in_hbm(requests))


def second_kernel(block, pre_ref, weight_ref, bias_ref, after_ref, normed_ref, q_ref, gate_ref, hidden_ref):
    edge_blocks(
        pre_ref, weight_ref, bias_ref, normed_ref, q_ref, gate_ref, hidden_ref, block, lambda at: None
    )


def second_part(pre, weight, bias, after, block=512):
    rows, width = pre.shape
    outs = [in_vmem((rows, width), BF16)] * 2 + [in_vmem((rows, width), F32)]
    return pl.pallas_call(
        functools.partial(second_kernel, block),
        in_specs=[VMEM, VMEM, VMEM, ANY],
        out_specs=[VMEM] * len(outs),
        out_shape=outs,
        scratch_shapes=[pltpu.VMEM((rows, width), BF16)],
        cost_estimate=cost(6 * rows * width * width, 10 * rows * width),
        compiler_params=params(16),
        name="second_part",
    )(pre, weight, bias, after)


def join_kernel(parts, *refs):
    out_ref, rows = refs[-1], refs[0].shape[0]
    for k in range(parts):
        out_ref[k * rows : (k + 1) * rows, :] = refs[k][...]


def join(pieces, after):
    rows, width = pieces[0].shape
    return pl.pallas_call(
        functools.partial(join_kernel, len(pieces)),
        in_specs=[VMEM] * len(pieces) + [ANY],
        out_specs=VMEM,
        out_shape=in_vmem((len(pieces) * rows, width), pieces[0].dtype),
        cost_estimate=cost(0, 4 * len(pieces) * rows * width),
        compiler_params=params(8),
        name="join",
    )(*pieces, after)


def after_kernel(
    parts, chunks, owned, caps, block, me_ref, ids_ref, slots_ref, senders_ref, weight_ref, gain_ref, *refs
):
    edge_refs = [refs[3 * k : 3 * k + 3] for k in range(parts)]
    refs = refs[3 * parts :]
    pieces, (d_ref, rim_ref), sums_refs = refs[: -2 - chunks], refs[-2 - chunks : -chunks], refs[-chunks:]
    slots = ids_ref.shape[0]
    count = slots // caps
    edges, width = d_ref.shape
    me = me_ref[0]
    weight = weight_ref[...]

    row = lax.broadcasted_iota(jnp.int32, (slots, 1), 0)
    distance, place, step = distance_of(row, caps, count), jnp.zeros_like(row), 1
    for shift, radix in stages_of(count):
        place = place + ((distance >> shift) & (radix - 1)) * step
        step *= radix
    place = place * owned + ids_ref[...][:, :1].astype(jnp.int32)
    piece_rows = pieces[0].shape[0]
    column = lax.broadcasted_iota(jnp.int32, (slots, piece_rows), 1)
    rows = jnp.zeros((slots, width), F32)
    for k, piece in enumerate(pieces):
        pick = (place == column + k * piece_rows).astype(F32).astype(BF16)
        rows += dot(pick, piece[...])
    rows = rows * gain_ref[...]
    rows = rows - jnp.mean(rows, axis=-1, keepdims=True)
    mean_rows = (rows * (1.0 / width)).astype(BF16)
    both = dot_t(jnp.concatenate(split(rows), axis=0), weight)
    s_both = jnp.concatenate(split(both[:slots] + both[slots:]), axis=0)

    key = (distance ^ me) * caps + row % caps
    key = jnp.concatenate([key, key], axis=0)
    mean_rows = jnp.concatenate([mean_rows, jnp.zeros_like(mean_rows)], axis=0)
    rim_row = lax.broadcasted_iota(jnp.int32, (RIM, block), 0) + G_DEV
    sums = jnp.zeros((slots, width), F32)
    rim = jnp.zeros((RIM, width), F32)
    edge_at = [(part, at) for part in edge_refs for at in range(0, part[0].shape[0], block)]
    last = None
    for number in range(len(edge_at) + 1):
        this = None
        if number < len(edge_at):
            (normed_ref, q_ref, gate_ref), at = edge_at[number]
            piece = slice(at, at + block)
            onehot_t = (key == slots_ref[:, number * block : (number + 1) * block]).astype(F32)
            onehot = onehot_t.T
            g = dot_t(normed_ref[piece], mean_rows)
            s_rows = dot(onehot.astype(BF16), s_both)
            this = (onehot_t[:slots].astype(BF16), onehot, g, s_rows, q_ref, gate_ref, at)
        if last is not None:
            onehot_t, onehot, g, s_rows, q_ref, gate_ref, first = last
            at = (number - 1) * block
            for row in range(0, block, CHUNK):
                piece, inner = slice(first + row, first + row + CHUNK), slice(row, row + CHUNK)
                c = jnp.sum(onehot[inner] * g[inner], axis=-1, keepdims=True)
                d = gate_ref[piece] * (s_rows[inner] - c * q_ref[piece].astype(F32))
                d_ref[at + row : at + row + CHUNK, :] = d.astype(BF16)
            d = d_ref[at : at + block, :]
            sums += dot(onehot_t, d)
            if at + block > G_DEV:
                pick = (rim_row == senders_ref[:, at : at + block]).astype(F32).astype(BF16)
                rim += dot(pick, d)
        last = this

    each = slots // chunks
    for k, sums_ref in enumerate(sums_refs):
        sums_ref[:, :width] = sums[k * each : (k + 1) * each]
        sums_ref[:, width:] = ids_ref[k * each : (k + 1) * each, :]
    rim_ref[...] = rim.astype(BF16)


def after(me, ids, slots, senders, weight, gain, parts, pieces, owned, caps, chunks, block=512):
    edges, width = slots.shape[1], weight.shape[0]
    each = ids.shape[0] // chunks
    return pl.pallas_call(
        functools.partial(after_kernel, len(parts), chunks, owned, caps, block),
        in_specs=[SMEM] + [VMEM] * (5 + 3 * len(parts) + len(pieces)),
        out_specs=[VMEM] * (2 + chunks),
        out_shape=[in_vmem((edges, width), BF16), in_vmem((RIM, width), BF16)]
        + [in_vmem((each, width + LANES), F32)] * chunks,
        cost_estimate=cost(6 * edges * width * width, 8 * edges * width),
        compiler_params=params(20),
        name="after",
    )(me, ids, slots, senders, weight, gain, *[a for part in parts for a in part], *pieces)


def segments_kernel(block, starts_ref, senders_ref, d_ref, total_ref):
    edges, width = d_ref.shape
    total_ref[:8, :] = jnp.zeros((8, width), F32)
    row = lax.broadcasted_iota(jnp.int32, (block + 16, block), 0)
    for at in range(0, edges, block):
        base = pl.multiple_of(starts_ref[at] // 8 * 8, 8)
        onehot = (row == senders_ref[:, at : at + block] - base).astype(F32).astype(BF16)
        sums = dot(onehot, d_ref[at : at + block, :])
        total_ref[pl.ds(base, 8), :] += sums[:8]
        total_ref[pl.ds(pl.multiple_of(base + 8, 8), block + 8), :] = sums[8:]


def segments(senders, d_preact, block=256):
    edges, width = d_preact.shape
    return pl.pallas_call(
        functools.partial(segments_kernel, block),
        in_specs=[SMEM] + [VMEM] * 2,
        out_specs=VMEM,
        out_shape=in_vmem((G_DEV + RIM + block + 16, width), F32),
        cost_estimate=cost(4 * edges * width * width, 4 * edges * width),
        compiler_params=params(16),
        name="segments",
    )(senders, senders.reshape(1, edges), d_preact)


def grid_kernel(block, total_ref, carried_ref, weight_ref, out_hbm, out_ref, sem):
    weight = weight_ref[...]
    copies = []
    for k, at in enumerate(range(0, G_DEV, block)):
        rows = total_ref[at : at + block, :]
        if at == 0:
            rows = jnp.concatenate([rows[:RIM] + carried_ref[...].astype(F32), rows[RIM:]], axis=0)
        out_ref[at : at + block, :] = dot_t(rows.astype(BF16), weight).astype(BF16)
        copies.append(
            pltpu.make_async_copy(out_ref.at[pl.ds(at, block)], out_hbm.at[pl.ds(at, block)], sem.at[k])
        )
        copies[-1].start()
    for copy in copies:
        copy.wait()


def grid_rows(total, carried, weight, block=512):
    width = weight.shape[0]
    return pl.pallas_call(
        functools.partial(grid_kernel, block),
        in_specs=[VMEM] * 3,
        out_specs=HBM,
        out_shape=like((G_DEV, width), BF16),
        scratch_shapes=[pltpu.VMEM((G_DEV, width), BF16), DMA((G_DEV // block,))],
        cost_estimate=cost(2 * G_DEV * width * width, 6 * G_DEV * width),
        compiler_params=params(16),
        name="grid_rows",
    )(total, carried, weight)


def regroup_kernel(groups, parts, *refs):
    outs = refs[parts + 1 :]
    low = groups // len(outs)
    each = refs[0].shape[0] // groups
    for j, out_ref in enumerate(outs):
        for g in range(low):
            for k in range(parts):
                to, at = (g * parts + k) * each, (j * low + g) * each
                out_ref[to : to + each, :] = refs[k][at : at + each, :]


def regroup(arrived, radix, low, after):
    rows, width = arrived[0].shape
    parts = len(arrived)
    return pl.pallas_call(
        functools.partial(regroup_kernel, radix * low, parts),
        in_specs=[VMEM] * parts + [ANY],
        out_specs=[VMEM] * radix,
        out_shape=[in_vmem((rows * parts // radix, width), F32)] * radix,
        cost_estimate=cost(0, 8 * rows * parts * width),
        compiler_params=params(8),
        name="regroup",
    )(*arrived, after)


def mesh_kernel(parts, *refs):
    pieces, weight_ref, out_ref = refs[:parts], refs[parts], refs[-1]
    owned, width = out_ref.shape
    rows = jnp.concatenate([piece[:, :width] for piece in pieces], axis=0)
    ids = jnp.concatenate([piece[:, width:] for piece in pieces], axis=0)
    ids = jnp.concatenate([ids, ids], axis=0).T[:owned].astype(jnp.int32)
    pick = (lax.broadcasted_iota(jnp.int32, ids.shape, 0) == ids).astype(F32)
    total = dot(pick.astype(BF16), jnp.concatenate(split(rows), axis=0))
    both = dot_t(jnp.concatenate(split(total), axis=0), weight_ref[...])
    out_ref[...] = (both[:owned] + both[owned:]).astype(BF16)


def mesh_rows(pieces, weight, owned, after):
    width = weight.shape[0]
    return pl.pallas_call(
        functools.partial(mesh_kernel, len(pieces)),
        in_specs=[VMEM] * (len(pieces) + 1) + [ANY],
        out_specs=VMEM,
        out_shape=like((owned, width), BF16),
        cost_estimate=cost(2 * owned * width * width, 2 * width * width),
        compiler_params=params(8),
        name="mesh_rows",
    )(*pieces, weight, in_hbm(after))


def on_device(
    saved_preact,
    edge_senders,
    edge_slots,
    mesh_requests,
    mesh_cotangent,
    out_weight,
    out_bias,
    ln_gain,
    grid_weight,
    mesh_weight,
):
    count = lax.axis_size("band")
    me = lax.axis_index("band")
    owned, width = mesh_cotangent.shape
    edges = saved_preact.shape[0]
    stages = stages_of(count)

    sources = (
        out_weight,
        out_bias.reshape(1, width),
        grid_weight,
        mesh_weight,
        ln_gain.reshape(1, width),
        mesh_cotangent,
    )
    weight, bias, weight_g, weight_m, gain, own_rows, ids, more, *first = first_part(
        saved_preact, edges // 3, sources, me.reshape(1), mesh_requests.swapaxes(1, 2)
    )

    held = [mesh_cotangent]
    for number, (shift, radix) in enumerate(stages):
        if number == 1:
            held = [join([own_rows, *held[1:]], first[0])]
        elif number > 1:
            held = [join(held, ids)]
        held += [swap(held[0], count, j << shift) for j in range(1, radix)]
        if number == 1:
            second = second_part(more, weight, bias, held[0])

    back = stages[::-1]
    d_preact, rim, *chunks = after(
        me.reshape(1),
        ids,
        edge_slots.reshape(1, edges),
        edge_senders.reshape(1, edges),
        weight,
        gain,
        [first, second],
        held,
        owned,
        mesh_requests.shape[2],
        back[0][1],
    )

    total = segments(edge_senders, d_preact)
    carried = lax.ppermute(rim, "band", [(i, (i + 1) % count) for i in range(count)])
    arrived, left = None, count
    for shift, radix in back:
        if arrived is not None:
            chunks = regroup(arrived, radix, left // radix, total)
        left //= radix
        arrived = [chunks[0]] + [swap(chunks[j], count, j << shift) for j in range(1, radix)]
    grid_adjoint = grid_rows(total, carried, weight_g)
    mesh_adjoint = mesh_rows(arrived, weight_m, owned, grid_adjoint)
    return (grid_adjoint, mesh_adjoint)


def solution(mesh):
    in_specs = (
        P(("groups", "band"), None),
        P("band"),
        P("band"),
        P("band", None, None),
        P(("groups", "band"), None),
        P(),
        P(),
        P(),
        P(),
        P(),
    )
    out_specs = (P(("groups", "band"), None), P(("groups", "band"), None))
    return jax.shard_map(
        on_device, mesh=mesh, in_specs=in_specs, out_specs=out_specs, check_vma=False
    )
```

```python
import functools

import jax
import jax.numpy as jnp
from jax import lax
from jax.experimental import pallas as pl
from jax.experimental.pallas import tpu as pltpu
from jax.sharding import PartitionSpec as P

G_DEV = 2048
RIM = 128
LANES = 128
EPS = 1e-05
CHUNK = 32
MIB = 1 << 20

BF16 = jnp.bfloat16
F32 = jnp.float32
VMEM = pl.BlockSpec(memory_space=pltpu.VMEM)
SMEM = pl.BlockSpec(memory_space=pltpu.SMEM)
HBM = pl.BlockSpec(memory_space=pltpu.HBM)
ANY = pl.BlockSpec(memory_space=pl.ANY)
DMA = pltpu.SemaphoreType.DMA


def stages_of(count):
    top = count.bit_length() - 1
    assert count == 1 << top
    stages = []
    while top > 0:
        low = max(0, top - 2)
        stages.append((low, 1 << (top - low)))
        top = low
    return stages


def distance_of(row, caps, count):
    group, distance, left = row // caps, 0, count
    for shift, radix in reversed(stages_of(count)):
        left //= radix
        distance = distance + ((group // left) % radix << shift)
    return distance


def swap(block, count, mask):
    return lax.ppermute(block, "band", [(i, i ^ mask) for i in range(count)])


def like(shape, dtype):
    return jax.ShapeDtypeStruct(shape, dtype)


def in_hbm(x):
    return pltpu.with_memory_space_constraint(x, pltpu.HBM)


def in_vmem(shape, dtype):
    return pltpu.VMEM(shape, dtype)


def dot(a, b):
    return jnp.dot(a, b, preferred_element_type=F32)


def dot_t(a, b):
    return lax.dot_general(a, b, (((1,), (1,)), ((), ())), preferred_element_type=F32)


def split(x):
    high = x.astype(BF16)
    return high, (x - high.astype(F32)).astype(BF16)


def cost(flops, size):
    return pl.CostEstimate(flops=int(flops), bytes_accessed=int(size), transcendentals=0)


def params(limit):
    return pltpu.CompilerParams(vmem_limit_bytes=limit * MIB)


def edge_blocks(pre_ref, weight_ref, bias_ref, normed_ref, q_ref, gate_ref, inv_ref, hidden_ref, block, arrive):
    weight, bias = weight_ref[...], bias_ref[...]
    rows, last = pre_ref.shape[0], None
    for at in range(0, rows + block, block):
        this = None
        if at < rows:
            arrive(at)
            for row in range(at, at + block, CHUNK):
                piece = slice(row, row + CHUNK)
                half = 0.5 * pre_ref[piece].astype(F32)
                t = jnp.tanh(half)
                double = 1.0 + t
                h = half * double
                hidden_ref[piece] = h.astype(BF16)
                gate_ref[piece] = double + h * (1.0 - t)
            this = dot(hidden_ref[at : at + block], weight)
        if last is not None:
            for row in range(0, block, CHUNK):
                piece = slice(at - block + row, at - block + row + CHUNK)
                out = last[row : row + CHUNK] + bias
                centre = out - jnp.mean(out, axis=-1, keepdims=True)
                inv = lax.rsqrt(jnp.mean(centre * centre, axis=-1, keepdims=True) + EPS)
                normed_ref[piece] = (centre * inv).astype(BF16)
                inv_ref[piece] = jnp.broadcast_to(0.5 * inv, (CHUNK, LANES))
            q_ref[at - block : at] = dot_t(normed_ref[at - block : at], weight).astype(BF16)
        last = this


def edge_outs(rows, width):
    return [in_vmem((rows, width), BF16)] * 2 + [in_vmem((rows, width), F32), in_vmem((rows, LANES), F32)]


def first_kernel(block, copies, pre_hbm, *refs):
    sources, (me_ref, requests_hbm), refs = refs[:copies], refs[copies : copies + 2], refs[copies + 2 :]
    targets, refs = refs[:copies], refs[copies:]
    ids_ref, other_ref, normed_ref, q_ref, gate_ref, inv_ref, pre_ref, hidden_ref, requests_ref, sem = refs
    rows = normed_ref.shape[0]

    def load(k, source, target):
        return pltpu.make_async_copy(source, target, sem.at[k])

    others = [load(k, a, b) for k, (a, b) in enumerate(zip(sources, targets))]
    starts = list(range(0, rows, block))
    more_rows = other_ref.shape[0]
    loads = [
        load(copies + k, pre_hbm.at[pl.ds(at, block)], pre_ref.at[pl.ds(at, block)])
        for k, at in enumerate(starts)
    ]
    more = load(copies + len(loads), pre_hbm.at[pl.ds(rows, more_rows)], other_ref)
    asked = load(copies + len(loads) + 1, requests_hbm, requests_ref)
    for copy in others[:2] + loads + others[2:] + [more, asked]:
        copy.start()
    for copy in others[:2]:
        copy.wait()
    edge_blocks(
        pre_ref,
        targets[0],
        targets[1],
        normed_ref,
        q_ref,
        gate_ref,
        inv_ref,
        hidden_ref,
        block,
        lambda at: loads[at // block].wait(),
    )
    for copy in others[2:] + [more, asked]:
        copy.wait()
    slots, caps = ids_ref.shape[0], requests_ref.shape[1]
    count = slots // caps
    row = lax.broadcasted_iota(jnp.int32, ids_ref.shape, 0)
    ids = jnp.zeros(ids_ref.shape, jnp.int32)
    for r in range(slots):
        owner = me_ref[0] ^ distance_of(r, caps, count)
        ids = jnp.where(row == r, requests_ref[0, r % caps, owner], ids)
    ids_ref[...] = ids.astype(F32)


def first_part(preact, rows, sources, me, requests, block=512):
    edges, width = preact.shape
    copies = len(sources)
    outs = [in_vmem(a.shape, a.dtype) for a in sources]
    outs += [in_vmem((requests.shape[1] * requests.shape[2], LANES), F32)]
    outs += [in_vmem((edges - rows, width), BF16)]
    outs += edge_outs(rows, width)
    return pl.pallas_call(
        functools.partial(first_kernel, block, copies),
        in_specs=[HBM] * (1 + copies) + [SMEM, HBM],
        out_specs=[VMEM] * len(outs),
        out_shape=outs,
        scratch_shapes=[
            pltpu.VMEM((rows, width), BF16),
            pltpu.VMEM((rows, width), BF16),
            pltpu.SMEM(requests.shape, jnp.int32),
            DMA((copies + rows // block + 2,)),
        ],
        cost_estimate=cost(6 * rows * width * width, 10 * rows * width),
        compiler_params=params(16),
        name="first_part",
    )(in_hbm(preact), *[in_hbm(a) for a in sources], me, in_hbm(requests))


def second_kernel(
    block, pre_ref, weight_ref, bias_ref, after_ref, normed_ref, q_ref, gate_ref, inv_ref, hidden_ref
):
    edge_blocks(
        pre_ref, weight_ref, bias_ref, normed_ref, q_ref, gate_ref, inv_ref, hidden_ref, block, lambda at: None
    )


def second_part(pre, weight, bias, after, block=512):
    rows, width = pre.shape
    outs = edge_outs(rows, width)
    return pl.pallas_call(
        functools.partial(second_kernel, block),
        in_specs=[VMEM, VMEM, VMEM, ANY],
        out_specs=[VMEM] * len(outs),
        out_shape=outs,
        scratch_shapes=[pltpu.VMEM((rows, width), BF16)],
        cost_estimate=cost(6 * rows * width * width, 10 * rows * width),
        compiler_params=params(16),
        name="second_part",
    )(pre, weight, bias, after)


def join_kernel(parts, *refs):
    out_ref, rows = refs[-1], refs[0].shape[0]
    for k in range(parts):
        out_ref[k * rows : (k + 1) * rows, :] = refs[k][...]


def join(pieces, after):
    rows, width = pieces[0].shape
    return pl.pallas_call(
        functools.partial(join_kernel, len(pieces)),
        in_specs=[VMEM] * len(pieces) + [ANY],
        out_specs=VMEM,
        out_shape=in_vmem((len(pieces) * rows, width), pieces[0].dtype),
        cost_estimate=cost(0, 4 * len(pieces) * rows * width),
        compiler_params=params(8),
        name="join",
    )(*pieces, after)


def after_kernel(
    parts, chunks, owned, caps, block, me_ref, ids_ref, slots_ref, weight_ref, gain_ref, *refs
):
    edge_refs = [refs[4 * k : 4 * k + 4] for k in range(parts)]
    refs = refs[4 * parts :]
    pieces, d_ref, sums_refs = refs[: -1 - chunks], refs[-1 - chunks], refs[-chunks:]
    slots = ids_ref.shape[0]
    count = slots // caps
    edges, width = d_ref.shape
    me = me_ref[0]
    weight = weight_ref[...]

    row = lax.broadcasted_iota(jnp.int32, (slots, 1), 0)
    distance, place, step = distance_of(row, caps, count), jnp.zeros_like(row), 1
    for shift, radix in stages_of(count):
        place = place + ((distance >> shift) & (radix - 1)) * step
        step *= radix
    place = place * owned + ids_ref[...][:, :1].astype(jnp.int32)
    piece_rows = pieces[0].shape[0]
    column = lax.broadcasted_iota(jnp.int32, (slots, piece_rows), 1)
    rows = jnp.zeros((slots, width), F32)
    for k, piece in enumerate(pieces):
        pick = (place == column + k * piece_rows).astype(F32).astype(BF16)
        rows += dot(pick, piece[...])
    rows = rows * gain_ref[...]
    rows = rows - jnp.mean(rows, axis=-1, keepdims=True)
    mean_rows = (rows * (1.0 / width)).astype(BF16)
    both = dot_t(jnp.concatenate(split(rows), axis=0), weight)
    s_both = jnp.concatenate(split(both[:slots] + both[slots:]), axis=0)

    key = (distance ^ me) * caps + row % caps
    key = jnp.concatenate([key, key], axis=0)
    mean_rows = jnp.concatenate([mean_rows, jnp.zeros_like(mean_rows)], axis=0)
    sums = jnp.zeros((slots, width), F32)
    edge_at = [(part, at) for part in edge_refs for at in range(0, part[0].shape[0], block)]
    last = None
    for number in range(len(edge_at) + 1):
        this = None
        if number < len(edge_at):
            (normed_ref, q_ref, gate_ref, inv_ref), at = edge_at[number]
            piece = slice(at, at + block)
            onehot_t = (key == slots_ref[:, number * block : (number + 1) * block]).astype(F32)
            onehot = onehot_t.T
            g = dot_t(normed_ref[piece], mean_rows)
            s_rows = dot(onehot.astype(BF16), s_both)
            this = (onehot_t[:slots].astype(BF16), onehot, g, s_rows, q_ref, gate_ref, inv_ref, at)
        if last is not None:
            onehot_t, onehot, g, s_rows, q_ref, gate_ref, inv_ref, first = last
            at = (number - 1) * block
            for row in range(0, block, CHUNK):
                piece, inner = slice(first + row, first + row + CHUNK), slice(row, row + CHUNK)
                c = jnp.sum(onehot[inner] * g[inner], axis=-1, keepdims=True)
                inv = jnp.concatenate([inv_ref[piece]] * (width // LANES), axis=1)
                d = gate_ref[piece] * inv * (s_rows[inner] - c * q_ref[piece].astype(F32))
                d_ref[at + row : at + row + CHUNK, :] = d.astype(BF16)
            d = d_ref[at : at + block, :]
            sums += dot(onehot_t, d)
        last = this

    each = slots // chunks
    for k, sums_ref in enumerate(sums_refs):
        sums_ref[:, :width] = sums[k * each : (k + 1) * each]
        sums_ref[:, width:] = ids_ref[k * each : (k + 1) * each, :]


def after(me, ids, slots, weight, gain, parts, pieces, owned, caps, chunks, block=512):
    edges, width = slots.shape[1], weight.shape[0]
    each = ids.shape[0] // chunks
    return pl.pallas_call(
        functools.partial(after_kernel, len(parts), chunks, owned, caps, block),
        in_specs=[SMEM] + [VMEM] * (4 + 4 * len(parts) + len(pieces)),
        out_specs=[VMEM] * (1 + chunks),
        out_shape=[in_vmem((edges, width), BF16)]
        + [in_vmem((each, width + LANES), F32)] * chunks,
        cost_estimate=cost(6 * edges * width * width, 8 * edges * width),
        compiler_params=params(20),
        name="after",
    )(me, ids, slots, weight, gain, *[a for part in parts for a in part], *pieces)


def segments_kernel(block, starts_ref, senders_ref, d_ref, total_ref):
    edges, width = d_ref.shape
    total_ref[:8, :] = jnp.zeros((8, width), F32)
    total_ref[G_DEV : G_DEV + RIM, :] = jnp.zeros((RIM, width), F32)
    row = lax.broadcasted_iota(jnp.int32, (block + 16, block), 0)
    for at in range(0, edges, block):
        base = pl.multiple_of(starts_ref[at] // 8 * 8, 8)
        onehot = (row == senders_ref[:, at : at + block] - base).astype(F32).astype(BF16)
        sums = dot(onehot, d_ref[at : at + block, :])
        total_ref[pl.ds(base, 8), :] += sums[:8]
        total_ref[pl.ds(pl.multiple_of(base + 8, 8), block + 8), :] = sums[8:]


def segments(senders, d_preact, block=256):
    edges, width = d_preact.shape
    return pl.pallas_call(
        functools.partial(segments_kernel, block),
        in_specs=[SMEM] + [VMEM] * 2,
        out_specs=VMEM,
        out_shape=in_vmem((G_DEV + RIM + block + 16, width), F32),
        cost_estimate=cost(4 * edges * width * width, 4 * edges * width),
        compiler_params=params(16),
        name="segments",
    )(senders, senders.reshape(1, edges), d_preact)


def grid_kernel(block, total_ref, carried_ref, weight_ref, out_hbm, out_ref, sem):
    weight = weight_ref[...]
    copies = []
    for k, at in enumerate(range(0, G_DEV, block)):
        rows = total_ref[at : at + block, :]
        if at == 0:
            rows = jnp.concatenate([rows[:RIM] + carried_ref[...].astype(F32), rows[RIM:]], axis=0)
        out_ref[at : at + block, :] = dot_t(rows.astype(BF16), weight).astype(BF16)
        copies.append(
            pltpu.make_async_copy(out_ref.at[pl.ds(at, block)], out_hbm.at[pl.ds(at, block)], sem.at[k])
        )
        copies[-1].start()
    for copy in copies:
        copy.wait()


def grid_rows(total, carried, weight, block=512):
    width = weight.shape[0]
    return pl.pallas_call(
        functools.partial(grid_kernel, block),
        in_specs=[VMEM] * 3,
        out_specs=HBM,
        out_shape=like((G_DEV, width), BF16),
        scratch_shapes=[pltpu.VMEM((G_DEV, width), BF16), DMA((G_DEV // block,))],
        cost_estimate=cost(2 * G_DEV * width * width, 6 * G_DEV * width),
        compiler_params=params(16),
        name="grid_rows",
    )(total, carried, weight)


def regroup_kernel(groups, parts, *refs):
    total_ref, rim_ref, *outs = refs[parts:]
    rim_ref[...] = total_ref[G_DEV : G_DEV + RIM, :].astype(BF16)
    low = groups // len(outs)
    each = refs[0].shape[0] // groups
    for j, out_ref in enumerate(outs):
        for g in range(low):
            for k in range(parts):
                to, at = (g * parts + k) * each, (j * low + g) * each
                out_ref[to : to + each, :] = refs[k][at : at + each, :]


def regroup(arrived, radix, low, total):
    rows, width = arrived[0].shape
    parts = len(arrived)
    return pl.pallas_call(
        functools.partial(regroup_kernel, radix * low, parts),
        in_specs=[VMEM] * (parts + 1),
        out_specs=[VMEM] * (1 + radix),
        out_shape=[in_vmem((RIM, total.shape[1]), BF16)]
        + [in_vmem((rows * parts // radix, width), F32)] * radix,
        cost_estimate=cost(0, 8 * rows * parts * width),
        compiler_params=params(8),
        name="regroup",
    )(*arrived, total)


def mesh_kernel(parts, *refs):
    pieces, weight_ref, out_ref = refs[:parts], refs[parts], refs[-1]
    owned, width = out_ref.shape
    rows = jnp.concatenate([piece[:, :width] for piece in pieces], axis=0)
    ids = jnp.concatenate([piece[:, width:] for piece in pieces], axis=0)
    ids = jnp.concatenate([ids, ids], axis=0).T[:owned].astype(jnp.int32)
    pick = (lax.broadcasted_iota(jnp.int32, ids.shape, 0) == ids).astype(F32)
    total = dot(pick.astype(BF16), jnp.concatenate(split(rows), axis=0))
    both = dot_t(jnp.concatenate(split(total), axis=0), weight_ref[...])
    out_ref[...] = (both[:owned] + both[owned:]).astype(BF16)


def mesh_rows(pieces, weight, owned, after):
    width = weight.shape[0]
    return pl.pallas_call(
        functools.partial(mesh_kernel, len(pieces)),
        in_specs=[VMEM] * (len(pieces) + 1) + [ANY],
        out_specs=VMEM,
        out_shape=like((owned, width), BF16),
        cost_estimate=cost(2 * owned * width * width, 2 * width * width),
        compiler_params=params(8),
        name="mesh_rows",
    )(*pieces, weight, in_hbm(after))


def on_device(
    saved_preact,
    edge_senders,
    edge_slots,
    mesh_requests,
    mesh_cotangent,
    out_weight,
    out_bias,
    ln_gain,
    grid_weight,
    mesh_weight,
):
    count = lax.axis_size("band")
    me = lax.axis_index("band")
    owned, width = mesh_cotangent.shape
    edges = saved_preact.shape[0]
    stages = stages_of(count)

    sources = (
        out_weight,
        out_bias.reshape(1, width),
        grid_weight,
        mesh_weight,
        ln_gain.reshape(1, width),
        mesh_cotangent,
    )
    weight, bias, weight_g, weight_m, gain, own_rows, ids, more, *first = first_part(
        saved_preact, edges // 6, sources, me.reshape(1), mesh_requests.swapaxes(1, 2)
    )

    held = [mesh_cotangent]
    for number, (shift, radix) in enumerate(stages):
        if number == 1:
            held = [join([own_rows, *held[1:]], first[0])]
        elif number > 1:
            held = [join(held, ids)]
        held += [swap(held[0], count, j << shift) for j in range(1, radix)]
        if number == 1:
            second = second_part(more, weight, bias, held[0])

    back = stages[::-1]
    d_preact, *chunks = after(
        me.reshape(1),
        ids,
        edge_slots.reshape(1, edges),
        weight,
        gain,
        [first, second],
        held,
        owned,
        mesh_requests.shape[2],
        back[0][1],
    )

    total = segments(edge_senders, d_preact)
    arrived, carried, left = None, None, count
    for shift, radix in back:
        if arrived is not None:
            rim, *chunks = regroup(arrived, radix, left // radix, total)
            if carried is None:
                carried = lax.ppermute(rim, "band", [(i, (i + 1) % count) for i in range(count)])
        left //= radix
        arrived = [chunks[0]] + [swap(chunks[j], count, j << shift) for j in range(1, radix)]
    grid_adjoint = grid_rows(total, carried, weight_g)
    mesh_adjoint = mesh_rows(arrived, weight_m, owned, grid_adjoint)
    return (grid_adjoint, mesh_adjoint)


def solution(mesh):
    in_specs = (
        P(("groups", "band"), None),
        P("band"),
        P("band"),
        P("band", None, None),
        P(("groups", "band"), None),
        P(),
        P(),
        P(),
        P(),
        P(),
    )
    out_specs = (P(("groups", "band"), None), P(("groups", "band"), None))
    return jax.shard_map(
        on_device, mesh=mesh, in_specs=in_specs, out_specs=out_specs, check_vma=False
    )
```

```python
import functools

import jax
import jax.numpy as jnp
from jax import lax
from jax.experimental import pallas as pl
from jax.experimental.pallas import tpu as pltpu
from jax.sharding import PartitionSpec as P

G_DEV = 2048
RIM = 128
LANES = 128
EPS = 1e-05
CHUNK = 32
MIB = 1 << 20

BF16 = jnp.bfloat16
F32 = jnp.float32
VMEM = pl.BlockSpec(memory_space=pltpu.VMEM)
SMEM = pl.BlockSpec(memory_space=pltpu.SMEM)
HBM = pl.BlockSpec(memory_space=pltpu.HBM)
ANY = pl.BlockSpec(memory_space=pl.ANY)
DMA = pltpu.SemaphoreType.DMA


def stages_of(count):
    top = count.bit_length() - 1
    assert count == 1 << top
    stages = []
    while top > 0:
        low = max(0, top - 2)
        stages.append((low, 1 << (top - low)))
        top = low
    return stages


def distance_of(row, caps, count):
    group, distance, left = row // caps, 0, count
    for shift, radix in reversed(stages_of(count)):
        left //= radix
        distance = distance + ((group // left) % radix << shift)
    return distance


def swap(block, count, mask):
    return lax.ppermute(block, "band", [(i, i ^ mask) for i in range(count)])


def like(shape, dtype):
    return jax.ShapeDtypeStruct(shape, dtype)


def in_hbm(x):
    return pltpu.with_memory_space_constraint(x, pltpu.HBM)


def in_vmem(shape, dtype):
    return pltpu.VMEM(shape, dtype)


def dot(a, b):
    return jnp.dot(a, b, preferred_element_type=F32)


def dot_t(a, b):
    return lax.dot_general(a, b, (((1,), (1,)), ((), ())), preferred_element_type=F32)


def split(x):
    high = x.astype(BF16)
    return high, (x - high.astype(F32)).astype(BF16)


def cost(flops, size):
    return pl.CostEstimate(flops=int(flops), bytes_accessed=int(size), transcendentals=0)


def params(limit):
    return pltpu.CompilerParams(vmem_limit_bytes=limit * MIB)


def edge_blocks(pre_at, weight_ref, bias_ref, normed_ref, q_ref, gate_ref, hidden_ref, block):
    weight, bias = weight_ref[...], bias_ref[...]
    rows, last = normed_ref.shape[0], None
    for at in range(0, rows + block, block):
        this = None
        if at < rows:
            pre_ref, first = pre_at(at)
            for row in range(at, at + block, CHUNK):
                piece = slice(row, row + CHUNK)
                half = 0.5 * pre_ref[row - first : row - first + CHUNK].astype(F32)
                t = jnp.tanh(half)
                double = 1.0 + t
                h = half * double
                hidden_ref[piece] = h.astype(BF16)
                gate_ref[piece] = double + h * (1.0 - t)
            this = dot(hidden_ref[at : at + block], weight)
        if last is not None:
            for row in range(0, block, CHUNK):
                piece = slice(at - block + row, at - block + row + CHUNK)
                out = last[row : row + CHUNK] + bias
                centre = out - jnp.mean(out, axis=-1, keepdims=True)
                inv = lax.rsqrt(jnp.mean(centre * centre, axis=-1, keepdims=True) + EPS)
                normed_ref[piece] = (centre * inv).astype(BF16)
                gate_ref[piece] = gate_ref[piece] * (0.5 * inv)
            q_ref[at - block : at] = dot_t(normed_ref[at - block : at], weight).astype(BF16)
        last = this


def arriving(loads, pre_ref, block, first=0):
    def pre_at(at):
        loads[(at - first) // block].wait()
        return pre_ref, first

    return pre_at


def first_kernel(block, copies, pre_hbm, *refs):
    sources, (me_ref, requests_hbm), refs = refs[:copies], refs[copies : copies + 2], refs[copies + 2 :]
    targets, refs = refs[:copies], refs[copies:]
    ids_ref, next_ref, normed_ref, q_ref, gate_ref, pre_ref, hidden_ref, requests_ref, sem = refs
    rows = normed_ref.shape[0]

    def load(k, source, target):
        return pltpu.make_async_copy(source, target, sem.at[k])

    others = [load(k, a, b) for k, (a, b) in enumerate(zip(sources, targets))]
    loads = [
        load(copies + at // block, pre_hbm.at[pl.ds(at, block)], pre_ref.at[pl.ds(at, block)])
        for at in range(0, rows, block)
    ]
    more = load(copies + len(loads), pre_hbm.at[pl.ds(rows, next_ref.shape[0])], next_ref)
    asked = load(copies + len(loads) + 1, requests_hbm, requests_ref)
    for copy in others[:2] + loads + others[2:] + [more, asked]:
        copy.start()
    for copy in others[:2]:
        copy.wait()
    edge_blocks(
        arriving(loads, pre_ref, block), targets[0], targets[1], normed_ref, q_ref, gate_ref, hidden_ref, block
    )
    for copy in others[2:] + [more, asked]:
        copy.wait()
    slots, caps = ids_ref.shape[0], requests_ref.shape[1]
    count = slots // caps
    row = lax.broadcasted_iota(jnp.int32, ids_ref.shape, 0)
    ids = jnp.zeros(ids_ref.shape, jnp.int32)
    for r in range(slots):
        owner = me_ref[0] ^ distance_of(r, caps, count)
        ids = jnp.where(row == r, requests_ref[0, r % caps, owner], ids)
    ids_ref[...] = ids.astype(F32)


def first_part(preact, rows, sources, me, requests, block=512):
    width = preact.shape[1]
    copies = len(sources)
    outs = [in_vmem(a.shape, a.dtype) for a in sources]
    outs += [in_vmem((requests.shape[1] * requests.shape[2], LANES), F32)]
    outs += [in_vmem((block, width), BF16)]
    outs += [in_vmem((rows, width), BF16)] * 2 + [in_vmem((rows, width), F32)]
    return pl.pallas_call(
        functools.partial(first_kernel, block, copies),
        in_specs=[HBM] * (1 + copies) + [SMEM, HBM],
        out_specs=[VMEM] * len(outs),
        out_shape=outs,
        scratch_shapes=[
            pltpu.VMEM((rows, width), BF16),
            pltpu.VMEM((rows, width), BF16),
            pltpu.SMEM(requests.shape, jnp.int32),
            DMA((copies + rows // block + 2,)),
        ],
        cost_estimate=cost(6 * rows * width * width, 10 * rows * width),
        compiler_params=params(16),
        name="first_part",
    )(in_hbm(preact), *[in_hbm(a) for a in sources], me, in_hbm(requests))


def second_kernel(block, copies, next_ref, weight_ref, bias_ref, after_ref, pre_hbm, *refs):
    sources, targets, refs = refs[:copies], refs[copies : 2 * copies], refs[2 * copies :]
    normed_ref, q_ref, gate_ref, pre_ref, hidden_ref, sem = refs
    done = pre_hbm.shape[0] - normed_ref.shape[0] + block
    loads = [
        pltpu.make_async_copy(
            pre_hbm.at[pl.ds(done + at, block)], pre_ref.at[pl.ds(at, block)], sem.at[copies + at // block]
        )
        for at in range(0, pre_ref.shape[0], block)
    ]
    others = [pltpu.make_async_copy(a, b, sem.at[k]) for k, (a, b) in enumerate(zip(sources, targets))]
    for copy in loads + others:
        copy.start()
    later = arriving(loads, pre_ref, block, block)
    edge_blocks(
        lambda at: later(at) if at else (next_ref, 0),
        weight_ref,
        bias_ref,
        normed_ref,
        q_ref,
        gate_ref,
        hidden_ref,
        block,
    )
    for copy in others:
        copy.wait()


def second_part(preact, rows, following, weight, bias, sources, after):
    block, width = following.shape
    copies = len(sources)
    outs = [in_vmem(a.shape, a.dtype) for a in sources]
    outs += [in_vmem((rows, width), BF16)] * 2 + [in_vmem((rows, width), F32)]
    return pl.pallas_call(
        functools.partial(second_kernel, block, copies),
        in_specs=[VMEM, VMEM, VMEM, ANY, HBM] + [HBM] * copies,
        out_specs=[VMEM] * len(outs),
        out_shape=outs,
        scratch_shapes=[
            pltpu.VMEM((rows - block, width), BF16),
            pltpu.VMEM((rows, width), BF16),
            DMA((copies + (rows - block) // block,)),
        ],
        cost_estimate=cost(6 * rows * width * width, 10 * rows * width),
        compiler_params=params(20),
        name="second_part",
    )(following, weight, bias, after, in_hbm(preact), *[in_hbm(a) for a in sources])


def join_kernel(parts, *refs):
    out_ref, rows = refs[-1], refs[0].shape[0]
    for k in range(parts):
        out_ref[k * rows : (k + 1) * rows, :] = refs[k][...]


def join(pieces, after):
    rows, width = pieces[0].shape
    return pl.pallas_call(
        functools.partial(join_kernel, len(pieces)),
        in_specs=[VMEM] * len(pieces) + [ANY],
        out_specs=VMEM,
        out_shape=in_vmem((len(pieces) * rows, width), pieces[0].dtype),
        cost_estimate=cost(0, 4 * len(pieces) * rows * width),
        compiler_params=params(8),
        name="join",
    )(*pieces, after)


def after_kernel(
    parts, chunks, owned, caps, block, me_ref, ids_ref, slots_ref, senders_ref, weight_ref, gain_ref, *refs
):
    edge_refs = [refs[3 * k : 3 * k + 3] for k in range(parts)]
    refs = refs[3 * parts :]
    pieces, (d_ref, rim_ref), sums_refs = refs[: -2 - chunks], refs[-2 - chunks : -chunks], refs[-chunks:]
    slots = ids_ref.shape[0]
    count = slots // caps
    edges, width = d_ref.shape
    me = me_ref[0]
    weight = weight_ref[...]

    row = lax.broadcasted_iota(jnp.int32, (slots, 1), 0)
    distance, place, step = distance_of(row, caps, count), jnp.zeros_like(row), 1
    for shift, radix in stages_of(count):
        place = place + ((distance >> shift) & (radix - 1)) * step
        step *= radix
    place = place * owned + ids_ref[...][:, :1].astype(jnp.int32)
    piece_rows = pieces[0].shape[0]
    column = lax.broadcasted_iota(jnp.int32, (slots, piece_rows), 1)
    rows = jnp.zeros((slots, width), F32)
    for k, piece in enumerate(pieces):
        pick = (place == column + k * piece_rows).astype(F32).astype(BF16)
        rows += dot(pick, piece[...])
    rows = rows * gain_ref[...]
    rows = rows - jnp.mean(rows, axis=-1, keepdims=True)
    mean_rows = (rows * (1.0 / width)).astype(BF16)
    both = dot_t(jnp.concatenate(split(rows), axis=0), weight)
    s_both = jnp.concatenate(split(both[:slots] + both[slots:]), axis=0)

    key = (distance ^ me) * caps + row % caps
    key = jnp.concatenate([key, key], axis=0)
    mean_rows = jnp.concatenate([mean_rows, jnp.zeros_like(mean_rows)], axis=0)
    rim_row = lax.broadcasted_iota(jnp.int32, (RIM, block), 0) + G_DEV
    sums = jnp.zeros((slots, width), F32)
    rim = jnp.zeros((RIM, width), F32)
    edge_at = [(part, at) for part in edge_refs for at in range(0, part[0].shape[0], block)]
    last = None
    for number in range(len(edge_at) + 1):
        this = None
        if number < len(edge_at):
            (normed_ref, q_ref, gate_ref), at = edge_at[number]
            piece = slice(at, at + block)
            onehot_t = (key == slots_ref[:, number * block : (number + 1) * block]).astype(F32)
            onehot = onehot_t.T
            g = dot_t(normed_ref[piece], mean_rows)
            s_rows = dot(onehot.astype(BF16), s_both)
            this = (onehot_t[:slots].astype(BF16), onehot, g, s_rows, q_ref, gate_ref, at)
        if last is not None:
            onehot_t, onehot, g, s_rows, q_ref, gate_ref, first = last
            at = (number - 1) * block
            for row in range(0, block, CHUNK):
                piece, inner = slice(first + row, first + row + CHUNK), slice(row, row + CHUNK)
                c = jnp.sum(onehot[inner] * g[inner], axis=-1, keepdims=True)
                d = gate_ref[piece] * (s_rows[inner] - c * q_ref[piece].astype(F32))
                d_ref[at + row : at + row + CHUNK, :] = d.astype(BF16)
            d = d_ref[at : at + block, :]
            sums += dot(onehot_t, d)
            if at + block > G_DEV:
                pick = (rim_row == senders_ref[:, at : at + block]).astype(F32).astype(BF16)
                rim += dot(pick, d)
        last = this

    each = slots // chunks
    for k, sums_ref in enumerate(sums_refs):
        sums_ref[:, :width] = sums[k * each : (k + 1) * each]
        sums_ref[:, width:] = ids_ref[k * each : (k + 1) * each, :]
    rim_ref[...] = rim.astype(BF16)


def after(me, ids, slots, senders, weight, gain, parts, pieces, owned, caps, chunks, block=512):
    edges, width = slots.shape[1], weight.shape[0]
    each = ids.shape[0] // chunks
    return pl.pallas_call(
        functools.partial(after_kernel, len(parts), chunks, owned, caps, block),
        in_specs=[SMEM] + [VMEM] * (5 + 3 * len(parts) + len(pieces)),
        out_specs=[VMEM] * (2 + chunks),
        out_shape=[in_vmem((edges, width), BF16), in_vmem((RIM, width), BF16)]
        + [in_vmem((each, width + LANES), F32)] * chunks,
        cost_estimate=cost(6 * edges * width * width, 8 * edges * width),
        compiler_params=params(20),
        name="after",
    )(me, ids, slots, senders, weight, gain, *[a for part in parts for a in part], *pieces)


def segments_kernel(block, starts_ref, senders_ref, d_ref, total_ref):
    edges, width = d_ref.shape
    total_ref[:8, :] = jnp.zeros((8, width), F32)
    row = lax.broadcasted_iota(jnp.int32, (block + 16, block), 0)
    for at in range(0, edges, block):
        base = pl.multiple_of(starts_ref[at] // 8 * 8, 8)
        onehot = (row == senders_ref[:, at : at + block] - base).astype(F32).astype(BF16)
        sums = dot(onehot, d_ref[at : at + block, :])
        total_ref[pl.ds(base, 8), :] += sums[:8]
        total_ref[pl.ds(pl.multiple_of(base + 8, 8), block + 8), :] = sums[8:]


def segments(senders, d_preact, block=256):
    edges, width = d_preact.shape
    return pl.pallas_call(
        functools.partial(segments_kernel, block),
        in_specs=[SMEM] + [VMEM] * 2,
        out_specs=VMEM,
        out_shape=in_vmem((G_DEV + RIM + block + 16, width), F32),
        cost_estimate=cost(4 * edges * width * width, 4 * edges * width),
        compiler_params=params(16),
        name="segments",
    )(senders, senders.reshape(1, edges), d_preact)


def grid_kernel(block, total_ref, carried_ref, weight_ref, out_hbm, out_ref, sem):
    weight = weight_ref[...]
    copies = []
    for k, at in enumerate(range(0, G_DEV, block)):
        rows = total_ref[at : at + block, :]
        if at == 0:
            rows = jnp.concatenate([rows[:RIM] + carried_ref[...].astype(F32), rows[RIM:]], axis=0)
        out_ref[at : at + block, :] = dot_t(rows.astype(BF16), weight).astype(BF16)
        copies.append(
            pltpu.make_async_copy(out_ref.at[pl.ds(at, block)], out_hbm.at[pl.ds(at, block)], sem.at[k])
        )
        copies[-1].start()
    for copy in copies:
        copy.wait()


def grid_rows(total, carried, weight, block=512):
    width = weight.shape[0]
    return pl.pallas_call(
        functools.partial(grid_kernel, block),
        in_specs=[VMEM] * 3,
        out_specs=HBM,
        out_shape=like((G_DEV, width), BF16),
        scratch_shapes=[pltpu.VMEM((G_DEV, width), BF16), DMA((G_DEV // block,))],
        cost_estimate=cost(2 * G_DEV * width * width, 6 * G_DEV * width),
        compiler_params=params(16),
        name="grid_rows",
    )(total, carried, weight)


def regroup_kernel(groups, parts, *refs):
    outs = refs[parts + 1 :]
    low = groups // len(outs)
    each = refs[0].shape[0] // groups
    for j, out_ref in enumerate(outs):
        for g in range(low):
            for k in range(parts):
                to, at = (g * parts + k) * each, (j * low + g) * each
                out_ref[to : to + each, :] = refs[k][at : at + each, :]


def regroup(arrived, radix, low, after):
    rows, width = arrived[0].shape
    parts = len(arrived)
    return pl.pallas_call(
        functools.partial(regroup_kernel, radix * low, parts),
        in_specs=[VMEM] * parts + [ANY],
        out_specs=[VMEM] * radix,
        out_shape=[in_vmem((rows * parts // radix, width), F32)] * radix,
        cost_estimate=cost(0, 8 * rows * parts * width),
        compiler_params=params(8),
        name="regroup",
    )(*arrived, after)


def mesh_kernel(parts, *refs):
    pieces, weight_ref, out_ref = refs[:parts], refs[parts], refs[-1]
    owned, width = out_ref.shape
    rows = jnp.concatenate([piece[:, :width] for piece in pieces], axis=0)
    ids = jnp.concatenate([piece[:, width:] for piece in pieces], axis=0)
    ids = jnp.concatenate([ids, ids], axis=0).T[:owned].astype(jnp.int32)
    pick = (lax.broadcasted_iota(jnp.int32, ids.shape, 0) == ids).astype(F32)
    total = dot(pick.astype(BF16), jnp.concatenate(split(rows), axis=0))
    both = dot_t(jnp.concatenate(split(total), axis=0), weight_ref[...])
    out_ref[...] = (both[:owned] + both[owned:]).astype(BF16)


def mesh_rows(pieces, weight, owned, after):
    width = weight.shape[0]
    return pl.pallas_call(
        functools.partial(mesh_kernel, len(pieces)),
        in_specs=[VMEM] * (len(pieces) + 1) + [ANY],
        out_specs=VMEM,
        out_shape=like((owned, width), BF16),
        cost_estimate=cost(2 * owned * width * width, 2 * width * width),
        compiler_params=params(8),
        name="mesh_rows",
    )(*pieces, weight, in_hbm(after))


def on_device(
    saved_preact,
    edge_senders,
    edge_slots,
    mesh_requests,
    mesh_cotangent,
    out_weight,
    out_bias,
    ln_gain,
    grid_weight,
    mesh_weight,
):
    count = lax.axis_size("band")
    me = lax.axis_index("band")
    owned, width = mesh_cotangent.shape
    edges = saved_preact.shape[0]
    stages = stages_of(count)

    sources = (
        out_weight,
        out_bias.reshape(1, width),
        ln_gain.reshape(1, width),
        mesh_cotangent,
    )
    weight, bias, gain, own_rows, ids, following, *first = first_part(
        saved_preact, edges // 6, sources, me.reshape(1), mesh_requests.swapaxes(1, 2)
    )

    held = [mesh_cotangent]
    for number, (shift, radix) in enumerate(stages):
        if number == 1:
            held = [join([own_rows, *held[1:]], first[0])]
        elif number > 1:
            held = [join(held, ids)]
        held += [swap(held[0], count, j << shift) for j in range(1, radix)]
        if number == 1:
            weight_g, weight_m, *second = second_part(
                saved_preact, edges - edges // 6, following, weight, bias, (grid_weight, mesh_weight), held[0]
            )

    back = stages[::-1]
    d_preact, rim, *chunks = after(
        me.reshape(1),
        ids,
        edge_slots.reshape(1, edges),
        edge_senders.reshape(1, edges),
        weight,
        gain,
        [first, second],
        held,
        owned,
        mesh_requests.shape[2],
        back[0][1],
    )

    total = segments(edge_senders, d_preact)
    carried = lax.ppermute(rim, "band", [(i, (i + 1) % count) for i in range(count)])
    arrived, left = None, count
    for shift, radix in back:
        if arrived is not None:
            chunks = regroup(arrived, radix, left // radix, total)
        left //= radix
        arrived = [chunks[0]] + [swap(chunks[j], count, j << shift) for j in range(1, radix)]
    grid_adjoint = grid_rows(total, carried, weight_g)
    mesh_adjoint = mesh_rows(arrived, weight_m, owned, grid_adjoint)
    return (grid_adjoint, mesh_adjoint)


def solution(mesh):
    in_specs = (
        P(("groups", "band"), None),
        P("band"),
        P("band"),
        P("band", None, None),
        P(("groups", "band"), None),
        P(),
        P(),
        P(),
        P(),
        P(),
    )
    out_specs = (P(("groups", "band"), None), P(("groups", "band"), None))
    return jax.shard_map(
        on_device, mesh=mesh, in_specs=in_specs, out_specs=out_specs, check_vma=False
    )
```

```python
import functools

import jax
import jax.numpy as jnp
from jax import lax
from jax.experimental import pallas as pl
from jax.experimental.pallas import tpu as pltpu
from jax.sharding import PartitionSpec as P

G_DEV = 2048
RIM = 128
LANES = 128
EPS = 1e-05
CHUNK = 32
MIB = 1 << 20

BF16 = jnp.bfloat16
F32 = jnp.float32
VMEM = pl.BlockSpec(memory_space=pltpu.VMEM)
SMEM = pl.BlockSpec(memory_space=pltpu.SMEM)
HBM = pl.BlockSpec(memory_space=pltpu.HBM)
ANY = pl.BlockSpec(memory_space=pl.ANY)
DMA = pltpu.SemaphoreType.DMA


def stages_of(count):
    top = count.bit_length() - 1
    assert count == 1 << top
    stages = []
    while top > 0:
        low = max(0, top - 2)
        stages.append((low, 1 << (top - low)))
        top = low
    return stages


def distance_of(row, caps, count):
    group, distance, left = row // caps, 0, count
    for shift, radix in reversed(stages_of(count)):
        left //= radix
        distance = distance + ((group // left) % radix << shift)
    return distance


def swap(block, count, mask):
    return lax.ppermute(block, "band", [(i, i ^ mask) for i in range(count)])


def like(shape, dtype):
    return jax.ShapeDtypeStruct(shape, dtype)


def in_hbm(x):
    return pltpu.with_memory_space_constraint(x, pltpu.HBM)


def in_vmem(shape, dtype):
    return pltpu.VMEM(shape, dtype)


def dot(a, b):
    return jnp.dot(a, b, preferred_element_type=F32)


def dot_t(a, b):
    return lax.dot_general(a, b, (((1,), (1,)), ((), ())), preferred_element_type=F32)


def split(x):
    high = x.astype(BF16)
    return high, (x - high.astype(F32)).astype(BF16)


def cost(flops, size):
    return pl.CostEstimate(flops=int(flops), bytes_accessed=int(size), transcendentals=0)


def params(limit):
    return pltpu.CompilerParams(vmem_limit_bytes=limit * MIB)


def edge_blocks(pre_ref, weight_ref, bias_ref, normed_ref, q_ref, gate_ref, hidden_ref, block, arrive):
    weight, bias = weight_ref[...], bias_ref[...]
    rows, last = pre_ref.shape[0], None
    for at in range(0, rows + block, block):
        this = None
        if at < rows:
            arrive(at)
            for row in range(at, at + block, CHUNK):
                piece = slice(row, row + CHUNK)
                half = 0.5 * pre_ref[piece].astype(F32)
                t = jnp.tanh(half)
                double = 1.0 + t
                h = half * double
                hidden_ref[piece] = h.astype(BF16)
                gate_ref[piece] = double + h * (1.0 - t)
            this = dot(hidden_ref[at : at + block], weight)
        if last is not None:
            for row in range(0, block, CHUNK):
                piece = slice(at - block + row, at - block + row + CHUNK)
                out = last[row : row + CHUNK] + bias
                centre = out - jnp.mean(out, axis=-1, keepdims=True)
                inv = lax.rsqrt(jnp.mean(centre * centre, axis=-1, keepdims=True) + EPS)
                normed_ref[piece] = (centre * inv).astype(BF16)
                gate_ref[piece] = gate_ref[piece] * (0.5 * inv)
            q_ref[at - block : at] = dot_t(normed_ref[at - block : at], weight).astype(BF16)
        last = this


def first_kernel(block, copies, pre_hbm, *refs):
    sources, (me_ref, requests_hbm), refs = refs[:copies], refs[copies : copies + 2], refs[copies + 2 :]
    targets, refs = refs[:copies], refs[copies:]
    ids_ref, other_ref, normed_ref, q_ref, gate_ref, pre_ref, hidden_ref, requests_ref, sem = refs
    rows = normed_ref.shape[0]

    def load(k, source, target):
        return pltpu.make_async_copy(source, target, sem.at[k])

    others = [load(k, a, b) for k, (a, b) in enumerate(zip(sources, targets))]
    starts = list(range(0, rows, block))
    more_rows = other_ref.shape[0]
    loads = [
        load(copies + k, pre_hbm.at[pl.ds(at, block)], pre_ref.at[pl.ds(at, block)])
        for k, at in enumerate(starts)
    ]
    more = load(copies + len(loads), pre_hbm.at[pl.ds(rows, more_rows)], other_ref)
    asked = load(copies + len(loads) + 1, requests_hbm, requests_ref)
    for copy in others[:2] + loads + others[2:] + [more, asked]:
        copy.start()
    for copy in others[:2]:
        copy.wait()
    edge_blocks(
        pre_ref,
        targets[0],
        targets[1],
        normed_ref,
        q_ref,
        gate_ref,
        hidden_ref,
        block,
        lambda at: loads[at // block].wait(),
    )
    for copy in others[2:] + [more, asked]:
        copy.wait()
    slots, caps = ids_ref.shape[0], requests_ref.shape[1]
    count = slots // caps
    row = lax.broadcasted_iota(jnp.int32, ids_ref.shape, 0)
    ids = jnp.zeros(ids_ref.shape, jnp.int32)
    for r in range(slots):
        owner = me_ref[0] ^ distance_of(r, caps, count)
        ids = jnp.where(row == r, requests_ref[0, r % caps, owner], ids)
    ids_ref[...] = ids.astype(F32)


def first_part(preact, rows, sources, me, requests, block=512):
    edges, width = preact.shape
    copies = len(sources)
    outs = [in_vmem(a.shape, a.dtype) for a in sources]
    outs += [in_vmem((requests.shape[1] * requests.shape[2], LANES), F32)]
    outs += [in_vmem((edges - rows, width), BF16)]
    outs += [in_vmem((rows, width), BF16)] * 2 + [in_vmem((rows, width), F32)]
    return pl.pallas_call(
        functools.partial(first_kernel, block, copies),
        in_specs=[HBM] * (1 + copies) + [SMEM, HBM],
        out_specs=[VMEM] * len(outs),
        out_shape=outs,
        scratch_shapes=[
            pltpu.VMEM((rows, width), BF16),
            pltpu.VMEM((rows, width), BF16),
            pltpu.SMEM(requests.shape, jnp.int32),
            DMA((copies + rows // block + 2,)),
        ],
        cost_estimate=cost(6 * rows * width * width, 10 * rows * width),
        compiler_params=params(16),
        name="first_part",
    )(in_hbm(preact), *[in_hbm(a) for a in sources], me, in_hbm(requests))


def second_kernel(block, pre_ref, weight_ref, bias_ref, after_ref, normed_ref, q_ref, gate_ref, hidden_ref):
    edge_blocks(
        pre_ref, weight_ref, bias_ref, normed_ref, q_ref, gate_ref, hidden_ref, block, lambda at: None
    )


def second_part(pre, weight, bias, after, block=512):
    rows, width = pre.shape
    outs = [in_vmem((rows, width), BF16)] * 2 + [in_vmem((rows, width), F32)]
    return pl.pallas_call(
        functools.partial(second_kernel, block),
        in_specs=[VMEM, VMEM, VMEM, ANY],
        out_specs=[VMEM] * len(outs),
        out_shape=outs,
        scratch_shapes=[pltpu.VMEM((rows, width), BF16)],
        cost_estimate=cost(6 * rows * width * width, 10 * rows * width),
        compiler_params=params(16),
        name="second_part",
    )(pre, weight, bias, after)


def join_kernel(parts, *refs):
    out_ref, rows = refs[-1], refs[0].shape[0]
    for k in range(parts):
        out_ref[k * rows : (k + 1) * rows, :] = refs[k][...]


def join(pieces, after):
    rows, width = pieces[0].shape
    return pl.pallas_call(
        functools.partial(join_kernel, len(pieces)),
        in_specs=[VMEM] * len(pieces) + [ANY],
        out_specs=VMEM,
        out_shape=in_vmem((len(pieces) * rows, width), pieces[0].dtype),
        cost_estimate=cost(0, 4 * len(pieces) * rows * width),
        compiler_params=params(8),
        name="join",
    )(*pieces, after)


def pack(ref, sums, ids):
    half = sums.shape[1] // 2
    left = jnp.concatenate([sums[:, :half], ids], axis=1)
    right = jnp.concatenate([sums[:, half:], ids], axis=1)
    ref[...] = jnp.concatenate([left, right], axis=0).astype(BF16)


def unpack(ref):
    rows, half = ref.shape[0] // 2, ref.shape[1] - LANES
    both = ref[...].astype(F32)
    return jnp.concatenate([both[:rows, :half], both[rows:, :half]], axis=1), both[:rows, half:]


def after_kernel(
    parts, chunks, owned, caps, block, me_ref, ids_ref, slots_ref, senders_ref, weight_ref, gain_ref, *refs
):
    edge_refs = [refs[3 * k : 3 * k + 3] for k in range(parts)]
    refs = refs[3 * parts :]
    pieces, (d_ref, rim_ref), sums_refs = refs[: -2 - chunks], refs[-2 - chunks : -chunks], refs[-chunks:]
    slots = ids_ref.shape[0]
    count = slots // caps
    edges, width = d_ref.shape
    me = me_ref[0]
    weight = weight_ref[...]

    row = lax.broadcasted_iota(jnp.int32, (slots, 1), 0)
    distance, place, step = distance_of(row, caps, count), jnp.zeros_like(row), 1
    for shift, radix in stages_of(count):
        place = place + ((distance >> shift) & (radix - 1)) * step
        step *= radix
    place = place * owned + ids_ref[...][:, :1].astype(jnp.int32)
    piece_rows = pieces[0].shape[0]
    column = lax.broadcasted_iota(jnp.int32, (slots, piece_rows), 1)
    rows = jnp.zeros((slots, width), F32)
    for k, piece in enumerate(pieces):
        pick = (place == column + k * piece_rows).astype(F32).astype(BF16)
        rows += dot(pick, piece[...])
    rows = rows * gain_ref[...]
    rows = rows - jnp.mean(rows, axis=-1, keepdims=True)
    mean_rows = (rows * (1.0 / width)).astype(BF16)
    both = dot_t(jnp.concatenate(split(rows), axis=0), weight)
    s_both = jnp.concatenate(split(both[:slots] + both[slots:]), axis=0)

    key = (distance ^ me) * caps + row % caps
    key = jnp.concatenate([key, key], axis=0)
    mean_rows = jnp.concatenate([mean_rows, jnp.zeros_like(mean_rows)], axis=0)
    rim_row = lax.broadcasted_iota(jnp.int32, (RIM, block), 0) + G_DEV
    sums = jnp.zeros((slots, width), F32)
    rim = jnp.zeros((RIM, width), F32)
    edge_at = [(part, at) for part in edge_refs for at in range(0, part[0].shape[0], block)]
    last = None
    for number in range(len(edge_at) + 1):
        this = None
        if number < len(edge_at):
            (normed_ref, q_ref, gate_ref), at = edge_at[number]
            piece = slice(at, at + block)
            onehot_t = (key == slots_ref[:, number * block : (number + 1) * block]).astype(F32)
            onehot = onehot_t.T
            g = dot_t(normed_ref[piece], mean_rows)
            s_rows = dot(onehot.astype(BF16), s_both)
            this = (onehot_t[:slots].astype(BF16), onehot, g, s_rows, q_ref, gate_ref, at)
        if last is not None:
            onehot_t, onehot, g, s_rows, q_ref, gate_ref, first = last
            at = (number - 1) * block
            for row in range(0, block, CHUNK):
                piece, inner = slice(first + row, first + row + CHUNK), slice(row, row + CHUNK)
                c = jnp.sum(onehot[inner] * g[inner], axis=-1, keepdims=True)
                d = gate_ref[piece] * (s_rows[inner] - c * q_ref[piece].astype(F32))
                d_ref[at + row : at + row + CHUNK, :] = d.astype(BF16)
            d = d_ref[at : at + block, :]
            sums += dot(onehot_t, d)
            if at + block > G_DEV:
                pick = (rim_row == senders_ref[:, at : at + block]).astype(F32).astype(BF16)
                rim += dot(pick, d)
        last = this

    each = slots // chunks
    for k, sums_ref in enumerate(sums_refs):
        pack(sums_ref, sums[k * each : (k + 1) * each], ids_ref[k * each : (k + 1) * each, :])
    rim_ref[...] = rim.astype(BF16)


def after(me, ids, slots, senders, weight, gain, parts, pieces, owned, caps, chunks, block=512):
    edges, width = slots.shape[1], weight.shape[0]
    each = ids.shape[0] // chunks
    return pl.pallas_call(
        functools.partial(after_kernel, len(parts), chunks, owned, caps, block),
        in_specs=[SMEM] + [VMEM] * (5 + 3 * len(parts) + len(pieces)),
        out_specs=[VMEM] * (2 + chunks),
        out_shape=[in_vmem((edges, width), BF16), in_vmem((RIM, width), BF16)]
        + [in_vmem((2 * each, width // 2 + LANES), BF16)] * chunks,
        cost_estimate=cost(6 * edges * width * width, 8 * edges * width),
        compiler_params=params(20),
        name="after",
    )(me, ids, slots, senders, weight, gain, *[a for part in parts for a in part], *pieces)


def segments_kernel(block, starts_ref, senders_ref, d_ref, total_ref):
    edges, width = d_ref.shape
    total_ref[:8, :] = jnp.zeros((8, width), F32)
    row = lax.broadcasted_iota(jnp.int32, (block + 16, block), 0)
    for at in range(0, edges, block):
        base = pl.multiple_of(starts_ref[at] // 8 * 8, 8)
        onehot = (row == senders_ref[:, at : at + block] - base).astype(F32).astype(BF16)
        sums = dot(onehot, d_ref[at : at + block, :])
        total_ref[pl.ds(base, 8), :] += sums[:8]
        total_ref[pl.ds(pl.multiple_of(base + 8, 8), block + 8), :] = sums[8:]


def segments(senders, d_preact, block=256):
    edges, width = d_preact.shape
    return pl.pallas_call(
        functools.partial(segments_kernel, block),
        in_specs=[SMEM] + [VMEM] * 2,
        out_specs=VMEM,
        out_shape=in_vmem((G_DEV + RIM + block + 16, width), F32),
        cost_estimate=cost(4 * edges * width * width, 4 * edges * width),
        compiler_params=params(16),
        name="segments",
    )(senders, senders.reshape(1, edges), d_preact)


def grid_kernel(block, total_ref, carried_ref, weight_ref, out_hbm, out_ref, sem):
    weight = weight_ref[...]
    copies = []
    for k, at in enumerate(range(0, G_DEV, block)):
        rows = total_ref[at : at + block, :]
        if at == 0:
            rows = jnp.concatenate([rows[:RIM] + carried_ref[...].astype(F32), rows[RIM:]], axis=0)
        out_ref[at : at + block, :] = dot_t(rows.astype(BF16), weight).astype(BF16)
        copies.append(
            pltpu.make_async_copy(out_ref.at[pl.ds(at, block)], out_hbm.at[pl.ds(at, block)], sem.at[k])
        )
        copies[-1].start()
    for copy in copies:
        copy.wait()


def grid_rows(total, carried, weight, block=512):
    width = weight.shape[0]
    return pl.pallas_call(
        functools.partial(grid_kernel, block),
        in_specs=[VMEM] * 3,
        out_specs=HBM,
        out_shape=like((G_DEV, width), BF16),
        scratch_shapes=[pltpu.VMEM((G_DEV, width), BF16), DMA((G_DEV // block,))],
        cost_estimate=cost(2 * G_DEV * width * width, 6 * G_DEV * width),
        compiler_params=params(16),
        name="grid_rows",
    )(total, carried, weight)


def regroup_kernel(groups, parts, *refs):
    outs = refs[parts + 1 :]
    low = groups // len(outs)
    loaded = [unpack(ref) for ref in refs[:parts]]
    each = loaded[0][0].shape[0] // groups
    for j, out_ref in enumerate(outs):
        spans = [(k, (j * low + g) * each) for g in range(low) for k in range(parts)]
        pack(out_ref, *[jnp.concatenate([loaded[k][n][at : at + each] for k, at in spans], axis=0) for n in (0, 1)])


def regroup(arrived, radix, low, after):
    rows, width = arrived[0].shape
    parts = len(arrived)
    return pl.pallas_call(
        functools.partial(regroup_kernel, radix * low, parts),
        in_specs=[VMEM] * parts + [ANY],
        out_specs=[VMEM] * radix,
        out_shape=[in_vmem((rows * parts // radix, width), BF16)] * radix,
        cost_estimate=cost(0, 8 * rows * parts * width),
        compiler_params=params(8),
        name="regroup",
    )(*arrived, after)


def mesh_kernel(parts, *refs):
    pieces, weight_ref, out_ref = refs[:parts], refs[parts], refs[-1]
    owned, width = out_ref.shape
    loaded = [unpack(piece) for piece in pieces]
    rows = jnp.concatenate([sums for sums, _ in loaded], axis=0)
    ids = jnp.concatenate([ids for _, ids in loaded], axis=0).T[:owned].astype(jnp.int32)
    pick = (lax.broadcasted_iota(jnp.int32, ids.shape, 0) == ids).astype(F32)
    total = dot(pick.astype(BF16), rows.astype(BF16))
    both = dot_t(jnp.concatenate(split(total), axis=0), weight_ref[...])
    out_ref[...] = (both[:owned] + both[owned:]).astype(BF16)


def mesh_rows(pieces, weight, owned, after):
    width = weight.shape[0]
    return pl.pallas_call(
        functools.partial(mesh_kernel, len(pieces)),
        in_specs=[VMEM] * (len(pieces) + 1) + [ANY],
        out_specs=VMEM,
        out_shape=like((owned, width), BF16),
        cost_estimate=cost(2 * owned * width * width, 2 * width * width),
        compiler_params=params(8),
        name="mesh_rows",
    )(*pieces, weight, in_hbm(after))


def on_device(
    saved_preact,
    edge_senders,
    edge_slots,
    mesh_requests,
    mesh_cotangent,
    out_weight,
    out_bias,
    ln_gain,
    grid_weight,
    mesh_weight,
):
    count = lax.axis_size("band")
    me = lax.axis_index("band")
    owned, width = mesh_cotangent.shape
    edges = saved_preact.shape[0]
    stages = stages_of(count)

    sources = (
        out_weight,
        out_bias.reshape(1, width),
        grid_weight,
        mesh_weight,
        ln_gain.reshape(1, width),
        mesh_cotangent,
    )
    weight, bias, weight_g, weight_m, gain, own_rows, ids, more, *first = first_part(
        saved_preact, edges // 3, sources, me.reshape(1), mesh_requests.swapaxes(1, 2)
    )

    held = [mesh_cotangent]
    for number, (shift, radix) in enumerate(stages):
        if number == 1:
            held = [join([own_rows, *held[1:]], first[0])]
        elif number > 1:
            held = [join(held, ids)]
        held += [swap(held[0], count, j << shift) for j in range(1, radix)]
        if number == 1:
            second = second_part(more, weight, bias, held[0])

    back = stages[::-1]
    d_preact, rim, *chunks = after(
        me.reshape(1),
        ids,
        edge_slots.reshape(1, edges),
        edge_senders.reshape(1, edges),
        weight,
        gain,
        [first, second],
        held,
        owned,
        mesh_requests.shape[2],
        back[0][1],
    )

    total = segments(edge_senders, d_preact)
    carried = lax.ppermute(rim, "band", [(i, (i + 1) % count) for i in range(count)])
    arrived, left = None, count
    for shift, radix in back:
        if arrived is not None:
            chunks = regroup(arrived, radix, left // radix, total)
        left //= radix
        arrived = [chunks[0]] + [swap(chunks[j], count, j << shift) for j in range(1, radix)]
    grid_adjoint = grid_rows(total, carried, weight_g)
    mesh_adjoint = mesh_rows(arrived, weight_m, owned, grid_adjoint)
    return (grid_adjoint, mesh_adjoint)


def solution(mesh):
    in_specs = (
        P(("groups", "band"), None),
        P("band"),
        P("band"),
        P("band", None, None),
        P(("groups", "band"), None),
        P(),
        P(),
        P(),
        P(),
        P(),
    )
    out_specs = (P(("groups", "band"), None), P(("groups", "band"), None))
    return jax.shard_map(
        on_device, mesh=mesh, in_specs=in_specs, out_specs=out_specs, check_vma=False
    )
```

```python
import functools

import jax
import jax.numpy as jnp
from jax import lax
from jax.experimental import pallas as pl
from jax.experimental.pallas import tpu as pltpu
from jax.sharding import PartitionSpec as P

G_DEV = 2048
RIM = 128
LANES = 128
EPS = 1e-05
CHUNK = 32
MIB = 1 << 20

BF16 = jnp.bfloat16
F32 = jnp.float32
VMEM = pl.BlockSpec(memory_space=pltpu.VMEM)
SMEM = pl.BlockSpec(memory_space=pltpu.SMEM)
HBM = pl.BlockSpec(memory_space=pltpu.HBM)
ANY = pl.BlockSpec(memory_space=pl.ANY)
DMA = pltpu.SemaphoreType.DMA


def stages_of(count):
    top = count.bit_length() - 1
    assert count == 1 << top
    stages = []
    while top > 0:
        low = max(0, top - 2)
        stages.append((low, 1 << (top - low)))
        top = low
    return stages


def distance_of(row, caps, count):
    group, distance, left = row // caps, 0, count
    for shift, radix in stages_of(count):
        left //= radix
        distance = distance + ((group // left) % radix << shift)
    return distance


def swap(block, count, mask):
    return lax.ppermute(block, "band", [(i, i ^ mask) for i in range(count)])


def like(shape, dtype):
    return jax.ShapeDtypeStruct(shape, dtype)


def in_hbm(x):
    return pltpu.with_memory_space_constraint(x, pltpu.HBM)


def in_vmem(shape, dtype):
    return pltpu.VMEM(shape, dtype)


def dot(a, b):
    return jnp.dot(a, b, preferred_element_type=F32)


def dot_t(a, b):
    return lax.dot_general(a, b, (((1,), (1,)), ((), ())), preferred_element_type=F32)


def split(x):
    high = x.astype(BF16)
    return high, (x - high.astype(F32)).astype(BF16)


def cost(flops, size):
    return pl.CostEstimate(flops=int(flops), bytes_accessed=int(size), transcendentals=0)


def params(limit):
    return pltpu.CompilerParams(vmem_limit_bytes=limit * MIB)


def edge_blocks(pre_ref, weight_ref, bias_ref, normed_ref, q_ref, gate_ref, hidden_ref, block, arrive):
    weight, bias = weight_ref[...], bias_ref[...]
    rows, last = pre_ref.shape[0], None
    for at in range(0, rows + block, block):
        this = None
        if at < rows:
            arrive(at)
            for row in range(at, at + block, CHUNK):
                piece = slice(row, row + CHUNK)
                half = 0.5 * pre_ref[piece].astype(F32)
                t = jnp.tanh(half)
                double = 1.0 + t
                h = half * double
                hidden_ref[piece] = h.astype(BF16)
                gate_ref[piece] = double + h * (1.0 - t)
            this = dot(hidden_ref[at : at + block], weight)
        if last is not None:
            for row in range(0, block, CHUNK):
                piece = slice(at - block + row, at - block + row + CHUNK)
                out = last[row : row + CHUNK] + bias
                centre = out - jnp.mean(out, axis=-1, keepdims=True)
                inv = lax.rsqrt(jnp.mean(centre * centre, axis=-1, keepdims=True) + EPS)
                normed_ref[piece] = (centre * inv).astype(BF16)
                gate_ref[piece] = gate_ref[piece] * (0.5 * inv)
            q_ref[at - block : at] = dot_t(normed_ref[at - block : at], weight).astype(BF16)
        last = this


def first_kernel(block, copies, pre_hbm, *refs):
    sources, (me_ref, requests_hbm), refs = refs[:copies], refs[copies : copies + 2], refs[copies + 2 :]
    targets, refs = refs[:copies], refs[copies:]
    ids_ref, other_ref, normed_ref, q_ref, gate_ref, pre_ref, hidden_ref, requests_ref, sem = refs
    rows = normed_ref.shape[0]

    def load(k, source, target):
        return pltpu.make_async_copy(source, target, sem.at[k])

    others = [load(k, a, b) for k, (a, b) in enumerate(zip(sources, targets))]
    starts = list(range(0, rows, block))
    more_rows = other_ref.shape[0]
    loads = [
        load(copies + k, pre_hbm.at[pl.ds(at, block)], pre_ref.at[pl.ds(at, block)])
        for k, at in enumerate(starts)
    ]
    more = load(copies + len(loads), pre_hbm.at[pl.ds(rows, more_rows)], other_ref)
    asked = load(copies + len(loads) + 1, requests_hbm, requests_ref)
    for copy in [asked] + others[:2] + loads + others[2:] + [more]:
        copy.start()
    for copy in others[:2] + [asked]:
        copy.wait()
    slots, caps = ids_ref.shape[0], requests_ref.shape[1]
    count = slots // caps
    row = lax.broadcasted_iota(jnp.int32, ids_ref.shape, 0)
    ids = jnp.zeros(ids_ref.shape, jnp.int32)
    for r in range(slots):
        owner = me_ref[0] ^ distance_of(r, caps, count)
        ids = jnp.where(row == r, requests_ref[0, r % caps, owner], ids)
    ids_ref[...] = ids.astype(F32)
    edge_blocks(
        pre_ref,
        targets[0],
        targets[1],
        normed_ref,
        q_ref,
        gate_ref,
        hidden_ref,
        block,
        lambda at: loads[at // block].wait(),
    )
    for copy in others[2:] + [more]:
        copy.wait()


def first_part(preact, rows, sources, me, requests, block=512):
    edges, width = preact.shape
    copies = len(sources)
    outs = [in_vmem(a.shape, a.dtype) for a in sources]
    outs += [in_vmem((requests.shape[1] * requests.shape[2], LANES), F32)]
    outs += [in_vmem((edges - rows, width), BF16)]
    outs += [in_vmem((rows, width), BF16)] * 2 + [in_vmem((rows, width), F32)]
    return pl.pallas_call(
        functools.partial(first_kernel, block, copies),
        in_specs=[HBM] * (1 + copies) + [SMEM, HBM],
        out_specs=[VMEM] * len(outs),
        out_shape=outs,
        scratch_shapes=[
            pltpu.VMEM((rows, width), BF16),
            pltpu.VMEM((rows, width), BF16),
            pltpu.SMEM(requests.shape, jnp.int32),
            DMA((copies + rows // block + 2,)),
        ],
        cost_estimate=cost(6 * rows * width * width, 10 * rows * width),
        compiler_params=params(16),
        name="first_part",
    )(in_hbm(preact), *[in_hbm(a) for a in sources], me, in_hbm(requests))


def second_kernel(block, pre_ref, weight_ref, bias_ref, after_ref, normed_ref, q_ref, gate_ref, hidden_ref):
    edge_blocks(
        pre_ref, weight_ref, bias_ref, normed_ref, q_ref, gate_ref, hidden_ref, block, lambda at: None
    )


def second_part(pre, weight, bias, after, block=512):
    rows, width = pre.shape
    outs = [in_vmem((rows, width), BF16)] * 2 + [in_vmem((rows, width), F32)]
    return pl.pallas_call(
        functools.partial(second_kernel, block),
        in_specs=[VMEM, VMEM, VMEM, ANY],
        out_specs=[VMEM] * len(outs),
        out_shape=outs,
        scratch_shapes=[pltpu.VMEM((rows, width), BF16)],
        cost_estimate=cost(6 * rows * width * width, 10 * rows * width),
        compiler_params=params(16),
        name="second_part",
    )(pre, weight, bias, after)


def join_kernel(parts, *refs):
    out_ref, rows = refs[-1], refs[0].shape[0]
    for k in range(parts):
        out_ref[k * rows : (k + 1) * rows, :] = refs[k][...]


def join(pieces, after):
    rows, width = pieces[0].shape
    return pl.pallas_call(
        functools.partial(join_kernel, len(pieces)),
        in_specs=[VMEM] * len(pieces) + [ANY],
        out_specs=VMEM,
        out_shape=in_vmem((len(pieces) * rows, width), pieces[0].dtype),
        cost_estimate=cost(0, 4 * len(pieces) * rows * width),
        compiler_params=params(8),
        name="join",
    )(*pieces, after)


def pack(ref, sums, ids):
    half = sums.shape[1] // 2
    left = jnp.concatenate([sums[:, :half], ids], axis=1)
    right = jnp.concatenate([sums[:, half:], ids], axis=1)
    ref[...] = jnp.concatenate([left, right], axis=0).astype(BF16)


def unpack(ref):
    rows, half = ref.shape[0] // 2, ref.shape[1] - LANES
    both = ref[...].astype(F32)
    return jnp.concatenate([both[:rows, :half], both[rows:, :half]], axis=1), both[:rows, half:]


def after_kernel(
    parts, chunks, owned, caps, block, me_ref, ids_ref, slots_ref, senders_ref, weight_ref, gain_ref, *refs
):
    edge_refs = [refs[3 * k : 3 * k + 3] for k in range(parts)]
    refs = refs[3 * parts :]
    pieces, (d_ref, rim_ref), sums_refs = refs[: -2 - chunks], refs[-2 - chunks : -chunks], refs[-chunks:]
    slots = ids_ref.shape[0]
    count = slots // caps
    edges, width = d_ref.shape
    me = me_ref[0]
    weight = weight_ref[...]

    row = lax.broadcasted_iota(jnp.int32, (slots, 1), 0)
    distance, place, step = distance_of(row, caps, count), jnp.zeros_like(row), 1
    for shift, radix in stages_of(count):
        place = place + ((distance >> shift) & (radix - 1)) * step
        step *= radix
    place = place * owned + ids_ref[...][:, :1].astype(jnp.int32)
    piece_rows = pieces[0].shape[0]
    column = lax.broadcasted_iota(jnp.int32, (slots, piece_rows), 1)
    rows = jnp.zeros((slots, width), F32)
    for k, piece in enumerate(pieces):
        pick = (place == column + k * piece_rows).astype(F32).astype(BF16)
        rows += dot(pick, piece[...])
    rows = rows * gain_ref[...]
    rows = rows - jnp.mean(rows, axis=-1, keepdims=True)
    mean_rows = (rows * (1.0 / width)).astype(BF16)
    both = dot_t(jnp.concatenate(split(rows), axis=0), weight)
    s_both = jnp.concatenate(split(both[:slots] + both[slots:]), axis=0)

    key = (distance ^ me) * caps + row % caps
    key = jnp.concatenate([key, key], axis=0)
    mean_rows = jnp.concatenate([mean_rows, jnp.zeros_like(mean_rows)], axis=0)
    rim_row = lax.broadcasted_iota(jnp.int32, (RIM, block), 0) + G_DEV
    sums = jnp.zeros((slots, width), F32)
    rim = jnp.zeros((RIM, width), F32)
    edge_at = [(part, at) for part in edge_refs for at in range(0, part[0].shape[0], block)]
    last = None
    for number in range(len(edge_at) + 1):
        this = None
        if number < len(edge_at):
            (normed_ref, q_ref, gate_ref), at = edge_at[number]
            piece = slice(at, at + block)
            onehot_t = (key == slots_ref[:, number * block : (number + 1) * block]).astype(F32)
            onehot = onehot_t.T
            g = dot_t(normed_ref[piece], mean_rows)
            s_rows = dot(onehot.astype(BF16), s_both)
            this = (onehot_t[:slots].astype(BF16), onehot, g, s_rows, q_ref, gate_ref, at)
        if last is not None:
            onehot_t, onehot, g, s_rows, q_ref, gate_ref, first = last
            at = (number - 1) * block
            for row in range(0, block, CHUNK):
                piece, inner = slice(first + row, first + row + CHUNK), slice(row, row + CHUNK)
                c = jnp.sum(onehot[inner] * g[inner], axis=-1, keepdims=True)
                d = gate_ref[piece] * (s_rows[inner] - c * q_ref[piece].astype(F32))
                d_ref[at + row : at + row + CHUNK, :] = d.astype(BF16)
            d = d_ref[at : at + block, :]
            sums += dot(onehot_t, d)
            if at + block > G_DEV:
                pick = (rim_row == senders_ref[:, at : at + block]).astype(F32).astype(BF16)
                rim += dot(pick, d)
        last = this

    each = slots // chunks
    for k, sums_ref in enumerate(sums_refs):
        pack(sums_ref, sums[k * each : (k + 1) * each], ids_ref[k * each : (k + 1) * each, :])
    rim_ref[...] = rim.astype(BF16)


def after(me, ids, slots, senders, weight, gain, parts, pieces, owned, caps, chunks, block=512):
    edges, width = slots.shape[1], weight.shape[0]
    each = ids.shape[0] // chunks
    return pl.pallas_call(
        functools.partial(after_kernel, len(parts), chunks, owned, caps, block),
        in_specs=[SMEM] + [VMEM] * (5 + 3 * len(parts) + len(pieces)),
        out_specs=[VMEM] * (2 + chunks),
        out_shape=[in_vmem((edges, width), BF16), in_vmem((RIM, width), BF16)]
        + [in_vmem((2 * each, width // 2 + LANES), BF16)] * chunks,
        cost_estimate=cost(6 * edges * width * width, 8 * edges * width),
        compiler_params=params(20),
        name="after",
    )(me, ids, slots, senders, weight, gain, *[a for part in parts for a in part], *pieces)


def segments_kernel(block, starts_ref, senders_ref, d_ref, total_ref):
    edges, width = d_ref.shape
    total_ref[:8, :] = jnp.zeros((8, width), F32)
    row = lax.broadcasted_iota(jnp.int32, (block + 16, block), 0)
    for at in range(0, edges, block):
        base = pl.multiple_of(starts_ref[at] // 8 * 8, 8)
        onehot = (row == senders_ref[:, at : at + block] - base).astype(F32).astype(BF16)
        sums = dot(onehot, d_ref[at : at + block, :])
        total_ref[pl.ds(base, 8), :] += sums[:8]
        total_ref[pl.ds(pl.multiple_of(base + 8, 8), block + 8), :] = sums[8:]


def segments(senders, d_preact, block=256):
    edges, width = d_preact.shape
    return pl.pallas_call(
        functools.partial(segments_kernel, block),
        in_specs=[SMEM] + [VMEM] * 2,
        out_specs=VMEM,
        out_shape=in_vmem((G_DEV + RIM + block + 16, width), F32),
        cost_estimate=cost(4 * edges * width * width, 4 * edges * width),
        compiler_params=params(16),
        name="segments",
    )(senders, senders.reshape(1, edges), d_preact)


def grid_kernel(block, total_ref, carried_ref, weight_ref, out_hbm, out_ref, sem):
    weight = weight_ref[...]
    copies = []
    for k, at in enumerate(range(0, G_DEV, block)):
        rows = total_ref[at : at + block, :]
        if at == 0:
            rows = jnp.concatenate([rows[:RIM] + carried_ref[...].astype(F32), rows[RIM:]], axis=0)
        out_ref[at : at + block, :] = dot_t(rows.astype(BF16), weight).astype(BF16)
        copies.append(
            pltpu.make_async_copy(out_ref.at[pl.ds(at, block)], out_hbm.at[pl.ds(at, block)], sem.at[k])
        )
        copies[-1].start()
    for copy in copies:
        copy.wait()


def grid_rows(total, carried, weight, block=512):
    width = weight.shape[0]
    return pl.pallas_call(
        functools.partial(grid_kernel, block),
        in_specs=[VMEM] * 3,
        out_specs=HBM,
        out_shape=like((G_DEV, width), BF16),
        scratch_shapes=[pltpu.VMEM((G_DEV, width), BF16), DMA((G_DEV // block,))],
        cost_estimate=cost(2 * G_DEV * width * width, 6 * G_DEV * width),
        compiler_params=params(16),
        name="grid_rows",
    )(total, carried, weight)


def regroup_kernel(groups, parts, *refs):
    outs = refs[parts + 1 :]
    low = groups // len(outs)
    loaded = [unpack(ref) for ref in refs[:parts]]
    each = loaded[0][0].shape[0] // groups
    for j, out_ref in enumerate(outs):
        spans = [(k, (j * low + g) * each) for g in range(low) for k in range(parts)]
        pack(out_ref, *[jnp.concatenate([loaded[k][n][at : at + each] for k, at in spans], axis=0) for n in (0, 1)])


def regroup(arrived, radix, low, after):
    rows, width = arrived[0].shape
    parts = len(arrived)
    return pl.pallas_call(
        functools.partial(regroup_kernel, radix * low, parts),
        in_specs=[VMEM] * parts + [ANY],
        out_specs=[VMEM] * radix,
        out_shape=[in_vmem((rows * parts // radix, width), BF16)] * radix,
        cost_estimate=cost(0, 8 * rows * parts * width),
        compiler_params=params(8),
        name="regroup",
    )(*arrived, after)


def mesh_kernel(parts, *refs):
    pieces, weight_ref, out_ref = refs[:parts], refs[parts], refs[-1]
    owned, width = out_ref.shape
    loaded = [unpack(piece) for piece in pieces]
    rows = jnp.concatenate([sums for sums, _ in loaded], axis=0)
    ids = jnp.concatenate([ids for _, ids in loaded], axis=0).T[:owned].astype(jnp.int32)
    pick = (lax.broadcasted_iota(jnp.int32, ids.shape, 0) == ids).astype(F32)
    total = dot(pick.astype(BF16), rows.astype(BF16))
    both = dot_t(jnp.concatenate(split(total), axis=0), weight_ref[...])
    out_ref[...] = (both[:owned] + both[owned:]).astype(BF16)


def mesh_rows(pieces, weight, owned, after):
    width = weight.shape[0]
    return pl.pallas_call(
        functools.partial(mesh_kernel, len(pieces)),
        in_specs=[VMEM] * (len(pieces) + 1) + [ANY],
        out_specs=VMEM,
        out_shape=like((owned, width), BF16),
        cost_estimate=cost(2 * owned * width * width, 2 * width * width),
        compiler_params=params(8),
        name="mesh_rows",
    )(*pieces, weight, in_hbm(after))


def on_device(
    saved_preact,
    edge_senders,
    edge_slots,
    mesh_requests,
    mesh_cotangent,
    out_weight,
    out_bias,
    ln_gain,
    grid_weight,
    mesh_weight,
):
    count = lax.axis_size("band")
    me = lax.axis_index("band")
    owned, width = mesh_cotangent.shape
    edges = saved_preact.shape[0]
    stages = stages_of(count)

    sources = (
        out_weight,
        out_bias.reshape(1, width),
        grid_weight,
        mesh_weight,
        ln_gain.reshape(1, width),
        mesh_cotangent,
    )
    weight, bias, weight_g, weight_m, gain, own_rows, ids, more, *first = first_part(
        saved_preact, edges // 3, sources, me.reshape(1), mesh_requests.swapaxes(1, 2)
    )

    held = [mesh_cotangent]
    for number, (shift, radix) in enumerate(stages):
        if number == 1:
            held = [join([own_rows, *held[1:]], first[0])]
        elif number > 1:
            held = [join(held, ids)]
        held += [swap(held[0], count, j << shift) for j in range(1, radix)]
        if number == 1:
            second = second_part(more, weight, bias, held[0])

    back = stages
    d_preact, rim, *chunks = after(
        me.reshape(1),
        ids,
        edge_slots.reshape(1, edges),
        edge_senders.reshape(1, edges),
        weight,
        gain,
        [first, second],
        held,
        owned,
        mesh_requests.shape[2],
        back[0][1],
    )

    total = segments(edge_senders, d_preact)
    carried = lax.ppermute(rim, "band", [(i, (i + 1) % count) for i in range(count)])
    arrived, left = None, count
    for shift, radix in back:
        if arrived is not None:
            chunks = regroup(arrived, radix, left // radix, total)
        left //= radix
        arrived = [chunks[0]] + [swap(chunks[j], count, j << shift) for j in range(1, radix)]
    grid_adjoint = grid_rows(total, carried, weight_g)
    mesh_adjoint = mesh_rows(arrived, weight_m, owned, grid_adjoint)
    return (grid_adjoint, mesh_adjoint)


def solution(mesh):
    in_specs = (
        P(("groups", "band"), None),
        P("band"),
        P("band"),
        P("band", None, None),
        P(("groups", "band"), None),
        P(),
        P(),
        P(),
        P(),
        P(),
    )
    out_specs = (P(("groups", "band"), None), P(("groups", "band"), None))
    return jax.shard_map(
        on_device, mesh=mesh, in_specs=in_specs, out_specs=out_specs, check_vma=False
    )
```

```python
import functools

import jax
import jax.numpy as jnp
from jax import lax
from jax.experimental import pallas as pl
from jax.experimental.pallas import tpu as pltpu
from jax.sharding import PartitionSpec as P

G_DEV = 2048
RIM = 128
LANES = 128
EPS = 1e-05
CHUNK = 32
MIB = 1 << 20

BF16 = jnp.bfloat16
F32 = jnp.float32
VMEM = pl.BlockSpec(memory_space=pltpu.VMEM)
SMEM = pl.BlockSpec(memory_space=pltpu.SMEM)
HBM = pl.BlockSpec(memory_space=pltpu.HBM)
ANY = pl.BlockSpec(memory_space=pl.ANY)
DMA = pltpu.SemaphoreType.DMA


def stages_of(count):
    top = count.bit_length() - 1
    assert count == 1 << top
    stages = []
    while top > 0:
        low = max(0, top - 2)
        stages.append((low, 1 << (top - low)))
        top = low
    return stages


def distance_of(row, caps, count):
    group, distance, left = row // caps, 0, count
    for shift, radix in reversed(stages_of(count)):
        left //= radix
        distance = distance + ((group // left) % radix << shift)
    return distance


def swap(block, count, mask):
    return lax.ppermute(block, "band", [(i, i ^ mask) for i in range(count)])


def like(shape, dtype):
    return jax.ShapeDtypeStruct(shape, dtype)


def in_hbm(x):
    return pltpu.with_memory_space_constraint(x, pltpu.HBM)


def in_vmem(shape, dtype):
    return pltpu.VMEM(shape, dtype)


def dot(a, b):
    return jnp.dot(a, b, preferred_element_type=F32)


def dot_t(a, b):
    return lax.dot_general(a, b, (((1,), (1,)), ((), ())), preferred_element_type=F32)


def split(x):
    high = x.astype(BF16)
    return high, (x - high.astype(F32)).astype(BF16)


def cost(flops, size):
    return pl.CostEstimate(flops=int(flops), bytes_accessed=int(size), transcendentals=0)


def params(limit):
    return pltpu.CompilerParams(vmem_limit_bytes=limit * MIB)


def edge_blocks(pre_ref, weight_ref, bias_ref, normed_ref, q_ref, gate_ref, hidden_ref, block, arrive):
    weight, bias = weight_ref[...], bias_ref[...]
    rows, last = pre_ref.shape[0], None
    for at in range(0, rows + block, block):
        this = None
        if at < rows:
            arrive(at)
            for row in range(at, at + block, CHUNK):
                piece = slice(row, row + CHUNK)
                half = 0.5 * pre_ref[piece].astype(F32)
                t = jnp.tanh(half)
                double = 1.0 + t
                h = half * double
                hidden_ref[piece] = h.astype(BF16)
                gate_ref[piece] = double + h * (1.0 - t)
            this = dot(hidden_ref[at : at + block], weight)
        if last is not None:
            for row in range(0, block, CHUNK):
                piece = slice(at - block + row, at - block + row + CHUNK)
                out = last[row : row + CHUNK] + bias
                centre = out - jnp.mean(out, axis=-1, keepdims=True)
                inv = lax.rsqrt(jnp.mean(centre * centre, axis=-1, keepdims=True) + EPS)
                normed_ref[piece] = (centre * inv).astype(BF16)
                gate_ref[piece] = gate_ref[piece] * (0.5 * inv)
            q_ref[at - block : at] = dot_t(normed_ref[at - block : at], weight).astype(BF16)
        last = this


def first_kernel(block, copies, pre_hbm, *refs):
    sources, (me_ref, requests_hbm), refs = refs[:copies], refs[copies : copies + 2], refs[copies + 2 :]
    targets, refs = refs[:copies], refs[copies:]
    ids_ref, other_ref, normed_ref, q_ref, gate_ref, pre_ref, hidden_ref, requests_ref, sem = refs
    rows = normed_ref.shape[0]

    def load(k, source, target):
        return pltpu.make_async_copy(source, target, sem.at[k])

    others = [load(k, a, b) for k, (a, b) in enumerate(zip(sources, targets))]
    starts = list(range(0, rows, block))
    more_rows = other_ref.shape[0]
    loads = [
        load(copies + k, pre_hbm.at[pl.ds(at, block)], pre_ref.at[pl.ds(at, block)])
        for k, at in enumerate(starts)
    ]
    more = load(copies + len(loads), pre_hbm.at[pl.ds(rows, more_rows)], other_ref)
    asked = load(copies + len(loads) + 1, requests_hbm, requests_ref)
    for copy in [asked] + others[:2] + loads + others[2:] + [more]:
        copy.start()
    for copy in others[:2] + [asked]:
        copy.wait()
    slots, caps = ids_ref.shape[0], requests_ref.shape[1]
    count = slots // caps
    row = lax.broadcasted_iota(jnp.int32, ids_ref.shape, 0)
    ids = jnp.zeros(ids_ref.shape, jnp.int32)
    for r in range(slots):
        owner = me_ref[0] ^ distance_of(r, caps, count)
        ids = jnp.where(row == r, requests_ref[0, r % caps, owner], ids)
    ids_ref[...] = ids.astype(F32)
    edge_blocks(
        pre_ref,
        targets[0],
        targets[1],
        normed_ref,
        q_ref,
        gate_ref,
        hidden_ref,
        block,
        lambda at: loads[at // block].wait(),
    )
    for copy in others[2:] + [more]:
        copy.wait()


def first_part(preact, rows, sources, me, requests, block=512):
    edges, width = preact.shape
    copies = len(sources)
    outs = [in_vmem(a.shape, a.dtype) for a in sources]
    outs += [in_vmem((requests.shape[1] * requests.shape[2], LANES), F32)]
    outs += [in_vmem((edges - rows, width), BF16)]
    outs += [in_vmem((rows, width), BF16)] * 2 + [in_vmem((rows, width), F32)]
    return pl.pallas_call(
        functools.partial(first_kernel, block, copies),
        in_specs=[HBM] * (1 + copies) + [SMEM, HBM],
        out_specs=[VMEM] * len(outs),
        out_shape=outs,
        scratch_shapes=[
            pltpu.VMEM((rows, width), BF16),
            pltpu.VMEM((rows, width), BF16),
            pltpu.SMEM(requests.shape, jnp.int32),
            DMA((copies + rows // block + 2,)),
        ],
        cost_estimate=cost(6 * rows * width * width, 10 * rows * width),
        compiler_params=params(16),
        name="first_part",
    )(in_hbm(preact), *[in_hbm(a) for a in sources], me, in_hbm(requests))


def second_kernel(block, pre_ref, weight_ref, bias_ref, after_ref, normed_ref, q_ref, gate_ref, hidden_ref):
    edge_blocks(
        pre_ref, weight_ref, bias_ref, normed_ref, q_ref, gate_ref, hidden_ref, block, lambda at: None
    )


def second_part(pre, weight, bias, after, block=512):
    rows, width = pre.shape
    outs = [in_vmem((rows, width), BF16)] * 2 + [in_vmem((rows, width), F32)]
    return pl.pallas_call(
        functools.partial(second_kernel, block),
        in_specs=[VMEM, VMEM, VMEM, ANY],
        out_specs=[VMEM] * len(outs),
        out_shape=outs,
        scratch_shapes=[pltpu.VMEM((rows, width), BF16)],
        cost_estimate=cost(6 * rows * width * width, 10 * rows * width),
        compiler_params=params(16),
        name="second_part",
    )(pre, weight, bias, after)


def join_kernel(parts, *refs):
    out_ref, rows = refs[-1], refs[0].shape[0]
    for k in range(parts):
        out_ref[k * rows : (k + 1) * rows, :] = refs[k][...]


def join(pieces, after):
    rows, width = pieces[0].shape
    return pl.pallas_call(
        functools.partial(join_kernel, len(pieces)),
        in_specs=[VMEM] * len(pieces) + [ANY],
        out_specs=VMEM,
        out_shape=in_vmem((len(pieces) * rows, width), pieces[0].dtype),
        cost_estimate=cost(0, 4 * len(pieces) * rows * width),
        compiler_params=params(8),
        name="join",
    )(*pieces, after)


def pack(ref, sums, ids):
    half = sums.shape[1] // 2
    left = jnp.concatenate([sums[:, :half], ids], axis=1)
    right = jnp.concatenate([sums[:, half:], ids], axis=1)
    ref[...] = jnp.concatenate([left, right], axis=0).astype(BF16)


def unpack(ref):
    rows, half = ref.shape[0] // 2, ref.shape[1] - LANES
    both = ref[...].astype(F32)
    return jnp.concatenate([both[:rows, :half], both[rows:, :half]], axis=1), both[:rows, half:]


def after_kernel(
    parts, chunks, owned, caps, block, me_ref, ids_ref, slots_ref, senders_ref, weight_ref, gain_ref, *refs
):
    edge_refs = [refs[3 * k : 3 * k + 3] for k in range(parts)]
    refs = refs[3 * parts :]
    pieces, (d_ref, rim_ref), sums_refs = refs[: -2 - chunks], refs[-2 - chunks : -chunks], refs[-chunks:]
    slots = ids_ref.shape[0]
    count = slots // caps
    edges, width = d_ref.shape
    me = me_ref[0]
    weight = weight_ref[...]

    row = lax.broadcasted_iota(jnp.int32, (slots, 1), 0)
    distance, place, step = distance_of(row, caps, count), jnp.zeros_like(row), 1
    for shift, radix in stages_of(count):
        place = place + ((distance >> shift) & (radix - 1)) * step
        step *= radix
    place = place * owned + ids_ref[...][:, :1].astype(jnp.int32)
    piece_rows = pieces[0].shape[0]
    column = lax.broadcasted_iota(jnp.int32, (slots, piece_rows), 1)
    rows = jnp.zeros((slots, width), F32)
    for k, piece in enumerate(pieces):
        pick = (place == column + k * piece_rows).astype(F32).astype(BF16)
        rows += dot(pick, piece[...])
    rows = rows * gain_ref[...]
    rows = rows - jnp.mean(rows, axis=-1, keepdims=True)
    mean_rows = (rows * (1.0 / width)).astype(BF16)
    both = dot_t(jnp.concatenate(split(rows), axis=0), weight)
    s_both = jnp.concatenate(split(both[:slots] + both[slots:]), axis=0)

    key = (distance ^ me) * caps + row % caps
    key = jnp.concatenate([key, key], axis=0)
    mean_rows = jnp.concatenate([mean_rows, jnp.zeros_like(mean_rows)], axis=0)
    rim_row = lax.broadcasted_iota(jnp.int32, (RIM, block), 0) + G_DEV
    sums = jnp.zeros((slots, width), F32)
    rim = jnp.zeros((RIM, width), F32)
    edge_at = [(part, at) for part in edge_refs for at in range(0, part[0].shape[0], block)]
    last = None
    for number in range(len(edge_at) + 1):
        this = None
        if number < len(edge_at):
            (normed_ref, q_ref, gate_ref), at = edge_at[number]
            piece = slice(at, at + block)
            onehot_t = (key == slots_ref[:, number * block : (number + 1) * block]).astype(F32)
            onehot = onehot_t.T
            g = dot_t(normed_ref[piece], mean_rows)
            s_rows = dot(onehot.astype(BF16), s_both)
            this = (onehot_t[:slots].astype(BF16), onehot, g, s_rows, q_ref, gate_ref, at)
        if last is not None:
            onehot_t, onehot, g, s_rows, q_ref, gate_ref, first = last
            at = (number - 1) * block
            for row in range(0, block, CHUNK):
                piece, inner = slice(first + row, first + row + CHUNK), slice(row, row + CHUNK)
                c = jnp.sum(onehot[inner] * g[inner], axis=-1, keepdims=True)
                d = gate_ref[piece] * (s_rows[inner] - c * q_ref[piece].astype(F32))
                d_ref[at + row : at + row + CHUNK, :] = d.astype(BF16)
            d = d_ref[at : at + block, :]
            sums += dot(onehot_t, d)
            if at + block > G_DEV:
                pick = (rim_row == senders_ref[:, at : at + block]).astype(F32).astype(BF16)
                rim += dot(pick, d)
        last = this

    each = slots // chunks
    for k, sums_ref in enumerate(sums_refs):
        pack(sums_ref, sums[k * each : (k + 1) * each], ids_ref[k * each : (k + 1) * each, :])
    rim_ref[...] = rim.astype(BF16)


def after(me, ids, slots, senders, weight, gain, parts, pieces, owned, caps, chunks, block=512):
    edges, width = slots.shape[1], weight.shape[0]
    each = ids.shape[0] // chunks
    return pl.pallas_call(
        functools.partial(after_kernel, len(parts), chunks, owned, caps, block),
        in_specs=[SMEM] + [VMEM] * (5 + 3 * len(parts) + len(pieces)),
        out_specs=[VMEM] * (2 + chunks),
        out_shape=[in_vmem((edges, width), BF16), in_vmem((RIM, width), BF16)]
        + [in_vmem((2 * each, width // 2 + LANES), BF16)] * chunks,
        cost_estimate=cost(6 * edges * width * width, 8 * edges * width),
        compiler_params=params(20),
        name="after",
    )(me, ids, slots, senders, weight, gain, *[a for part in parts for a in part], *pieces)


def segments_kernel(block, starts_ref, senders_ref, d_ref, total_ref):
    edges, width = d_ref.shape
    total_ref[:8, :] = jnp.zeros((8, width), F32)
    row = lax.broadcasted_iota(jnp.int32, (block + 16, block), 0)
    for at in range(0, edges, block):
        base = pl.multiple_of(starts_ref[at] // 8 * 8, 8)
        onehot = (row == senders_ref[:, at : at + block] - base).astype(F32).astype(BF16)
        sums = dot(onehot, d_ref[at : at + block, :])
        total_ref[pl.ds(base, 8), :] += sums[:8]
        total_ref[pl.ds(pl.multiple_of(base + 8, 8), block + 8), :] = sums[8:]


def segments(senders, d_preact, block=256):
    edges, width = d_preact.shape
    return pl.pallas_call(
        functools.partial(segments_kernel, block),
        in_specs=[SMEM] + [VMEM] * 2,
        out_specs=VMEM,
        out_shape=in_vmem((G_DEV + RIM + block + 16, width), F32),
        cost_estimate=cost(4 * edges * width * width, 4 * edges * width),
        compiler_params=params(16),
        name="segments",
    )(senders, senders.reshape(1, edges), d_preact)


def grid_kernel(block, total_ref, carried_ref, weight_ref, out_hbm, out_ref, sem):
    weight = weight_ref[...]
    copies = []
    for k, at in enumerate(range(0, G_DEV, block)):
        rows = total_ref[at : at + block, :]
        if at == 0:
            rows = jnp.concatenate([rows[:RIM] + carried_ref[...].astype(F32), rows[RIM:]], axis=0)
        out_ref[at : at + block, :] = dot_t(rows.astype(BF16), weight).astype(BF16)
        copies.append(
            pltpu.make_async_copy(out_ref.at[pl.ds(at, block)], out_hbm.at[pl.ds(at, block)], sem.at[k])
        )
        copies[-1].start()
    for copy in copies:
        copy.wait()


def grid_rows(total, carried, weight, block=512):
    width = weight.shape[0]
    return pl.pallas_call(
        functools.partial(grid_kernel, block),
        in_specs=[VMEM] * 3,
        out_specs=HBM,
        out_shape=like((G_DEV, width), BF16),
        scratch_shapes=[pltpu.VMEM((G_DEV, width), BF16), DMA((G_DEV // block,))],
        cost_estimate=cost(2 * G_DEV * width * width, 6 * G_DEV * width),
        compiler_params=params(16),
        name="grid_rows",
    )(total, carried, weight)


def regroup_kernel(groups, parts, *refs):
    outs = refs[parts + 1 :]
    low = groups // len(outs)
    loaded = [unpack(ref) for ref in refs[:parts]]
    each = loaded[0][0].shape[0] // groups
    for j, out_ref in enumerate(outs):
        spans = [(k, (j * low + g) * each) for g in range(low) for k in range(parts)]
        pack(out_ref, *[jnp.concatenate([loaded[k][n][at : at + each] for k, at in spans], axis=0) for n in (0, 1)])


def regroup(arrived, radix, low, after):
    rows, width = arrived[0].shape
    parts = len(arrived)
    return pl.pallas_call(
        functools.partial(regroup_kernel, radix * low, parts),
        in_specs=[VMEM] * parts + [ANY],
        out_specs=[VMEM] * radix,
        out_shape=[in_vmem((rows * parts // radix, width), BF16)] * radix,
        cost_estimate=cost(0, 8 * rows * parts * width),
        compiler_params=params(8),
        name="regroup",
    )(*arrived, after)


def mesh_kernel(parts, *refs):
    pieces, weight_ref, out_ref = refs[:parts], refs[parts], refs[-1]
    owned, width = out_ref.shape
    loaded = [unpack(piece) for piece in pieces]
    rows = jnp.concatenate([sums for sums, _ in loaded], axis=0)
    ids = jnp.concatenate([ids for _, ids in loaded], axis=0).T[:owned].astype(jnp.int32)
    pick = (lax.broadcasted_iota(jnp.int32, ids.shape, 0) == ids).astype(F32)
    total = dot(pick.astype(BF16), rows.astype(BF16))
    both = dot_t(jnp.concatenate(split(total), axis=0), weight_ref[...])
    out_ref[...] = (both[:owned] + both[owned:]).astype(BF16)


def mesh_rows(pieces, weight, owned, after):
    width = weight.shape[0]
    return pl.pallas_call(
        functools.partial(mesh_kernel, len(pieces)),
        in_specs=[VMEM] * (len(pieces) + 1) + [ANY],
        out_specs=VMEM,
        out_shape=like((owned, width), BF16),
        cost_estimate=cost(2 * owned * width * width, 2 * width * width),
        compiler_params=params(8),
        name="mesh_rows",
    )(*pieces, weight, in_hbm(after))


def on_device(
    saved_preact,
    edge_senders,
    edge_slots,
    mesh_requests,
    mesh_cotangent,
    out_weight,
    out_bias,
    ln_gain,
    grid_weight,
    mesh_weight,
):
    count = lax.axis_size("band")
    me = lax.axis_index("band")
    owned, width = mesh_cotangent.shape
    edges = saved_preact.shape[0]
    stages = stages_of(count)

    sources = (
        out_weight,
        out_bias.reshape(1, width),
        grid_weight,
        mesh_weight,
        ln_gain.reshape(1, width),
        mesh_cotangent,
    )
    weight, bias, weight_g, weight_m, gain, own_rows, ids, more, *first = first_part(
        saved_preact, edges // 3, sources, me.reshape(1), mesh_requests.swapaxes(1, 2)
    )

    held = [mesh_cotangent]
    for number, (shift, radix) in enumerate(stages):
        if number == 1:
            held = [join([own_rows, *held[1:]], first[0])]
        elif number > 1:
            held = [join(held, ids)]
        held += [swap(held[0], count, j << shift) for j in range(1, radix)]
        if number == 1:
            second = second_part(more, weight, bias, held[0])

    back = stages[::-1]
    d_preact, rim, *chunks = after(
        me.reshape(1),
        ids,
        edge_slots.reshape(1, edges),
        edge_senders.reshape(1, edges),
        weight,
        gain,
        [first, second],
        held,
        owned,
        mesh_requests.shape[2],
        back[0][1],
    )

    total = segments(edge_senders, d_preact)
    carried = lax.ppermute(rim, "band", [(i, (i + 1) % count) for i in range(count)])
    arrived, left = None, count
    for shift, radix in back:
        if arrived is not None:
            chunks = regroup(arrived, radix, left // radix, total)
        left //= radix
        arrived = [chunks[0]] + [swap(chunks[j], count, j << shift) for j in range(1, radix)]
    grid_adjoint = grid_rows(total, carried, weight_g)
    mesh_adjoint = mesh_rows(arrived, weight_m, owned, grid_adjoint)
    return (grid_adjoint, mesh_adjoint)


def solution(mesh):
    in_specs = (
        P(("groups", "band"), None),
        P("band"),
        P("band"),
        P("band", None, None),
        P(("groups", "band"), None),
        P(),
        P(),
        P(),
        P(),
        P(),
    )
    out_specs = (P(("groups", "band"), None), P(("groups", "band"), None))
    return jax.shard_map(
        on_device, mesh=mesh, in_specs=in_specs, out_specs=out_specs, check_vma=False
    )
```

```python
import functools

import jax
import jax.numpy as jnp
from jax import lax
from jax.experimental import pallas as pl
from jax.experimental.pallas import tpu as pltpu
from jax.sharding import PartitionSpec as P

G_DEV = 2048
RIM = 128
LANES = 128
EPS = 1e-05
CHUNK = 32
MIB = 1 << 20

BF16 = jnp.bfloat16
F32 = jnp.float32
VMEM = pl.BlockSpec(memory_space=pltpu.VMEM)
SMEM = pl.BlockSpec(memory_space=pltpu.SMEM)
HBM = pl.BlockSpec(memory_space=pltpu.HBM)
ANY = pl.BlockSpec(memory_space=pl.ANY)
DMA = pltpu.SemaphoreType.DMA


def stages_of(count):
    top = count.bit_length() - 1
    assert count == 1 << top
    stages = []
    while top > 0:
        low = max(0, top - 2)
        stages.append((low, 1 << (top - low)))
        top = low
    return stages


def distance_of(row, caps, count):
    group, distance, left = row // caps, 0, count
    for shift, radix in reversed(stages_of(count)):
        left //= radix
        distance = distance + ((group // left) % radix << shift)
    return distance


def swap(block, count, mask):
    return lax.ppermute(block, "band", [(i, i ^ mask) for i in range(count)])


def like(shape, dtype):
    return jax.ShapeDtypeStruct(shape, dtype)


def in_hbm(x):
    return pltpu.with_memory_space_constraint(x, pltpu.HBM)


def in_vmem(shape, dtype):
    return pltpu.VMEM(shape, dtype)


def dot(a, b):
    return jnp.dot(a, b, preferred_element_type=F32)


def dot_t(a, b):
    return lax.dot_general(a, b, (((1,), (1,)), ((), ())), preferred_element_type=F32)


def split(x):
    high = x.astype(BF16)
    return high, (x - high.astype(F32)).astype(BF16)


def cost(flops, size):
    return pl.CostEstimate(flops=int(flops), bytes_accessed=int(size), transcendentals=0)


def params(limit):
    return pltpu.CompilerParams(vmem_limit_bytes=limit * MIB)


def edge_blocks(pre_ref, weight_ref, bias_ref, normed_ref, q_ref, gate_ref, hidden_ref, block, arrive):
    weight, bias = weight_ref[...], bias_ref[...]
    rows, last = pre_ref.shape[0], None
    for at in range(0, rows + block, block):
        this = None
        if at < rows:
            arrive(at)
            for row in range(at, at + block, CHUNK):
                piece = slice(row, row + CHUNK)
                half = 0.5 * pre_ref[piece].astype(F32)
                t = jnp.tanh(half)
                double = 1.0 + t
                h = half * double
                hidden_ref[piece] = h.astype(BF16)
                gate_ref[piece] = double + h * (1.0 - t)
            this = dot(hidden_ref[at : at + block], weight)
        if last is not None:
            for row in range(0, block, CHUNK):
                piece = slice(at - block + row, at - block + row + CHUNK)
                out = last[row : row + CHUNK] + bias
                centre = out - jnp.mean(out, axis=-1, keepdims=True)
                inv = lax.rsqrt(jnp.mean(centre * centre, axis=-1, keepdims=True) + EPS)
                normed_ref[piece] = (centre * inv).astype(BF16)
                gate_ref[piece] = gate_ref[piece] * (0.5 * inv)
            q_ref[at - block : at] = dot_t(normed_ref[at - block : at], weight).astype(BF16)
        last = this


def first_kernel(block, copies, pre_hbm, *refs):
    sources, (me_ref, requests_hbm), refs = refs[:copies], refs[copies : copies + 2], refs[copies + 2 :]
    targets, refs = refs[:copies], refs[copies:]
    ids_ref, other_ref, normed_ref, q_ref, gate_ref, pre_ref, hidden_ref, requests_ref, sem = refs
    rows = normed_ref.shape[0]

    def load(k, source, target):
        return pltpu.make_async_copy(source, target, sem.at[k])

    others = [load(k, a, b) for k, (a, b) in enumerate(zip(sources, targets))]
    starts = list(range(0, rows, block))
    more_rows = other_ref.shape[0]
    loads = [
        load(copies + k, pre_hbm.at[pl.ds(at, block)], pre_ref.at[pl.ds(at, block)])
        for k, at in enumerate(starts)
    ]
    more = load(copies + len(loads), pre_hbm.at[pl.ds(rows, more_rows)], other_ref)
    asked = load(copies + len(loads) + 1, requests_hbm, requests_ref)
    for copy in [asked] + others[:2] + loads + others[2:] + [more]:
        copy.start()
    for copy in others[:2] + [asked]:
        copy.wait()
    slots, caps = ids_ref.shape[0], requests_ref.shape[1]
    count = slots // caps
    row = lax.broadcasted_iota(jnp.int32, ids_ref.shape, 0)
    ids = jnp.zeros(ids_ref.shape, jnp.int32)
    for r in range(slots):
        owner = me_ref[0] ^ distance_of(r, caps, count)
        ids = jnp.where(row == r, requests_ref[0, r % caps, owner], ids)
    ids_ref[...] = ids.astype(F32)
    edge_blocks(
        pre_ref,
        targets[0],
        targets[1],
        normed_ref,
        q_ref,
        gate_ref,
        hidden_ref,
        block,
        lambda at: loads[at // block].wait(),
    )
    for copy in others[2:] + [more]:
        copy.wait()


def first_part(preact, rows, sources, me, requests, block=512):
    edges, width = preact.shape
    copies = len(sources)
    outs = [in_vmem(a.shape, a.dtype) for a in sources]
    outs += [in_vmem((requests.shape[1] * requests.shape[2], LANES), F32)]
    outs += [in_vmem((edges - rows, width), BF16)]
    outs += [in_vmem((rows, width), BF16)] * 2 + [in_vmem((rows, width), F32)]
    return pl.pallas_call(
        functools.partial(first_kernel, block, copies),
        in_specs=[HBM] * (1 + copies) + [SMEM, HBM],
        out_specs=[VMEM] * len(outs),
        out_shape=outs,
        scratch_shapes=[
            pltpu.VMEM((rows, width), BF16),
            pltpu.VMEM((rows, width), BF16),
            pltpu.SMEM(requests.shape, jnp.int32),
            DMA((copies + rows // block + 2,)),
        ],
        cost_estimate=cost(6 * rows * width * width, 10 * rows * width),
        compiler_params=params(16),
        name="first_part",
    )(in_hbm(preact), *[in_hbm(a) for a in sources], me, in_hbm(requests))


def second_kernel(block, pre_ref, weight_ref, bias_ref, after_ref, normed_ref, q_ref, gate_ref, hidden_ref):
    edge_blocks(
        pre_ref, weight_ref, bias_ref, normed_ref, q_ref, gate_ref, hidden_ref, block, lambda at: None
    )


def second_part(pre, weight, bias, after, block=512):
    rows, width = pre.shape
    outs = [in_vmem((rows, width), BF16)] * 2 + [in_vmem((rows, width), F32)]
    return pl.pallas_call(
        functools.partial(second_kernel, block),
        in_specs=[VMEM, VMEM, VMEM, ANY],
        out_specs=[VMEM] * len(outs),
        out_shape=outs,
        scratch_shapes=[pltpu.VMEM((rows, width), BF16)],
        cost_estimate=cost(6 * rows * width * width, 10 * rows * width),
        compiler_params=params(16),
        name="second_part",
    )(pre, weight, bias, after)


def join_kernel(parts, *refs):
    out_ref, rows = refs[-1], refs[0].shape[0]
    for k in range(parts):
        out_ref[k * rows : (k + 1) * rows, :] = refs[k][...]


def join(pieces, after):
    rows, width = pieces[0].shape
    return pl.pallas_call(
        functools.partial(join_kernel, len(pieces)),
        in_specs=[VMEM] * len(pieces) + [ANY],
        out_specs=VMEM,
        out_shape=in_vmem((len(pieces) * rows, width), pieces[0].dtype),
        cost_estimate=cost(0, 4 * len(pieces) * rows * width),
        compiler_params=params(8),
        name="join",
    )(*pieces, after)


def pack(ref, sums, ids):
    half = sums.shape[1] // 2
    left = jnp.concatenate([sums[:, :half], ids], axis=1)
    right = jnp.concatenate([sums[:, half:], ids], axis=1)
    ref[...] = jnp.concatenate([left, right], axis=0).astype(BF16)


def unpack(ref):
    rows, half = ref.shape[0] // 2, ref.shape[1] - LANES
    both = ref[...].astype(F32)
    return jnp.concatenate([both[:rows, :half], both[rows:, :half]], axis=1), both[:rows, half:]


def after_kernel(
    parts, chunks, owned, caps, block, me_ref, ids_ref, slots_ref, senders_ref, weight_ref, gain_ref, *refs
):
    edge_refs = [refs[3 * k : 3 * k + 3] for k in range(parts)]
    refs = refs[3 * parts :]
    pieces, (d_ref, rim_ref), sums_refs = refs[: -2 - chunks], refs[-2 - chunks : -chunks], refs[-chunks:]
    slots = ids_ref.shape[0]
    count = slots // caps
    edges, width = d_ref.shape
    me = me_ref[0]
    weight = weight_ref[...]

    row = lax.broadcasted_iota(jnp.int32, (slots, 1), 0)
    distance, place, step = distance_of(row, caps, count), jnp.zeros_like(row), 1
    for shift, radix in stages_of(count):
        place = place + ((distance >> shift) & (radix - 1)) * step
        step *= radix
    place = place * owned + ids_ref[...][:, :1].astype(jnp.int32)
    piece_rows = pieces[0].shape[0]
    column = lax.broadcasted_iota(jnp.int32, (slots, piece_rows), 1)
    rows = jnp.zeros((slots, width), F32)
    for k, piece in enumerate(pieces):
        pick = (place == column + k * piece_rows).astype(F32).astype(BF16)
        rows += dot(pick, piece[...])
    rows = rows * gain_ref[...]
    rows = rows - jnp.mean(rows, axis=-1, keepdims=True)
    mean_rows = (rows * (1.0 / width)).astype(BF16)
    both = dot_t(jnp.concatenate(split(rows), axis=0), weight)
    s_both = jnp.concatenate(split(both[:slots] + both[slots:]), axis=0)

    key = (distance ^ me) * caps + row % caps
    key = jnp.concatenate([key, key], axis=0)
    mean_rows = jnp.concatenate([mean_rows, jnp.zeros_like(mean_rows)], axis=0)
    rim_row = lax.broadcasted_iota(jnp.int32, (RIM, block), 0) + G_DEV
    sums = jnp.zeros((slots, width), F32)
    rim = jnp.zeros((RIM, width), F32)
    edge_at = [(part, at) for part in edge_refs for at in range(0, part[0].shape[0], block)]
    last = None
    for number in range(len(edge_at) + 1):
        this = None
        if number < len(edge_at):
            (normed_ref, q_ref, gate_ref), at = edge_at[number]
            piece = slice(at, at + block)
            onehot_t = (key == slots_ref[:, number * block : (number + 1) * block]).astype(F32)
            onehot = onehot_t.T
            g = dot_t(normed_ref[piece], mean_rows)
            s_rows = dot(onehot.astype(BF16), s_both)
            this = (onehot_t[:slots].astype(BF16), onehot, g, s_rows, q_ref, gate_ref, at)
        if last is not None:
            onehot_t, onehot, g, s_rows, q_ref, gate_ref, first = last
            at = (number - 1) * block
            for row in range(0, block, CHUNK):
                piece, inner = slice(first + row, first + row + CHUNK), slice(row, row + CHUNK)
                c = jnp.sum(onehot[inner] * g[inner], axis=-1, keepdims=True)
                d = gate_ref[piece] * (s_rows[inner] - c * q_ref[piece].astype(F32))
                d_ref[at + row : at + row + CHUNK, :] = d.astype(BF16)
            d = d_ref[at : at + block, :]
            sums += dot(onehot_t, d)
            if at + block > G_DEV:
                pick = (rim_row == senders_ref[:, at : at + block]).astype(F32).astype(BF16)
                rim += dot(pick, d)
        last = this

    each = slots // chunks
    for k, sums_ref in enumerate(sums_refs):
        pack(sums_ref, sums[k * each : (k + 1) * each], ids_ref[k * each : (k + 1) * each, :])
    rim_ref[...] = rim.astype(BF16)


def after(me, ids, slots, senders, weight, gain, parts, pieces, owned, caps, chunks, block=512):
    edges, width = slots.shape[1], weight.shape[0]
    each = ids.shape[0] // chunks
    return pl.pallas_call(
        functools.partial(after_kernel, len(parts), chunks, owned, caps, block),
        in_specs=[SMEM] + [VMEM] * (5 + 3 * len(parts) + len(pieces)),
        out_specs=[VMEM] * (2 + chunks),
        out_shape=[in_vmem((edges, width), BF16), in_vmem((RIM, width), BF16)]
        + [in_vmem((2 * each, width // 2 + LANES), BF16)] * chunks,
        cost_estimate=cost(6 * edges * width * width, 8 * edges * width),
        compiler_params=params(20),
        name="after",
    )(me, ids, slots, senders, weight, gain, *[a for part in parts for a in part], *pieces)


def segments_kernel(block, starts_ref, senders_ref, d_ref, total_ref):
    edges, width = d_ref.shape
    total_ref[:8, :] = jnp.zeros((8, width), F32)
    row = lax.broadcasted_iota(jnp.int32, (block + 16, block), 0)
    for at in range(0, edges, block):
        base = pl.multiple_of(starts_ref[at] // 8 * 8, 8)
        onehot = (row == senders_ref[:, at : at + block] - base).astype(F32).astype(BF16)
        sums = dot(onehot, d_ref[at : at + block, :])
        total_ref[pl.ds(base, 8), :] += sums[:8]
        total_ref[pl.ds(pl.multiple_of(base + 8, 8), block + 8), :] = sums[8:]


def segments(senders, d_preact, block=256):
    edges, width = d_preact.shape
    return pl.pallas_call(
        functools.partial(segments_kernel, block),
        in_specs=[SMEM] + [VMEM] * 2,
        out_specs=VMEM,
        out_shape=in_vmem((G_DEV + RIM + block + 16, width), F32),
        cost_estimate=cost(4 * edges * width * width, 4 * edges * width),
        compiler_params=params(16),
        name="segments",
    )(senders, senders.reshape(1, edges), d_preact)


def grid_kernel(block, total_ref, carried_ref, weight_ref, out_hbm, out_ref, sem):
    weight = weight_ref[...]
    copies = []
    for k, at in enumerate(range(0, G_DEV, block)):
        rows = total_ref[at : at + block, :]
        if at == 0:
            rows = jnp.concatenate([rows[:RIM] + carried_ref[...].astype(F32), rows[RIM:]], axis=0)
        out_ref[at : at + block, :] = dot_t(rows.astype(BF16), weight).astype(BF16)
        copies.append(
            pltpu.make_async_copy(out_ref.at[pl.ds(at, block)], out_hbm.at[pl.ds(at, block)], sem.at[k])
        )
        copies[-1].start()
    for copy in copies:
        copy.wait()


def grid_rows(total, carried, weight, block=512):
    width = weight.shape[0]
    return pl.pallas_call(
        functools.partial(grid_kernel, block),
        in_specs=[VMEM] * 3,
        out_specs=HBM,
        out_shape=like((G_DEV, width), BF16),
        scratch_shapes=[pltpu.VMEM((G_DEV, width), BF16), DMA((G_DEV // block,))],
        cost_estimate=cost(2 * G_DEV * width * width, 6 * G_DEV * width),
        compiler_params=params(16),
        name="grid_rows",
    )(total, carried, weight)


def regroup_kernel(groups, parts, *refs):
    outs = refs[parts + 1 :]
    low = groups // len(outs)
    loaded = [unpack(ref) for ref in refs[:parts]]
    each = loaded[0][0].shape[0] // groups
    for j, out_ref in enumerate(outs):
        spans = [(k, (j * low + g) * each) for g in range(low) for k in range(parts)]
        pack(out_ref, *[jnp.concatenate([loaded[k][n][at : at + each] for k, at in spans], axis=0) for n in (0, 1)])


def regroup(arrived, radix, low, after):
    rows, width = arrived[0].shape
    parts = len(arrived)
    return pl.pallas_call(
        functools.partial(regroup_kernel, radix * low, parts),
        in_specs=[VMEM] * parts + [ANY],
        out_specs=[VMEM] * radix,
        out_shape=[in_vmem((rows * parts // radix, width), BF16)] * radix,
        cost_estimate=cost(0, 8 * rows * parts * width),
        compiler_params=params(8),
        name="regroup",
    )(*arrived, after)


def mesh_kernel(parts, *refs):
    pieces, weight_ref, out_ref = refs[:parts], refs[parts], refs[-1]
    owned, width = out_ref.shape
    loaded = [unpack(piece) for piece in pieces]
    rows = jnp.concatenate([sums for sums, _ in loaded], axis=0)
    ids = jnp.concatenate([ids for _, ids in loaded], axis=0).astype(jnp.int32)
    pick = (lax.broadcasted_iota(jnp.int32, ids.shape, 1) == ids).astype(F32).astype(BF16)
    total = lax.dot_general(pick, rows.astype(BF16), (((0,), (0,)), ((), ())), preferred_element_type=F32)
    total = total[:owned]
    both = dot_t(jnp.concatenate(split(total), axis=0), weight_ref[...])
    out_ref[...] = (both[:owned] + both[owned:]).astype(BF16)


def mesh_rows(pieces, weight, owned, after):
    width = weight.shape[0]
    return pl.pallas_call(
        functools.partial(mesh_kernel, len(pieces)),
        in_specs=[VMEM] * (len(pieces) + 1) + [ANY],
        out_specs=VMEM,
        out_shape=like((owned, width), BF16),
        cost_estimate=cost(2 * owned * width * width, 2 * width * width),
        compiler_params=params(8),
        name="mesh_rows",
    )(*pieces, weight, in_hbm(after))


def on_device(
    saved_preact,
    edge_senders,
    edge_slots,
    mesh_requests,
    mesh_cotangent,
    out_weight,
    out_bias,
    ln_gain,
    grid_weight,
    mesh_weight,
):
    count = lax.axis_size("band")
    me = lax.axis_index("band")
    owned, width = mesh_cotangent.shape
    edges = saved_preact.shape[0]
    stages = stages_of(count)

    sources = (
        out_weight,
        out_bias.reshape(1, width),
        grid_weight,
        mesh_weight,
        ln_gain.reshape(1, width),
        mesh_cotangent,
    )
    weight, bias, weight_g, weight_m, gain, own_rows, ids, more, *first = first_part(
        saved_preact, edges // 3, sources, me.reshape(1), mesh_requests.swapaxes(1, 2)
    )

    held = [mesh_cotangent]
    for number, (shift, radix) in enumerate(stages):
        if number == 1:
            held = [join([own_rows, *held[1:]], first[0])]
        elif number > 1:
            held = [join(held, ids)]
        held += [swap(held[0], count, j << shift) for j in range(1, radix)]
        if number == 1:
            second = second_part(more, weight, bias, held[0])

    back = stages[::-1]
    d_preact, rim, *chunks = after(
        me.reshape(1),
        ids,
        edge_slots.reshape(1, edges),
        edge_senders.reshape(1, edges),
        weight,
        gain,
        [first, second],
        held,
        owned,
        mesh_requests.shape[2],
        back[0][1],
    )

    total = segments(edge_senders, d_preact)
    carried = lax.ppermute(rim, "band", [(i, (i + 1) % count) for i in range(count)])
    arrived, left = None, count
    for shift, radix in back:
        if arrived is not None:
            chunks = regroup(arrived, radix, left // radix, total)
        left //= radix
        arrived = [chunks[0]] + [swap(chunks[j], count, j << shift) for j in range(1, radix)]
    grid_adjoint = grid_rows(total, carried, weight_g)
    mesh_adjoint = mesh_rows(arrived, weight_m, owned, grid_adjoint)
    return (grid_adjoint, mesh_adjoint)


def solution(mesh):
    in_specs = (
        P(("groups", "band"), None),
        P("band"),
        P("band"),
        P("band", None, None),
        P(("groups", "band"), None),
        P(),
        P(),
        P(),
        P(),
        P(),
    )
    out_specs = (P(("groups", "band"), None), P(("groups", "band"), None))
    return jax.shard_map(
        on_device, mesh=mesh, in_specs=in_specs, out_specs=out_specs, check_vma=False
    )
```
